32 devices in a mesh: dp: 8 (over y, x, core), tensor: 4 (over z).
Axes of the slice: x: 2, y: 2, z: 4, core: 2. Of those that a mesh axis runs over, the one named last changes fastest.
Arguments:
- inputs: bfloat16 [16384, 2048], P(('dp', 'tensor')), may hold values from -6 to 6
- cotangent: bfloat16 [16384, 2048], P(('dp', 'tensor')), may hold values from -6 to 6
- lengths: int32 [8, 4], P('dp'), may hold values from 1 to 512, 1024 in all within a row
- held_blocks: int32 [4, 8], replicated, may hold values from 0 to 7, each once within a row
- master: float32 [8, 4, 96, 128, 128], P('dp', 'tensor')
- first_moment: float32 [8, 4, 96, 128, 128], P('dp', 'tensor')
- second_moment: float32 [8, 4, 96, 128, 128], P('dp', 'tensor')
- left_stats: float32 [8, 4, 96, 128, 128], P('dp', 'tensor')
- right_stats: float32 [8, 4, 96, 128, 128], P('dp', 'tensor')
- left_basis: float32 [8, 4, 96, 128, 128], P('dp', 'tensor')
- right_basis: float32 [8, 4, 96, 128, 128], P('dp', 'tensor')
- small_params: float32 [24576], replicated
- small_first: float32 [24576], replicated
- small_second: float32 [24576], replicated
Outputs:
- outputs: bfloat16 [16384, 2048], P(('dp', 'tensor'))
- input_grad: bfloat16 [16384, 2048], P(('dp', 'tensor'))
- new_first: float32 [8, 4, 96, 128, 128], P('dp', 'tensor')
- new_second: float32 [8, 4, 96, 128, 128], P('dp', 'tensor')
- new_master: float32 [8, 4, 96, 128, 128], P('dp', 'tensor')
- new_weights: bfloat16 [8, 4, 96, 128, 128], P('dp', 'tensor')
- new_left_stats: float32 [8, 4, 96, 128, 128], P('dp', 'tensor')
- new_right_stats: float32 [8, 4, 96, 128, 128], P('dp', 'tensor')
- new_left_basis: float32 [8, 4, 96, 128, 128], P('dp', 'tensor')
- new_right_basis: float32 [8, 4, 96, 128, 128], P('dp', 'tensor')
- small_first_new: float32 [24576], replicated
- small_second_new: float32 [24576], replicated
- small_new: float32 [24576], replicated
The draws below stay inside these ranges and needn't reach their ends.
Inputs may be any that keep to these rules, and one draw needn't show every extreme that they name: Each row of held_blocks names every block once. A group's lengths sum to 1024; one of them is 512.
All inputs are finite; a program needn't handle non-finite values.
Results may differ from the reference program's by a relative error of at most 0.018.
Values may be sent and summed in bfloat16 or wider, within the bound.
No kernel may reach another device: no remote copies, remote signals or barrier semaphores. Data moves between devices by JAX's collectives and lax.ppermute only.
A program may use at most 384 MiB of HBM per device.

```python
import math
import jax
import jax.numpy as jnp
import numpy as np
from jax import lax

D = 2048
H = 16
HD = 128
FF = 8192
PROMPT = 1024
CONT = 4
CLEN = 256
QBLK = 512
STEP = 5
NS_ITERS = 3
SEQ = 2048
GROUPS = 8
TOKENS = 16384
TQ = 24
TO = 8
TU = 32
TILES = 96
SMALL = 24576
N_DP = 8
N_TENSOR = 4


def tile_scales(first_value, second_value, third_value, fourth_value):
    index = jnp.arange(TILES)
    picked = jnp.where(index < TQ, first_value, jnp.where(index < TQ + TO, second_value, jnp.where(index < TQ + TO + TU, third_value, fourth_value)))
    return picked.astype(jnp.float32)[:, None, None]


def gradient_scales():
    return math.sqrt(TOKENS) * tile_scales(1.0, math.sqrt(2.0 / SEQ), 0.3, 0.65)


def bank_shape():
    return (N_DP, N_TENSOR, TILES, HD, HD)


def draw_master(key, part):
    key = jax.random.fold_in(key, 11)
    spread = tile_scales(D ** (-0.5), math.sqrt(SEQ / (2.0 * D)), D ** (-0.5), FF ** (-0.5))
    noise = jax.random.truncated_normal(key, -4.0, 4.0, bank_shape(), jnp.float32)
    return noise * spread


def draw_first_moment(key, part):
    key = jax.random.fold_in(key, 12)
    noise = jax.random.truncated_normal(key, -4.0, 4.0, bank_shape(), jnp.float32)
    return noise * gradient_scales()


def draw_second_moment(key, part):
    key = jax.random.fold_in(key, 13)
    factor = jnp.exp(jax.random.uniform(key, bank_shape(), jnp.float32, 0.0, math.log(4.0)))
    scales = gradient_scales()
    return factor * scales * scales


def statistic_draw(key):
    first_key, second_key = jax.random.split(key)
    diagonal = jnp.exp(jax.random.uniform(first_key, bank_shape()[:-1], jnp.float32, 0.0, math.log(4.0)))
    noise = jax.random.truncated_normal(second_key, -4.0, 4.0, bank_shape(), jnp.float32)
    paired = (noise + jnp.swapaxes(noise, -1, -2)) * (0.5 / math.sqrt(2.0 * HD))
    identity = jnp.eye(HD, dtype=jnp.float32)
    size_sq = tile_scales(1.0, 2.0 / SEQ, 0.09, 0.4225)
    return (identity * diagonal[..., :, None] + (1.0 - identity) * paired) * size_sq


def draw_left_stats(key, part):
    key = jax.random.fold_in(key, 14)
    return statistic_draw(key)


def draw_right_stats(key, part):
    key = jax.random.fold_in(key, 15)
    return statistic_draw(key)


def basis_draw(key):
    noise = jax.random.truncated_normal(key, -4.0, 4.0, bank_shape(), jnp.float32)
    return 0.8 * jnp.eye(HD, dtype=jnp.float32) + noise * (0.6 / math.sqrt(HD))


def draw_left_basis(key, part):
    key = jax.random.fold_in(key, 16)
    return basis_draw(key)


def draw_right_basis(key, part):
    key = jax.random.fold_in(key, 17)
    return basis_draw(key)


def small_segments():
    return jnp.minimum(jnp.arange(SMALL) // D, 8)


def small_scales():
    table = jnp.array([1.0, 1.0, 1.2, 1.0, 1.7, 1.7, 0.6, 0.6, 0.3], jnp.float32)
    return math.sqrt(TOKENS) * table[small_segments()]


def draw_small_params(key, part):
    key = jax.random.fold_in(key, 18)
    segment = small_segments()
    noise = jax.random.truncated_normal(key, -4.0, 4.0, (SMALL,), jnp.float32)
    is_gain = (segment == 4) | (segment == 6)
    return jnp.where(is_gain, 1.0 + 0.1 * noise, 0.2 * noise)


def draw_small_first(key, part):
    key = jax.random.fold_in(key, 19)
    noise = jax.random.truncated_normal(key, -4.0, 4.0, (SMALL,), jnp.float32)
    return noise * small_scales()


def draw_small_second(key, part):
    key = jax.random.fold_in(key, 20)
    factor = jnp.exp(jax.random.uniform(key, (SMALL,), jnp.float32, 0.0, math.log(4.0)))
    scales = small_scales()
    return factor * scales * scales


def steps_of(own_key, shape, shards, smallest, top_value):
    def one(axis_at, parts):
        draws = jax.random.uniform(jax.random.fold_in(jax.random.fold_in(own_key, 6), axis_at), (parts,), jnp.float32, smallest / len(shards), top_value / len(shards))
        return jnp.repeat(jnp.exp(draws), shape[axis_at] // parts).reshape((-1,) + (1,) * (len(shape) - axis_at - 1))

    level = one(*shards[0])
    for cut in shards[1:]:
        level = level * one(*cut)
    return level


def length_profile(count, total, limit, skew):
    weights = [(1 << 20) // math.isqrt(rank ** skew) + 1 for rank in range(2, count + 1)]
    spare, given = total - limit - (count - 1), [1] * (count - 1)
    while spare > 0:
        movable = [i for i in range(count - 1) if given[i] < limit]
        whole, left = sum([weights[i] for i in movable]), spare
        for i in movable:
            addition = min(limit - given[i], max(1, left * weights[i] // whole), spare)
            given[i] = given[i] + addition
            spare = spare - addition
    return np.array([limit] + given)


def ragged(own_key, number_of, total, reach, lean):
    if number_of == 2:
        one = jax.random.randint(own_key, (), max(1, total - reach), min(reach, total - 1) + 1)
        return jnp.stack([one, total - one])
    tallies = jnp.asarray(length_profile(number_of, total, reach, lean), jnp.int32)
    couples = (number_of - 1) // 2
    donor, receiver = tallies[1:1 + 2 * couples:2], tallies[2:2 + 2 * couples:2]
    room = jnp.minimum(donor - 1, reach - receiver)
    moved = jax.random.randint(jax.random.fold_in(own_key, 1), (couples,), 0, 1 << 20) % (room + 1)
    tallies = tallies.at[1:1 + 2 * couples:2].set(donor - moved).at[2:2 + 2 * couples:2].set(receiver + moved)
    return tallies[jax.random.permutation(jax.random.fold_in(own_key, 2), number_of)]


def normal_values(key, extent, scale, reach, shards=(), kind=jnp.bfloat16):
    level = steps_of(key, extent, shards, -0.22, 0.18) if shards else 1.0
    drawn = jax.random.normal(key, extent, jnp.float32) * scale * level
    return jnp.minimum(jnp.maximum(drawn, -reach), reach).astype(kind)


def setup_inputs(seed: int = 0) -> dict:
    keys = jax.random.split(jax.random.key(seed), 15)
    return {
        "inputs": normal_values(keys[0], (TOKENS, D), 1.0, 6.0, ((0, 32),)),
        "cotangent": normal_values(keys[1], (TOKENS, D), 1.0, 6.0, ((0, 32),)),
        "lengths": jax.vmap(lambda own: ragged(own, CONT, CONT * CLEN, 2 * CLEN, 2))(jax.random.split(keys[2], GROUPS)).reshape((GROUPS, CONT)).astype(jnp.int32),
        "held_blocks": jax.vmap(lambda own: jax.random.permutation(own, N_DP))(jax.random.split(keys[3], 4)).reshape((4, N_DP)).astype(jnp.int32),
        "master": draw_master(jax.random.fold_in(keys[14], 71), 0),
        "first_moment": draw_first_moment(jax.random.fold_in(keys[14], 71), 0),
        "second_moment": draw_second_moment(jax.random.fold_in(keys[14], 71), 0),
        "left_stats": draw_left_stats(jax.random.fold_in(keys[14], 71), 0),
        "right_stats": draw_right_stats(jax.random.fold_in(keys[14], 71), 0),
        "left_basis": draw_left_basis(jax.random.fold_in(keys[14], 71), 0),
        "right_basis": draw_right_basis(jax.random.fold_in(keys[14], 71), 0),
        "small_params": draw_small_params(jax.random.fold_in(keys[14], 71), 0),
        "small_first": draw_small_first(jax.random.fold_in(keys[14], 71), 0),
        "small_second": draw_small_second(jax.random.fold_in(keys[14], 71), 0),
    }


@jax.custom_vjp
def low(v):
    return lax.optimization_barrier(v.astype(jnp.bfloat16)).astype(jnp.float32)

@jax.custom_vjp
def low_back(v):
    return v

def low_keep(v):
    return (low(v), None)

def low_pass(kept, grad):
    return (grad,)

def back_keep(v):
    return (v, None)

def back_low(kept, grad):
    return (low(grad),)
low.defvjp(low_keep, low_pass)
low_back.defvjp(back_keep, back_low)
exact_mode = lax.Precision.HIGHEST
NORM_EPS = 1e-05
NEG_FILL = -1e+30
BETA_ONE = 0.5
BETA_TWO = 0.5
ADAM_EPS = 1e-08
WEIGHT_DECAY = 0.1
CLIP_LIMIT = 1.0
SMALL_RATE = 0.1

def layer_norm(token_rows, gain, shift):
    centre = lax.optimization_barrier(jnp.mean(token_rows, axis=-1, keepdims=True))
    centred = token_rows - centre
    spread = lax.optimization_barrier(jnp.mean(centred * centred, axis=-1, keepdims=True))
    return centred * lax.rsqrt(spread + NORM_EPS) * gain + shift

def tiles_to_matrix(tiles, row_tiles, col_tiles):
    leading = tiles.shape[:-3]
    edge = tiles.shape[-1]
    grid = tiles.reshape(leading + (row_tiles, col_tiles, edge, edge))
    grid = jnp.swapaxes(grid, -3, -2)
    return grid.reshape(leading + (row_tiles * edge, col_tiles * edge))

def matrix_to_tiles(matrix, edge):
    leading = matrix.shape[:-2]
    row_count, col_count = (matrix.shape[-2], matrix.shape[-1])
    grid = matrix.reshape(leading + (row_count // edge, edge, col_count // edge, edge))
    grid = jnp.swapaxes(grid, -3, -2)
    return grid.reshape(leading + (row_count // edge * (col_count // edge), edge, edge))

def segment_ids(length_row):
    ends = jnp.cumsum(length_row).astype(jnp.int32)
    place = jnp.arange(SEQ, dtype=jnp.int32) - PROMPT
    counted = lax.optimization_barrier(jnp.sum((ends[None, :] <= place[:, None]).astype(jnp.int32), axis=1)).astype(jnp.int32)
    return jnp.where(place < 0, -1, counted).astype(jnp.int32)

def visible(query_pos, key_pos, query_segments, key_segments):
    causal = key_pos[None, :] <= query_pos[:, None]
    shared = (key_pos[None, :] < PROMPT) | (key_segments[None, :] == query_segments[:, None])
    return causal & shared

def orthonormal(matrix):
    frob = jnp.sqrt(lax.optimization_barrier(jnp.sum(matrix * matrix, axis=(-2, -1), keepdims=True)))
    current = matrix / (frob + 1e-06)
    for sweep_index in range(NS_ITERS):
        gram = jnp.einsum('...ji,...jk->...ik', current, current, precision=exact_mode)
        current = 1.5 * current - 0.5 * jnp.einsum('...ij,...jk->...ik', current, gram, precision=exact_mode)
    return current

def soap_step(summed, master, first, second, left_stat, right_stat, left_base, right_base, step_rate, factor, token_count):
    rotated = jnp.einsum('...ji,...jk->...ik', left_base, summed, precision=exact_mode)
    rotated = jnp.einsum('...ij,...jk->...ik', rotated, right_base, precision=exact_mode)
    new_first = BETA_ONE * first + (1.0 - BETA_ONE) * rotated
    new_second = BETA_TWO * second + (1.0 - BETA_TWO) * rotated * rotated
    direction = new_first / (1.0 - BETA_ONE ** STEP) / (jnp.sqrt(new_second / (1.0 - BETA_TWO ** STEP)) + ADAM_EPS)
    turned = jnp.einsum('...ij,...jk->...ik', left_base, direction, precision=exact_mode)
    turned = jnp.einsum('...ij,...kj->...ik', turned, right_base, precision=exact_mode)
    new_master = (master - step_rate * (turned + WEIGHT_DECAY * master)) * factor
    outer_rows = jnp.einsum('...ij,...kj->...ik', summed, summed, precision=exact_mode)
    outer_cols = jnp.einsum('...ji,...jk->...ik', summed, summed, precision=exact_mode)
    new_left = BETA_TWO * left_stat + (1.0 - BETA_TWO) * outer_rows / (HD * token_count)
    new_right = BETA_TWO * right_stat + (1.0 - BETA_TWO) * outer_cols / (HD * token_count)
    left_next = orthonormal(jnp.einsum('...ij,...jk->...ik', new_left, left_base, precision=exact_mode))
    right_next = orthonormal(jnp.einsum('...ij,...jk->...ik', new_right, right_base, precision=exact_mode))
    return (new_first, new_second, new_master, new_left, new_right, left_next, right_next)

def small_step(summed, params, first, second, shrink):
    new_first = BETA_ONE * first + (1.0 - BETA_ONE) * summed
    new_second = BETA_TWO * second + (1.0 - BETA_TWO) * summed * summed
    direction = new_first / (1.0 - BETA_ONE ** STEP) / (jnp.sqrt(new_second / (1.0 - BETA_TWO ** STEP)) + ADAM_EPS)
    scaled = jnp.concatenate([jnp.repeat(shrink, HD), jnp.ones((7 * D + FF,), jnp.float32)])
    return (new_first, new_second, (params - SMALL_RATE * direction) * scaled)

def tile_rates(tile_q, tile_o, tile_u, count):
    index = jnp.arange(count, dtype=jnp.int32)
    rates = jnp.where(index < tile_q, D ** (-0.5), jnp.where(index < tile_q + tile_o, (SEQ / (2.0 * D)) ** 0.5, jnp.where(index < tile_q + tile_o + tile_u, D ** (-0.5), FF ** (-0.5))))
    return rates.astype(jnp.float32)

def tile_factors(shrink, tensor_index, heads_local, tile_q, count):
    index = jnp.arange(count, dtype=jnp.int32)
    column = index % (3 * heads_local)
    head_index = tensor_index * heads_local + column % heads_local
    picked = lax.optimization_barrier(jnp.sum(jnp.where(head_index[:, None] == jnp.arange(H, dtype=jnp.int32)[None, :], shrink[None, :], 0.0), axis=1))
    return jnp.where((index < tile_q) & (column < 2 * heads_local), picked, 1.0).astype(jnp.float32)

def unpack(master, held_blocks):
    inverse = jnp.argsort(held_blocks, axis=1).astype(jnp.int32)
    bounds = [0, TQ, TQ + TO, TQ + TO + TU, TILES]

    def logical(kind_index):
        return master[:, :, bounds[kind_index]:bounds[kind_index + 1]][inverse[kind_index]]
    rows_dp = D // N_DP
    width_tp = D // N_TENSOR
    hidden_tp = FF // N_TENSOR
    weight_qkv = tiles_to_matrix(logical(0), rows_dp // HD, 3 * width_tp // HD)
    weight_qkv = weight_qkv.reshape(N_DP, N_TENSOR, rows_dp, 3, width_tp).transpose(0, 2, 3, 1, 4).reshape(D, 3, D)
    weight_out = tiles_to_matrix(logical(1), width_tp // HD, rows_dp // HD).transpose(1, 2, 0, 3).reshape(D, D)
    weight_up = tiles_to_matrix(logical(2), rows_dp // HD, hidden_tp // HD).transpose(0, 2, 1, 3).reshape(D, FF)
    weight_down = tiles_to_matrix(logical(3), hidden_tp // HD, rows_dp // HD).transpose(1, 2, 0, 3).reshape(FF, D)
    return (weight_qkv, weight_out, weight_up, weight_down)

def pack(grad_qkv, grad_out, grad_up, grad_down, held_blocks):
    rows_dp = D // N_DP
    width_tp = D // N_TENSOR
    hidden_tp = FF // N_TENSOR
    part_qkv = grad_qkv.reshape(N_DP, rows_dp, 3, N_TENSOR, width_tp).transpose(0, 3, 1, 2, 4).reshape(N_DP, N_TENSOR, rows_dp, 3 * width_tp)
    part_out = grad_out.reshape(N_TENSOR, width_tp, N_DP, rows_dp).transpose(2, 0, 1, 3)
    part_up = grad_up.reshape(N_DP, rows_dp, N_TENSOR, hidden_tp).transpose(0, 2, 1, 3)
    part_down = grad_down.reshape(N_TENSOR, hidden_tp, N_DP, rows_dp).transpose(2, 0, 1, 3)
    pieces = []
    for kind_index, part_matrix in enumerate([part_qkv, part_out, part_up, part_down]):
        pieces.append(matrix_to_tiles(part_matrix, HD)[held_blocks[kind_index]])
    return jnp.concatenate(pieces, axis=2)

def layer_group(weight_qkv, weight_out, weight_up, weight_down, small_vec, token_rows, segments):
    bias_q = small_vec[0:D]
    bias_v = small_vec[D:2 * D]
    bias_o = small_vec[2 * D:3 * D]
    bias_two = small_vec[3 * D:4 * D]
    gain_one = small_vec[4 * D:5 * D]
    shift_one = small_vec[5 * D:6 * D]
    gain_two = small_vec[6 * D:7 * D]
    shift_two = small_vec[7 * D:8 * D]
    bias_up = small_vec[8 * D:]
    normed = low(layer_norm(token_rows, gain_one, shift_one))
    projected = jnp.einsum('sd,dje->sje', normed, low(weight_qkv), precision=exact_mode)
    queries = low(low_back(projected[:, 0] + bias_q)).reshape(SEQ, H, HD)
    key_rows = low(low_back(projected[:, 1])).reshape(SEQ, H, HD)
    value_rows = low(low_back(projected[:, 2] + bias_v)).reshape(SEQ, H, HD)
    positions = jnp.arange(SEQ, dtype=jnp.int32)
    score_scale = HD ** (-0.5)

    def attend(block):
        query_block, start = block
        query_pos = start + jnp.arange(QBLK, dtype=jnp.int32)
        query_segments = lax.dynamic_slice_in_dim(segments, start, QBLK)
        product = low_back(jnp.einsum('qhd,khd->hqk', query_block, key_rows, precision=exact_mode))
        scores = jnp.where(visible(query_pos, positions, query_segments, segments)[None], product * score_scale, NEG_FILL)
        row_top = lax.optimization_barrier(jnp.max(scores, axis=-1, keepdims=True))
        weights = jnp.exp(scores - row_top)
        probs = weights / lax.optimization_barrier(jnp.sum(weights, axis=-1, keepdims=True))
        block_out = jnp.einsum('hqk,khd->qhd', low(probs), value_rows, precision=exact_mode)
        return (block_out, lax.optimization_barrier(jnp.max(row_top[:, :, 0], axis=1)))
    starts = jnp.arange(SEQ // QBLK, dtype=jnp.int32) * QBLK
    attended, peaks = lax.map(jax.checkpoint(attend), (queries.reshape(SEQ // QBLK, QBLK, H, HD), starts))
    attended = low(low_back(attended.reshape(SEQ, D)))
    hidden = token_rows + low_back(jnp.dot(attended, low(weight_out), precision=exact_mode) + bias_o)
    normed_two = low(layer_norm(hidden, gain_two, shift_two))
    pre_act = low_back(jnp.dot(normed_two, low(weight_up), precision=exact_mode) + bias_up)
    activation = low(jax.nn.gelu(pre_act, approximate=False))
    result = hidden + low_back(jnp.dot(activation, low(weight_down), precision=exact_mode) + bias_two)
    return (result, lax.optimization_barrier(jnp.max(peaks, axis=0)))

def reference(inputs, cotangent, lengths, held_blocks, master, first_moment, second_moment, left_stats, right_stats, left_basis, right_basis, small_params, small_first, small_second):
    weight_qkv, weight_out, weight_up, weight_down = unpack(master, held_blocks)
    rows_all = inputs.astype(jnp.float32).reshape(GROUPS, SEQ, D)
    backs_all = cotangent.astype(jnp.float32).reshape(GROUPS, SEQ, D)
    zero_grads = (jnp.zeros_like(weight_qkv), jnp.zeros_like(weight_out), jnp.zeros_like(weight_up), jnp.zeros_like(weight_down), jnp.zeros_like(small_params))

    def one_group(carry, item):
        token_rows, back_rows, length_row = item
        segments = segment_ids(length_row)

        def forward(first_w, second_w, third_w, fourth_w, small_vec, rows_in):
            return layer_group(first_w, second_w, third_w, fourth_w, small_vec, rows_in, segments)
        result, pullback, peaks = jax.vjp(forward, weight_qkv, weight_out, weight_up, weight_down, small_params, token_rows, has_aux=True)
        grads = pullback(back_rows)
        carry = tuple((total + piece for total, piece in zip(carry, grads[:5])))
        return (carry, (result, grads[5], peaks))
    totals, (results, input_rows, peaks) = lax.scan(one_group, zero_grads, (rows_all, backs_all, lengths))
    outputs = results.reshape(TOKENS, D).astype(jnp.bfloat16)
    input_grad = input_rows.reshape(TOKENS, D).astype(jnp.bfloat16)
    peak_all = lax.optimization_barrier(jnp.max(peaks, axis=0))
    shrink = jnp.sqrt(CLIP_LIMIT / jnp.maximum(peak_all, CLIP_LIMIT))
    grad_bank = pack(totals[0], totals[1], totals[2], totals[3], held_blocks)
    rates = tile_rates(TQ, TO, TU, TILES)[:, None, None]
    factors = jax.vmap(lambda t: tile_factors(shrink, t, H // N_TENSOR, TQ, TILES))(jnp.arange(N_TENSOR, dtype=jnp.int32))[:, :, None, None]
    token_count = float(GROUPS * SEQ)

    def slot_update(items):
        return soap_step(items[0], items[1], items[2], items[3], items[4], items[5], items[6], items[7], rates, factors, token_count)
    new_first, new_second, new_master, new_left, new_right, left_next, right_next = lax.map(slot_update, (grad_bank, master, first_moment, second_moment, left_stats, right_stats, left_basis, right_basis))
    new_weights = new_master.astype(jnp.bfloat16)
    small_first_new, small_second_new, small_new = small_step(totals[4], small_params, small_first, small_second, shrink)
    return (outputs, input_grad, new_first, new_second, new_master, new_weights, new_left, new_right, left_next, right_next, small_first_new, small_second_new, small_new)
```

```python
import math

import jax
import jax.numpy as jnp
from jax import lax
from jax.experimental import pallas as pl
from jax.experimental.pallas import tpu as pltpu
from jax.sharding import PartitionSpec as P

D = 2048
H = 16
HD = 128
FF = 8192
PROMPT = 1024
STEP = 5
NS_ITERS = 3
SEQ = 2048
BQ = 256
BF = jnp.bfloat16
F32 = jnp.float32
SCALE = HD ** (-0.5)
LOG2E = 1.4426950408889634
VMEM_CAP = 56 * 1024 * 1024


def dot_nt(a, b):
    return lax.dot_general(a, b, (((1,), (1,)), ((), ())), preferred_element_type=F32)


def dot_tn(a, b):
    return lax.dot_general(a, b, (((0,), (0,)), ((), ())), preferred_element_type=F32)


def dot_nn(a, b):
    return lax.dot_general(a, b, (((1,), (0,)), ((), ())), preferred_element_type=F32)


def key_parts(lo):
    if lo < PROMPT:
        return ([(0, lo, False)] if lo else []) + [(lo, lo + BQ, True)]
    return [(0, PROMPT, False), (PROMPT, lo + BQ, True)]


def part_scores(keys, query_block, lo, part, start_row):
    first, last, masked = part
    product = dot_nt(keys[first:last], query_block)
    if masked:
        key_pos = first + lax.broadcasted_iota(jnp.int32, product.shape, 0)
        query_pos = lo + lax.broadcasted_iota(jnp.int32, product.shape, 1)
        seen = (key_pos <= query_pos) & (key_pos >= start_row)
        product = jnp.where(seen, product, -1e30)
    return product


def softmax_parts(scores):
    top = scores[0].max(axis=0, keepdims=True)
    for piece in scores[1:]:
        top = jnp.maximum(top, piece.max(axis=0, keepdims=True))
    weights = [jnp.exp2((piece - top) * (SCALE * LOG2E)) for piece in scores]
    total = weights[0].sum(axis=0, keepdims=True)
    for piece in weights[1:]:
        total = total + piece.sum(axis=0, keepdims=True)
    return top, weights, total


def attend_kernel(start_ref, qkv_ref, out_ref, peak_ref):
    keys = qkv_ref[:, HD : 2 * HD]
    values_t = qkv_ref[:, 2 * HD :].T
    peak = jnp.full((1, BQ), -1e30, F32)
    for lo in range(0, SEQ, BQ):
        query_block = qkv_ref[lo : lo + BQ, :HD]
        start_row = start_ref[:, lo : lo + BQ]
        parts = key_parts(lo)
        scores = [part_scores(keys, query_block, lo, part, start_row) for part in parts]
        top, weights, total = softmax_parts(scores)
        peak = jnp.maximum(peak, top)
        mixed = None
        for (first, last, _), piece in zip(parts, weights):
            term = dot_nn(values_t[:, first:last], piece.astype(BF))
            mixed = term if mixed is None else mixed + term
        out_ref[lo : lo + BQ, :] = (mixed * (1.0 / total)).T.astype(BF)
    peak_ref[...] = jnp.broadcast_to(peak.max(axis=1, keepdims=True) * SCALE, peak_ref.shape)


def attend(start_rows, qkv):
    heads = qkv.shape[1] // (3 * HD)
    return pl.pallas_call(
        attend_kernel,
        grid=(heads,),
        in_specs=[
            pl.BlockSpec((1, SEQ), lambda h: (0, 0)),
            pl.BlockSpec((SEQ, 3 * HD), lambda h: (0, h)),
        ],
        out_specs=[
            pl.BlockSpec((SEQ, HD), lambda h: (0, h)),
            pl.BlockSpec((1, 8, HD), lambda h: (h, 0, 0)),
        ],
        out_shape=[
            jax.ShapeDtypeStruct((SEQ, heads * HD), BF),
            jax.ShapeDtypeStruct((heads, 8, HD), F32),
        ],
        compiler_params=pltpu.CompilerParams(vmem_limit_bytes=VMEM_CAP),
        cost_estimate=pl.CostEstimate(
            flops=heads * SEQ * SEQ * HD * 4, bytes_accessed=heads * SEQ * HD * 8, transcendentals=heads * SEQ * SEQ // 2
        ),
        name="attend",
    )(start_rows, qkv)


def attend_back_kernel(start_ref, qkv_ref, back_ref, out_ref, key_acc, value_acc):
    keys = qkv_ref[:, HD : 2 * HD]
    values = qkv_ref[:, 2 * HD :]
    keys_t = keys.T
    key_acc[...] = jnp.zeros_like(key_acc)
    value_acc[...] = jnp.zeros_like(value_acc)
    for lo in range(0, SEQ, BQ):
        query_block = qkv_ref[lo : lo + BQ, :HD]
        back_block = back_ref[lo : lo + BQ, :]
        start_row = start_ref[:, lo : lo + BQ]
        parts = key_parts(lo)
        scores = [part_scores(keys, query_block, lo, part, start_row) for part in parts]
        top, weights, total = softmax_parts(scores)
        inverse = 1.0 / total
        probs = [piece * inverse for piece in weights]
        grads = [dot_nt(values[first:last], back_block) for first, last, _ in parts]
        mean = None
        for piece, grad in zip(probs, grads):
            term = (piece * grad).sum(axis=0, keepdims=True)
            mean = term if mean is None else mean + term
        query_t = None
        for (first, last, _), piece, grad in zip(parts, probs, grads):
            low = (piece * ((grad - mean) * SCALE)).astype(BF)
            value_acc[first:last, :] += dot_nn(piece.astype(BF), back_block)
            key_acc[first:last, :] += dot_nn(low, query_block)
            term = dot_nn(keys_t[:, first:last], low)
            query_t = term if query_t is None else query_t + term
        out_ref[lo : lo + BQ, :HD] = query_t.T.astype(BF)
    out_ref[:, HD : 2 * HD] = key_acc[...].astype(BF)
    out_ref[:, 2 * HD :] = value_acc[...].astype(BF)


def attend_back(start_rows, qkv, back):
    heads = qkv.shape[1] // (3 * HD)
    return pl.pallas_call(
        attend_back_kernel,
        grid=(heads,),
        in_specs=[
            pl.BlockSpec((1, SEQ), lambda h: (0, 0)),
            pl.BlockSpec((SEQ, 3 * HD), lambda h: (0, h)),
            pl.BlockSpec((SEQ, HD), lambda h: (0, h)),
        ],
        out_specs=pl.BlockSpec((SEQ, 3 * HD), lambda h: (0, h)),
        out_shape=jax.ShapeDtypeStruct(qkv.shape, BF),
        scratch_shapes=[pltpu.VMEM((SEQ, HD), F32), pltpu.VMEM((SEQ, HD), F32)],
        compiler_params=pltpu.CompilerParams(vmem_limit_bytes=VMEM_CAP),
        cost_estimate=pl.CostEstimate(
            flops=heads * SEQ * SEQ * HD * 10, bytes_accessed=heads * SEQ * HD * 14, transcendentals=heads * SEQ * SEQ // 2
        ),
        name="attend_back",
    )(start_rows, qkv, back)


TILE_GROUP = 8


def orthonormal_all(matrices):
    currents = []
    for matrix in matrices:
        frob = jnp.sqrt(jnp.sum(matrix * matrix, axis=(0, 1), keepdims=True))
        currents.append(matrix * (1.0 / (frob + 1e-06)))
    for _ in range(NS_ITERS):
        lows = [current.astype(BF) for current in currents]
        grams = [dot_nt(low, low).astype(BF) for low in lows]
        terms = [dot_nn(gram, low) for gram, low in zip(grams, lows)]
        currents = [1.5 * current - 0.5 * term for current, term in zip(currents, terms)]
    return currents


def update_kernel(tile_group, turned_grad, token_count, *refs):
    rate_ref, factor_ref, grad_ref = refs[:3]
    master_ref, first_ref, second_ref, left_stat_ref, right_stat_ref, left_ref, right_ref = refs[3:10]
    outs = refs[-8:]
    first_out, second_out, master_out, weight_out, left_stat_out, right_stat_out, left_out, right_out = outs
    base = pl.program_id(0) * tile_group
    group = range(tile_group)
    grads = [grad_ref[i] for i in group]
    lefts = [left_ref[i].astype(BF) for i in group]
    rights = [right_ref[i].astype(BF) for i in group]
    if turned_grad:
        outer_rows = [dot_tn(grad, grad) for grad in grads]
        outer_cols = [dot_nt(grad, grad) for grad in grads]
        halves = [dot_nn(grad, left).astype(BF) for grad, left in zip(grads, lefts)]
        rotated = [dot_tn(half, right) for half, right in zip(halves, rights)]
    else:
        outer_rows = [dot_nt(grad, grad) for grad in grads]
        outer_cols = [dot_tn(grad, grad) for grad in grads]
        halves = [dot_nn(grad, right).astype(BF) for grad, right in zip(grads, rights)]
        rotated = [dot_tn(left, half) for left, half in zip(lefts, halves)]
    directions = []
    for i in group:
        new_first = 0.5 * first_ref[i] + 0.5 * rotated[i]
        new_second = 0.5 * second_ref[i] + 0.5 * rotated[i] * rotated[i]
        first_out[i] = new_first
        second_out[i] = new_second
        direction = (
            new_first
            * (1.0 / (1.0 - 0.5**STEP))
            / (jnp.sqrt(new_second * (1.0 / (1.0 - 0.5**STEP))) + 1e-08)
        )
        directions.append(direction.astype(BF))
    turned = [dot_nn(left, direction).astype(BF) for left, direction in zip(lefts, directions)]
    turned = [dot_nt(half, right) for half, right in zip(turned, rights)]
    for i in group:
        master = master_ref[i]
        new_master = (master - rate_ref[base + i] * (turned[i] + 0.1 * master)) * factor_ref[base + i]
        master_out[i] = new_master
        weight_out[i] = new_master.astype(BF)
    moved = []
    for stat_ref, stat_out, outers, bases in (
        (left_stat_ref, left_stat_out, outer_rows, lefts),
        (right_stat_ref, right_stat_out, outer_cols, rights),
    ):
        for i in group:
            new_stat = 0.5 * stat_ref[i] + (0.5 / (HD * token_count)) * outers[i]
            stat_out[i] = new_stat
            moved.append(dot_nn(new_stat.astype(BF), bases[i]))
    moved = orthonormal_all(moved)
    for i in group:
        left_out[i] = moved[i]
        right_out[i] = moved[tile_group + i]


def update_tiles(grads, state, rates, factors, first_tile, earlier, turned_grad, token_count):
    count = grads.shape[0]
    tiles = state[0].shape[0]
    group = math.gcd(math.gcd(count, first_tile), TILE_GROUP)
    offset = first_tile // group
    block = (group, HD, HD)
    here = pl.BlockSpec(block, lambda i: (i + offset, 0, 0))
    smem = pl.BlockSpec(memory_space=pltpu.SMEM)
    kinds = [F32, F32, F32, BF, F32, F32, F32, F32]
    earlier = list(earlier) if earlier is not None else []

    def body(*refs):
        update_kernel(group, turned_grad, token_count, *refs)

    return pl.pallas_call(
        body,
        grid=(count // group,),
        in_specs=[smem, smem, pl.BlockSpec(block, lambda i: (i, 0, 0))]
        + [here] * 7
        + [pl.BlockSpec(memory_space=pl.ANY)] * len(earlier),
        out_specs=[here] * 8,
        out_shape=[jax.ShapeDtypeStruct((tiles, HD, HD), kind) for kind in kinds],
        input_output_aliases={10 + i: i for i in range(len(earlier))},
        compiler_params=pltpu.CompilerParams(vmem_limit_bytes=VMEM_CAP),
        cost_estimate=pl.CostEstimate(
            flops=count * 20 * HD**3 * 2 * 4, bytes_accessed=count * HD * HD * 56, transcendentals=count * HD * HD * 2
        ),
        name="update_tiles",
    )(rates[first_tile : first_tile + count], factors[first_tile : first_tile + count], grads, *state, *earlier)


def grad_kernel(chunks, block_ref, *refs):
    lefts, rights, out_ref = refs[:chunks], refs[chunks : 2 * chunks], refs[2 * chunks]
    width = out_ref.shape[2]
    step = min(512, width)
    for lo in range(0, width, step):
        total = None
        for left, right in zip(lefts, rights):
            term = dot_tn(left[...], right[:, lo : lo + step])
            total = term if total is None else total + term
        out_ref[0, :, lo : lo + step] = total.astype(BF)


def grad_blocks(blocks, lefts, rights, edge):
    count = blocks.shape[0]
    width = rights[0].shape[1]
    rows = sum(left.shape[0] for left in lefts)
    chunks = len(lefts)

    def body(*refs):
        grad_kernel(chunks, *refs)

    return pl.pallas_call(
        body,
        grid_spec=pltpu.PrefetchScalarGridSpec(
            num_scalar_prefetch=1,
            grid=(count,),
            in_specs=[pl.BlockSpec((left.shape[0], edge), lambda i, blocks: (0, blocks[i])) for left in lefts]
            + [pl.BlockSpec(right.shape, lambda i, blocks: (0, 0)) for right in rights],
            out_specs=pl.BlockSpec((1, edge, width), lambda i, blocks: (i, 0, 0)),
        ),
        out_shape=jax.ShapeDtypeStruct((count, edge, width), BF),
        compiler_params=pltpu.CompilerParams(vmem_limit_bytes=VMEM_CAP),
        cost_estimate=pl.CostEstimate(
            flops=2 * count * edge * width * rows,
            bytes_accessed=2 * (count * edge * (width + rows) + rows * width),
            transcendentals=0,
        ),
        name="grad_blocks",
    )(blocks, *lefts, *rights)


def shift(value, axis, mask):
    return lax.ppermute(value, axis, [(i, i ^ mask) for i in range(lax.axis_size(axis))])


def add_low(left, right):
    return (left.astype(F32) + right.astype(F32)).astype(BF)


def chip_gather(value, masks):
    pieces = {0: value}
    for mask in masks:
        pieces.update({q | (mask >> 1): shift(piece, "dp", mask) for q, piece in pieces.items()})
    return [pieces[q] for q in range(len(pieces))]


def chip_reduce(pieces, masks):
    pieces = dict(enumerate(pieces))
    for mask in masks:
        bit = mask >> 1
        pieces = {
            q: add_low(piece, shift(pieces[q | bit], "dp", mask)) for q, piece in pieces.items() if not q & bit
        }
    return pieces[0]


def layer_norm(token_rows, gain, shift_by):
    centre = jnp.mean(token_rows, axis=-1, keepdims=True)
    centred = token_rows - centre
    spread = jnp.mean(centred * centred, axis=-1, keepdims=True)
    return centred * lax.rsqrt(spread + 1e-05) * gain + shift_by


def layer_norm_back(token_rows, gain, grad):
    centre = jnp.mean(token_rows, axis=-1, keepdims=True)
    centred = token_rows - centre
    inverse = lax.rsqrt(jnp.mean(centred * centred, axis=-1, keepdims=True) + 1e-05)
    normal = centred * inverse
    scaled = grad * gain
    back = (
        scaled - jnp.mean(scaled, axis=-1, keepdims=True) - normal * jnp.mean(scaled * normal, axis=-1, keepdims=True)
    ) * inverse
    return back, jnp.sum(grad * normal, axis=0), jnp.sum(grad, axis=0)


def gelu_pair(pre_act):
    cdf = 0.5 * (1.0 + lax.erf(pre_act * (0.5**0.5)))
    density = jnp.exp(-0.5 * pre_act * pre_act) * 0.3989422804014327
    return pre_act * cdf, cdf + pre_act * density


def small_step(summed, params, first, second):
    new_first = 0.5 * first + 0.5 * summed
    new_second = 0.5 * second + 0.5 * summed * summed
    direction = new_first / (1.0 - 0.5**STEP) / (jnp.sqrt(new_second / (1.0 - 0.5**STEP)) + 1e-08)
    return new_first, new_second, params - 0.1 * direction


def per_device(
    inputs,
    cotangent,
    lengths,
    held_blocks,
    master,
    first_moment,
    second_moment,
    left_stats,
    right_stats,
    left_basis,
    right_basis,
    small_params,
    small_first,
    small_second,
):
    dp_count = lax.axis_size("dp")
    tp_count = lax.axis_size("tensor")
    me = lax.axis_index("dp")
    place = lax.axis_index("tensor")
    core = me & 1
    first_core = core == 0
    rows = inputs.shape[0]
    edge = D // dp_count
    width = D // tp_count
    hidden = FF // tp_count
    half = hidden // 2
    heads = width // HD
    edge_tiles = edge // HD
    hidden_tiles = hidden // HD
    tile_q = edge_tiles * 3 * heads
    tile_o = heads * edge_tiles
    tile_u = edge_tiles * hidden_tiles
    tile_count = master.shape[2]
    near = [1 << bit for bit in range(1, dp_count.bit_length() - 1)]
    far = near[::-1]
    slices = tp_count // 2
    inverse = jnp.argsort(held_blocks, axis=1).astype(jnp.int32)
    relative = jnp.arange(dp_count, dtype=jnp.int32) ^ me
    block_of = jnp.take(held_blocks, relative, axis=1)
    source_of = inverse ^ me

    bias_q = lax.dynamic_slice_in_dim(small_params, place * width, width)
    bias_v = lax.dynamic_slice_in_dim(small_params, D + place * width, width)
    bias_o = small_params[2 * D : 3 * D]
    bias_two = small_params[3 * D : 4 * D]
    gain_one = small_params[4 * D : 5 * D]
    shift_one = small_params[5 * D : 6 * D]
    gain_two = small_params[6 * D : 7 * D]
    shift_two = small_params[7 * D : 8 * D]
    hidden_starts = [(place ^ (2 * j)) * hidden + core * half for j in range(slices)]
    bias_up = jnp.concatenate(
        [lax.dynamic_slice_in_dim(small_params, 8 * D + start, half) for start in hidden_starts]
    )

    token_rows = inputs.astype(F32)
    normed_one = layer_norm(token_rows, gain_one, shift_one).astype(BF)
    normed_all = lax.all_gather(normed_one, "tensor", axis=0, tiled=True)

    low = master[0, 0].astype(BF)
    bounds = [0, tile_q, tile_q + tile_o, tile_q + tile_o + tile_u, tile_count]
    own_qkv = low[: bounds[1]].reshape(edge_tiles, 3, heads, HD, HD).transpose(0, 3, 2, 1, 4).reshape(edge, 3 * width)
    own_out = low[bounds[1] : bounds[2]].reshape(heads, edge_tiles, HD, HD).transpose(1, 3, 0, 2).reshape(edge, width)
    own_up = low[bounds[2] : bounds[3]].reshape(edge_tiles, hidden_tiles, HD, HD).transpose(0, 2, 1, 3).reshape(edge, hidden)
    own_down = low[bounds[3] :].reshape(hidden_tiles, edge_tiles, HD, HD).transpose(1, 3, 0, 2).reshape(edge, hidden)

    def split_pair(own):
        part = own.shape[1] // 2
        mine = lax.dynamic_slice_in_dim(own, core * part, part, 1)
        other = lax.dynamic_slice_in_dim(own, (1 - core) * part, part, 1)
        return jnp.stack([mine, shift(other, "dp", 1)])

    def join_halves(mine, other):
        return jnp.concatenate([jnp.where(first_core, mine, other), jnp.where(first_core, other, mine)], axis=-1)

    def in_order(pieces, kind):
        whole = jnp.concatenate(pieces, axis=0)
        return jnp.take(whole, source_of[kind], axis=0).reshape(D, whole.shape[2])

    pieces_qkv = chip_gather(split_pair(own_qkv), near)
    mine_qkv = jnp.concatenate(pieces_qkv, axis=0)
    other_qkv = shift(mine_qkv, "dp", 1).reshape(dp_count // 2, 2, edge, -1)[:, ::-1].reshape(mine_qkv.shape)
    w_qkv = jnp.take(join_halves(mine_qkv, other_qkv), source_of[0], axis=0).reshape(D, 3 * width)

    pair_up = split_pair(own_up)
    pair_down = split_pair(own_down)
    pairs_up = [pair_up] + [shift(pair_up, "tensor", 2 * j) for j in range(1, slices)]
    pairs_down = [pair_down] + [shift(pair_down, "tensor", 2 * j) for j in range(1, slices)]

    pair_out = split_pair(own_out)
    pairs_out = jnp.stack([pair_out] + [shift(pair_out, "tensor", j) for j in range(1, tp_count)], axis=1)
    mine_out = jnp.concatenate(chip_gather(pairs_out, far), axis=0)
    other_out = shift(mine_out, "dp", 1).reshape((dp_count // 2, 2) + mine_out.shape[1:])[:, ::-1].reshape(mine_out.shape)
    w_out = jnp.take(join_halves(mine_out, other_out), source_of[1], axis=0)
    w_out = w_out.transpose(0, 2, 1, 3).reshape(D, D)

    w_up = jnp.concatenate([in_order(chip_gather(pair, near), 2) for pair in pairs_up], axis=1)
    w_down = jnp.concatenate([in_order(chip_gather(pair, far), 3) for pair in pairs_down], axis=1)

    bias_mixed = jnp.stack(
        [bias_q.reshape(heads, HD), jnp.zeros((heads, HD), F32), bias_v.reshape(heads, HD)], axis=1
    ).reshape(3 * width)
    qkv = (jnp.dot(normed_all, w_qkv, preferred_element_type=F32) + bias_mixed).astype(BF)
    ends = jnp.cumsum(lengths[0])
    spot = jnp.arange(SEQ, dtype=jnp.int32) - PROMPT
    started = jnp.max(jnp.where(ends[None, :] <= spot[:, None], ends[None, :], 0), axis=1)
    start_rows = jnp.where(spot < 0, 0, PROMPT + started).astype(jnp.int32)[None]
    attended, peaks = attend(start_rows, qkv)

    def rows_of(value, j):
        return lax.dynamic_slice_in_dim(value, (place ^ j) * rows, rows, 0)

    attended_rows = jnp.concatenate(
        [rows_of(attended, 0)] + [shift(rows_of(attended, j), "tensor", j) for j in range(1, tp_count)], axis=1
    )
    hidden_rows = token_rows + dot_nt(attended_rows, w_out) + bias_o
    normed_two = layer_norm(hidden_rows, gain_two, shift_two).astype(BF)

    def four_rows(value):
        sibling = shift(value, "dp", 1)
        across = shift(value, "tensor", 1)
        return [value, sibling, across, shift(across, "dp", 1)]

    def sum_rows(partial):
        near_rows = add_low(partial[0], shift(partial[1], "dp", 1))
        far_rows = add_low(partial[2], shift(partial[3], "dp", 1))
        return near_rows.astype(F32) + shift(far_rows, "tensor", 1).astype(F32)

    back_list = four_rows(cotangent)
    back_four = jnp.concatenate(back_list, axis=0)
    normed_four = jnp.concatenate(four_rows(normed_two), axis=0)
    grad_act = jnp.dot(back_four, w_down, preferred_element_type=F32).astype(BF)
    pre_act = jnp.dot(normed_four, w_up, preferred_element_type=F32) + bias_up
    activation, slope = gelu_pair(pre_act)
    activation = activation.astype(BF)
    grad_pre = (grad_act.astype(F32) * slope).astype(BF)
    grad_normed = dot_nt(grad_pre, w_up).astype(BF)
    grad_two = sum_rows([grad_normed[i * rows : (i + 1) * rows] for i in range(4)])
    grad_bias_up = jnp.sum(grad_pre, axis=0, dtype=F32)

    def ffn_grad(kind, left, right, masks):
        blocks = block_of[kind]
        bit = masks[0] >> 1
        order = [q for q in range(dp_count // 2) if q & bit] + [q for q in range(dp_count // 2) if not q & bit]
        pieces = [None] * len(order)
        for group in (order[: len(order) // 2], order[len(order) // 2 :]):
            picked = jnp.concatenate([blocks[2 * q : 2 * q + 2] for q in group])
            out = grad_blocks(picked, [left], [right], edge)
            for i, q in enumerate(group):
                pieces[q] = out[2 * i : 2 * i + 2]
        reduced = chip_reduce(pieces, masks).reshape(2, edge, slices, half)
        total = reduced[:, :, 0].astype(F32)
        for j in range(1, slices):
            total = total + shift(reduced[:, :, j], "tensor", 2 * j).astype(F32)
        total = total.astype(BF)
        return join_halves(total[0], shift(total[1], "dp", 1))

    sum_up = ffn_grad(2, normed_four, grad_pre, near)
    sum_down = ffn_grad(3, back_four, activation, far)

    result = dot_nt(activation, w_down).astype(BF)
    ffn_rows = sum_rows([result[i * rows : (i + 1) * rows] for i in range(4)])
    outputs = (hidden_rows + ffn_rows + bias_two).astype(BF)

    back_rows = cotangent.astype(F32)
    grad_part, grad_gain_two, grad_shift_two = layer_norm_back(hidden_rows, gain_two, grad_two)
    grad_hidden = back_rows + grad_part
    branch = grad_hidden.astype(BF)
    grad_attended_rows = jnp.dot(branch, w_out, preferred_element_type=F32).astype(BF)
    arrived = [
        grad_attended_rows[:, j * width : (j + 1) * width]
        if j == 0
        else shift(grad_attended_rows[:, j * width : (j + 1) * width], "tensor", j)
        for j in range(tp_count)
    ]
    grad_attended = jnp.zeros((SEQ, width), BF)
    for j in range(tp_count):
        grad_attended = lax.dynamic_update_slice_in_dim(grad_attended, arrived[j], (place ^ j) * rows, 0)
    grad_qkv_rows = attend_back(start_rows, qkv, grad_attended)

    def core_reduce(blocks):
        pairs = blocks.reshape(dp_count // 2, 2, edge, blocks.shape[2])
        return add_low(pairs[:, 0], shift(pairs[:, 1], "dp", 1))

    def full_reduce(blocks):
        summed = core_reduce(blocks)
        part = summed.shape[2] // 2
        left = chip_reduce([summed[q, :, :part] for q in range(dp_count // 2)], near)
        right = chip_reduce([summed[q, :, part:] for q in range(dp_count // 2)], far)
        return jnp.concatenate([left, right], axis=1)

    sum_out = full_reduce(grad_blocks(block_of[1], [branch], [attended_rows], edge))
    total_out = sum_out[:, :width].astype(F32)
    for j in range(1, tp_count):
        total_out = total_out + shift(sum_out[:, j * width : (j + 1) * width], "tensor", j).astype(F32)
    sum_out = total_out.astype(BF)

    grad_normed_one = lax.psum_scatter(
        dot_nt(grad_qkv_rows, w_qkv).astype(BF), "tensor", scatter_dimension=0, tiled=True
    ).astype(F32)
    sum_qkv = full_reduce(grad_blocks(block_of[0], [normed_all], [grad_qkv_rows], edge))
    rows_part, grad_gain_one, grad_shift_one = layer_norm_back(token_rows, gain_one, grad_normed_one)
    input_grad = (grad_hidden + rows_part).astype(BF)

    column_sums = jnp.sum(grad_qkv_rows, axis=0, dtype=F32).reshape(heads, 3, HD)
    head_sums = lambda part: lax.dynamic_update_slice(
        jnp.zeros((D,), F32), column_sums[:, part].reshape(width), (place * width,)
    )
    wide = jnp.zeros((FF,), F32)
    for j in range(slices):
        wide = lax.dynamic_update_slice(wide, grad_bias_up[j * half : (j + 1) * half], (hidden_starts[j],))
    peak_row = lax.dynamic_update_slice(
        jnp.zeros((dp_count * H,), F32), peaks[:, 0, 0], (me * H + place * heads,)
    )
    early = lax.psum(
        jnp.concatenate(
            [
                head_sums(0),
                head_sums(2),
                jnp.sum(branch, axis=0, dtype=F32),
                jnp.sum(cotangent, axis=0, dtype=F32),
                grad_gain_two,
                grad_shift_two,
                wide,
                peak_row,
            ]
        ),
        ("dp", "tensor"),
    )
    late = lax.psum(jnp.concatenate([grad_gain_one, grad_shift_one]), ("dp", "tensor"))
    grad_small = jnp.concatenate([early[: 4 * D], late, early[4 * D : 6 * D + FF]])
    peak_all = jnp.max(early[6 * D + FF :].reshape(dp_count, H), axis=0)
    shrink = jnp.sqrt(1.0 / jnp.maximum(peak_all, 1.0))
    small_first_new, small_second_new, small_new = small_step(grad_small, small_params, small_first, small_second)
    small_new = jnp.concatenate([(small_new[:D].reshape(H, HD) * shrink[:, None]).reshape(D), small_new[D:]])

    index = jnp.arange(tile_count, dtype=jnp.int32)
    rates = jnp.where(
        index < bounds[1],
        D ** (-0.5),
        jnp.where(index < bounds[2], (SEQ / (2.0 * D)) ** 0.5, jnp.where(index < bounds[3], D ** (-0.5), FF ** (-0.5))),
    ).astype(F32)
    column = index % (3 * heads)
    shrink_here = lax.dynamic_slice_in_dim(shrink, place * heads, heads)
    factors = jnp.where((index < bounds[1]) & (column < 2 * heads), shrink_here[column % heads], 1.0)
    ones = jnp.ones((tile_count,), F32)
    token_count = float(dp_count * SEQ)
    state = [value[0, 0] for value in (master, first_moment, second_moment, left_stats, right_stats, left_basis, right_basis)]
    tiles_up = sum_up.reshape(edge_tiles, HD, hidden_tiles, HD).transpose(0, 2, 1, 3).reshape(tile_u, HD, HD)
    tiles_down = sum_down.reshape(edge_tiles, HD, hidden_tiles, HD).transpose(2, 0, 1, 3).reshape(tile_u, HD, HD)
    tiles_out = sum_out.reshape(edge_tiles, HD, heads, HD).transpose(2, 0, 1, 3).reshape(tile_o, HD, HD)
    tiles_qkv = sum_qkv.reshape(edge_tiles, HD, heads, 3, HD).transpose(0, 3, 2, 1, 4).reshape(tile_q, HD, HD)
    done = update_tiles(tiles_down, state, rates, ones, bounds[3], None, True, token_count)
    done = update_tiles(tiles_up, state, rates, ones, bounds[2], done, False, token_count)
    done = update_tiles(tiles_out, state, rates, ones, bounds[1], done, True, token_count)
    done = update_tiles(tiles_qkv, state, rates, factors, 0, done, False, token_count)
    return (
        outputs,
        input_grad,
        *[value[None, None] for value in done],
        small_first_new,
        small_second_new,
        small_new,
    )


def solution(mesh):
    rows = P(("dp", "tensor"), None)
    tiles = P("dp", "tensor", None, None, None)
    return jax.shard_map(
        per_device,
        mesh=mesh,
        in_specs=(rows, rows, P("dp", None), P()) + (tiles,) * 7 + (P(), P(), P()),
        out_specs=(rows, rows) + (tiles,) * 8 + (P(), P(), P()),
        check_vma=False,
    )
```

```python
import math

import jax
import jax.numpy as jnp
from jax import lax
from jax.experimental import pallas as pl
from jax.experimental.pallas import tpu as pltpu
from jax.sharding import PartitionSpec as P

D = 2048
H = 16
HD = 128
FF = 8192
PROMPT = 1024
STEP = 5
NS_ITERS = 3
SEQ = 2048
BQ = 256
BF = jnp.bfloat16
F32 = jnp.float32
SCALE = HD ** (-0.5)
LOG2E = 1.4426950408889634
VMEM_CAP = 56 * 1024 * 1024


def cost(seconds):
    return pl.CostEstimate(flops=0, bytes_accessed=int(seconds * 3.5e12), transcendentals=0)


def dot_nt(a, b):
    return lax.dot_general(a, b, (((1,), (1,)), ((), ())), preferred_element_type=F32)


def dot_tn(a, b):
    return lax.dot_general(a, b, (((0,), (0,)), ((), ())), preferred_element_type=F32)


def dot_nn(a, b):
    return lax.dot_general(a, b, (((1,), (0,)), ((), ())), preferred_element_type=F32)


def key_parts(lo):
    if lo < PROMPT:
        return ([(0, lo, False)] if lo else []) + [(lo, lo + BQ, True)]
    return [(0, PROMPT, False), (PROMPT, lo + BQ, True)]


def part_scores(keys, query_block, lo, part, start_row):
    first, last, masked = part
    product = dot_nt(keys[first:last], query_block)
    if masked:
        key_pos = first + lax.broadcasted_iota(jnp.int32, product.shape, 0)
        query_pos = lo + lax.broadcasted_iota(jnp.int32, product.shape, 1)
        seen = (key_pos <= query_pos) & (key_pos >= start_row)
        product = jnp.where(seen, product, -1e30)
    return product


def softmax_parts(scores):
    top = scores[0].max(axis=0, keepdims=True)
    for piece in scores[1:]:
        top = jnp.maximum(top, piece.max(axis=0, keepdims=True))
    weights = [jnp.exp2((piece - top) * (SCALE * LOG2E)) for piece in scores]
    total = weights[0].sum(axis=0, keepdims=True)
    for piece in weights[1:]:
        total = total + piece.sum(axis=0, keepdims=True)
    return top, weights, total


def attend_kernel(start_ref, qkv_ref, out_ref, peak_ref):
    keys = qkv_ref[:, HD : 2 * HD]
    values_t = qkv_ref[:, 2 * HD :].T
    peak = jnp.full((1, BQ), -1e30, F32)
    for lo in range(0, SEQ, BQ):
        query_block = qkv_ref[lo : lo + BQ, :HD]
        start_row = start_ref[:, lo : lo + BQ]
        parts = key_parts(lo)
        scores = [part_scores(keys, query_block, lo, part, start_row) for part in parts]
        top, weights, total = softmax_parts(scores)
        peak = jnp.maximum(peak, top)
        mixed = None
        for (first, last, _), piece in zip(parts, weights):
            term = dot_nn(values_t[:, first:last], piece.astype(BF))
            mixed = term if mixed is None else mixed + term
        out_ref[lo : lo + BQ, :] = (mixed * (1.0 / total)).T.astype(BF)
    peak_ref[...] = jnp.broadcast_to(peak.max(axis=1, keepdims=True) * SCALE, peak_ref.shape)


def attend(start_rows, qkv):
    heads = qkv.shape[1] // (3 * HD)
    return pl.pallas_call(
        attend_kernel,
        grid=(heads,),
        in_specs=[
            pl.BlockSpec((1, SEQ), lambda h: (0, 0)),
            pl.BlockSpec((SEQ, 3 * HD), lambda h: (0, h)),
        ],
        out_specs=[
            pl.BlockSpec((SEQ, HD), lambda h: (0, h)),
            pl.BlockSpec((1, 8, HD), lambda h: (h, 0, 0)),
        ],
        out_shape=[
            jax.ShapeDtypeStruct((SEQ, heads * HD), BF),
            jax.ShapeDtypeStruct((heads, 8, HD), F32),
        ],
        compiler_params=pltpu.CompilerParams(vmem_limit_bytes=VMEM_CAP),
        cost_estimate=cost(heads * 5e-6),
        name="attend",
    )(start_rows, qkv)


def attend_back_kernel(start_ref, qkv_ref, back_ref, out_ref, key_acc, value_acc):
    keys = qkv_ref[:, HD : 2 * HD]
    values = qkv_ref[:, 2 * HD :]
    keys_t = keys.T
    key_acc[...] = jnp.zeros_like(key_acc)
    value_acc[...] = jnp.zeros_like(value_acc)
    for lo in range(0, SEQ, BQ):
        query_block = qkv_ref[lo : lo + BQ, :HD]
        back_block = back_ref[lo : lo + BQ, :]
        start_row = start_ref[:, lo : lo + BQ]
        parts = key_parts(lo)
        scores = [part_scores(keys, query_block, lo, part, start_row) for part in parts]
        top, weights, total = softmax_parts(scores)
        inverse = 1.0 / total
        probs = [piece * inverse for piece in weights]
        grads = [dot_nt(values[first:last], back_block) for first, last, _ in parts]
        mean = None
        for piece, grad in zip(probs, grads):
            term = (piece * grad).sum(axis=0, keepdims=True)
            mean = term if mean is None else mean + term
        query_t = None
        for (first, last, _), piece, grad in zip(parts, probs, grads):
            low = (piece * ((grad - mean) * SCALE)).astype(BF)
            value_acc[first:last, :] += dot_nn(piece.astype(BF), back_block)
            key_acc[first:last, :] += dot_nn(low, query_block)
            term = dot_nn(keys_t[:, first:last], low)
            query_t = term if query_t is None else query_t + term
        out_ref[lo : lo + BQ, :HD] = query_t.T.astype(BF)
    out_ref[:, HD : 2 * HD] = key_acc[...].astype(BF)
    out_ref[:, 2 * HD :] = value_acc[...].astype(BF)


def attend_back(start_rows, qkv, back):
    heads = qkv.shape[1] // (3 * HD)
    return pl.pallas_call(
        attend_back_kernel,
        grid=(heads,),
        in_specs=[
            pl.BlockSpec((1, SEQ), lambda h: (0, 0)),
            pl.BlockSpec((SEQ, 3 * HD), lambda h: (0, h)),
            pl.BlockSpec((SEQ, HD), lambda h: (0, h)),
        ],
        out_specs=pl.BlockSpec((SEQ, 3 * HD), lambda h: (0, h)),
        out_shape=jax.ShapeDtypeStruct(qkv.shape, BF),
        scratch_shapes=[pltpu.VMEM((SEQ, HD), F32), pltpu.VMEM((SEQ, HD), F32)],
        compiler_params=pltpu.CompilerParams(vmem_limit_bytes=VMEM_CAP),
        cost_estimate=cost(heads * 10e-6),
        name="attend_back",
    )(start_rows, qkv, back)


TILE_GROUP = 8


def orthonormal_all(matrices):
    currents = []
    for matrix in matrices:
        frob = jnp.sqrt(jnp.sum(matrix * matrix, axis=(0, 1), keepdims=True))
        currents.append(matrix * (1.0 / (frob + 1e-06)))
    for _ in range(NS_ITERS):
        lows = [current.astype(BF) for current in currents]
        grams = [dot_nt(low, low).astype(BF) for low in lows]
        terms = [dot_nn(gram, low) for gram, low in zip(grams, lows)]
        currents = [1.5 * current - 0.5 * term for current, term in zip(currents, terms)]
    return currents


def update_kernel(tile_group, turned_grad, token_count, *refs):
    rate_ref, factor_ref, grad_ref = refs[:3]
    master_ref, first_ref, second_ref, left_stat_ref, right_stat_ref, left_ref, right_ref = refs[3:10]
    outs = refs[-8:]
    first_out, second_out, master_out, weight_out, left_stat_out, right_stat_out, left_out, right_out = outs
    base = pl.program_id(0) * tile_group
    group = range(tile_group)
    grads = [grad_ref[i] for i in group]
    lefts = [left_ref[i].astype(BF) for i in group]
    rights = [right_ref[i].astype(BF) for i in group]
    if turned_grad:
        outer_rows = [dot_tn(grad, grad) for grad in grads]
        outer_cols = [dot_nt(grad, grad) for grad in grads]
        halves = [dot_nn(grad, left).astype(BF) for grad, left in zip(grads, lefts)]
        rotated = [dot_tn(half, right) for half, right in zip(halves, rights)]
    else:
        outer_rows = [dot_nt(grad, grad) for grad in grads]
        outer_cols = [dot_tn(grad, grad) for grad in grads]
        halves = [dot_nn(grad, right).astype(BF) for grad, right in zip(grads, rights)]
        rotated = [dot_tn(left, half) for left, half in zip(lefts, halves)]
    directions = []
    for i in group:
        new_first = 0.5 * first_ref[i] + 0.5 * rotated[i]
        new_second = 0.5 * second_ref[i] + 0.5 * rotated[i] * rotated[i]
        first_out[i] = new_first
        second_out[i] = new_second
        direction = (
            new_first
            * (1.0 / (1.0 - 0.5**STEP))
            / (jnp.sqrt(new_second * (1.0 / (1.0 - 0.5**STEP))) + 1e-08)
        )
        directions.append(direction.astype(BF))
    turned = [dot_nn(left, direction).astype(BF) for left, direction in zip(lefts, directions)]
    turned = [dot_nt(half, right) for half, right in zip(turned, rights)]
    for i in group:
        master = master_ref[i]
        new_master = (master - rate_ref[base + i] * (turned[i] + 0.1 * master)) * factor_ref[base + i]
        master_out[i] = new_master
        weight_out[i] = new_master.astype(BF)
    moved = []
    for stat_ref, stat_out, outers, bases in (
        (left_stat_ref, left_stat_out, outer_rows, lefts),
        (right_stat_ref, right_stat_out, outer_cols, rights),
    ):
        for i in group:
            new_stat = 0.5 * stat_ref[i] + (0.5 / (HD * token_count)) * outers[i]
            stat_out[i] = new_stat
            moved.append(dot_nn(new_stat.astype(BF), bases[i]))
    moved = orthonormal_all(moved)
    for i in group:
        left_out[i] = moved[i]
        right_out[i] = moved[tile_group + i]


def update_tiles(grads, state, rates, factors, first_tile, earlier, turned_grad, token_count):
    count = grads.shape[0]
    tiles = state[0].shape[0]
    group = math.gcd(math.gcd(count, first_tile), TILE_GROUP)
    offset = first_tile // group
    block = (group, HD, HD)
    here = pl.BlockSpec(block, lambda i: (i + offset, 0, 0))
    smem = pl.BlockSpec(memory_space=pltpu.SMEM)
    kinds = [F32, F32, F32, BF, F32, F32, F32, F32]
    earlier = list(earlier) if earlier is not None else []

    def body(*refs):
        update_kernel(group, turned_grad, token_count, *refs)

    return pl.pallas_call(
        body,
        grid=(count // group,),
        in_specs=[smem, smem, pl.BlockSpec(block, lambda i: (i, 0, 0))]
        + [here] * 7
        + [pl.BlockSpec(memory_space=pl.ANY)] * len(earlier),
        out_specs=[here] * 8,
        out_shape=[jax.ShapeDtypeStruct((tiles, HD, HD), kind) for kind in kinds],
        input_output_aliases={10 + i: i for i in range(len(earlier))},
        compiler_params=pltpu.CompilerParams(vmem_limit_bytes=VMEM_CAP),
        cost_estimate=cost(count * 5e-7),
        name="update_tiles",
    )(rates[first_tile : first_tile + count], factors[first_tile : first_tile + count], grads, *state, *earlier)


def grad_kernel(groups, block_ref, left_ref, *refs):
    rights, out_ref = refs[:groups], refs[groups]
    turned = left_ref[...].T
    lo = 0
    for right in rights:
        width = right.shape[1]
        step = min(512, width)
        for at in range(0, width, step):
            out_ref[0, :, lo + at : lo + at + step] = dot_nn(turned, right[:, at : at + step]).astype(BF)
        lo += width


def grad_blocks(blocks, left, rights, edge):
    count = blocks.shape[0]
    rows = rights[0].shape[0]
    width = sum(right.shape[1] for right in rights)

    def body(*refs):
        grad_kernel(len(rights), *refs)

    return pl.pallas_call(
        body,
        grid_spec=pltpu.PrefetchScalarGridSpec(
            num_scalar_prefetch=1,
            grid=(count,),
            in_specs=[pl.BlockSpec((rows, edge), lambda i, blocks: (0, blocks[i]))]
            + [pl.BlockSpec(right.shape, lambda i, blocks: (0, 0)) for right in rights],
            out_specs=pl.BlockSpec((1, edge, width), lambda i, blocks: (i, 0, 0)),
        ),
        out_shape=jax.ShapeDtypeStruct((count, edge, width), BF),
        compiler_params=pltpu.CompilerParams(vmem_limit_bytes=VMEM_CAP),
        cost_estimate=cost(2 * count * edge * width * rows / 8e14),
        name="grad_blocks",
    )(blocks, left, *rights)


def matmul_kernel(terms, *refs):
    lefts, rights, out_ref = refs[:terms], refs[terms : 2 * terms], refs[2 * terms]
    total = dot_nt(lefts[0][...], rights[0][...])
    for left, right in zip(lefts[1:], rights[1:]):
        total = total + dot_nt(left[...], right[...])
    out_ref[...] = total.astype(BF)


def matmul_sum(lefts, rights, first=0, rows=None):
    terms = len(lefts)
    depth = lefts[0].shape[1]
    rows = rows or lefts[0].shape[0]
    columns = rights[0].shape[0]
    row_step, step = min(1024, rows), min(512, columns)
    offset = first // row_step

    def body(*refs):
        matmul_kernel(terms, *refs)

    return pl.pallas_call(
        body,
        grid=(rows // row_step, columns // step),
        in_specs=[pl.BlockSpec((row_step, depth), lambda m, n: (m + offset, 0))] * terms
        + [pl.BlockSpec((step, depth), lambda m, n: (n, 0))] * terms,
        out_specs=pl.BlockSpec((row_step, step), lambda m, n: (m, n)),
        out_shape=jax.ShapeDtypeStruct((rows, columns), BF),
        compiler_params=pltpu.CompilerParams(vmem_limit_bytes=VMEM_CAP),
        cost_estimate=cost(2 * terms * rows * columns * depth / 8e14),
        name="matmul_sum",
    )(*lefts, *rights)


def pack_kernel(heads, edge_tiles, hidden_tiles, core_ref, tiles_ref, halves_ref, qkv_ref, out_ref):
    core = core_ref[0]
    half = hidden_tiles // 2 * HD
    first = 0
    for row in range(edge_tiles):
        for part in range(3):
            for head in range(heads):
                tile = tiles_ref[first + (row * 3 + part) * heads + head].astype(BF)
                at = (head * 3 + part) * HD
                qkv_ref[row * HD : (row + 1) * HD, at : at + HD] = tile
    first += edge_tiles * 3 * heads
    for head in range(heads):
        for row in range(edge_tiles):
            tile = tiles_ref[first + head * edge_tiles + row].T.astype(BF)
            out_ref[row * HD : (row + 1) * HD, head * HD : (head + 1) * HD] = tile
    first += heads * edge_tiles
    for kind in range(2):
        for row in range(edge_tiles):
            for column in range(hidden_tiles):
                part, inner = divmod(column, hidden_tiles // 2)
                at = kind * half + inner * HD
                if kind == 0:
                    tile = tiles_ref[first + row * hidden_tiles + column].astype(BF)
                else:
                    tile = tiles_ref[first + column * edge_tiles + row].T.astype(BF)
                halves_ref[part ^ core, row * HD : (row + 1) * HD, at : at + HD] = tile
        first += edge_tiles * hidden_tiles


def pack_weights(tiles, core, heads, edge_tiles, hidden_tiles):
    edge = edge_tiles * HD

    def body(*refs):
        pack_kernel(heads, edge_tiles, hidden_tiles, *refs)

    shapes = [(2, edge, hidden_tiles * HD), (edge, 3 * heads * HD), (edge, heads * HD)]
    return pl.pallas_call(
        body,
        grid_spec=pltpu.PrefetchScalarGridSpec(
            num_scalar_prefetch=1,
            grid=(1,),
            in_specs=[pl.BlockSpec(tiles.shape, lambda i, core: (0, 0, 0))],
            out_specs=[pl.BlockSpec(shapes[0], lambda i, core: (0, 0, 0))]
            + [pl.BlockSpec(shape, lambda i, core: (0, 0)) for shape in shapes[1:]],
        ),
        out_shape=[jax.ShapeDtypeStruct(shape, BF) for shape in shapes],
        compiler_params=pltpu.CompilerParams(vmem_limit_bytes=VMEM_CAP),
        cost_estimate=cost(5e-6),
        name="pack_weights",
    )(core[None], tiles)


def scatter_kernel(tables, *refs):
    source_ref, outs = refs[tables], refs[tables + 1 :]
    lo = 0
    for out in outs:
        width = out.shape[1]
        out[...] = source_ref[0, :, lo : lo + width]
        lo += width


def scatter_blocks(tables, source):
    count, edge, columns = source.shape
    parts = len(tables)
    width = columns // parts

    def body(*refs):
        scatter_kernel(parts, *refs)

    def out_spec(k):
        return pl.BlockSpec((edge, width), lambda i, *tables: (tables[k][i], 0))

    return pl.pallas_call(
        body,
        grid_spec=pltpu.PrefetchScalarGridSpec(
            num_scalar_prefetch=parts,
            grid=(count,),
            in_specs=[pl.BlockSpec((1, edge, columns), lambda i, *tables: (i, 0, 0))],
            out_specs=[out_spec(k) for k in range(parts)],
        ),
        out_shape=[jax.ShapeDtypeStruct((count * edge, width), BF)] * parts,
        compiler_params=pltpu.CompilerParams(vmem_limit_bytes=VMEM_CAP),
        cost_estimate=cost(4 * count * edge * columns / 3e12),
        name="scatter_blocks",
    )(*tables, source)


def project_kernel(sources, pick_ref, *refs):
    pieces = refs[:sources]
    gain_ref, shift_ref, weight_ref, bias_ref, normal_out, normed_out, out_ref = refs[sources:]
    picked = pick_ref[pl.program_id(0)]
    for i in range(sources):

        @pl.when(picked == i)
        def _():
            normal_out[...] = pieces[i][...]

    normed = (normal_out[...].astype(F32) * gain_ref[...] + shift_ref[...]).astype(BF)
    normed_out[...] = normed
    out_ref[...] = (dot_nn(normed, weight_ref[...]) + bias_ref[...]).astype(BF)


def project(pick, pieces, gain, shift_by, weight, bias):
    count = pick.shape[0]
    rows, depth = pieces[0].shape
    columns = weight.shape[1]

    def body(*refs):
        project_kernel(len(pieces), *refs)

    def held(shape):
        return pl.BlockSpec(shape, lambda t, pick: (0, 0), pipeline_mode=pl.Buffered(1))

    return pl.pallas_call(
        body,
        grid_spec=pltpu.PrefetchScalarGridSpec(
            num_scalar_prefetch=1,
            grid=(count,),
            in_specs=[held((rows, depth)) for _ in pieces]
            + [held((1, depth)), held((1, depth)), held((depth, columns)), held((1, columns))],
            out_specs=[
                pl.BlockSpec((rows, depth), lambda t, pick: (t, 0)),
                pl.BlockSpec((rows, depth), lambda t, pick: (t, 0)),
                pl.BlockSpec((rows, columns), lambda t, pick: (t, 0)),
            ],
        ),
        out_shape=[
            jax.ShapeDtypeStruct((count * rows, depth), BF),
            jax.ShapeDtypeStruct((count * rows, depth), BF),
            jax.ShapeDtypeStruct((count * rows, columns), BF),
        ],
        compiler_params=pltpu.CompilerParams(vmem_limit_bytes=VMEM_CAP),
        cost_estimate=cost(2e-5),
        name="project",
    )(pick, *pieces, gain[None], shift_by[None], weight, bias[None])


def sync(*values):
    return lax.optimization_barrier(values)


def shift(value, axis, mask):
    return lax.ppermute(value, axis, [(i, i ^ mask) for i in range(lax.axis_size(axis))])


def move(value, axis, pairs):
    return lax.ppermute(value, axis, pairs)


def add_low(left, right):
    return (left.astype(F32) + right.astype(F32)).astype(BF)


def join_halves(mine, other):
    first = (lax.axis_index("dp") & 1) == 0
    return jnp.concatenate([jnp.where(first, mine, other), jnp.where(first, other, mine)], axis=-1)


def halving_order(chips, masks):
    return sorted(chips, key=lambda q: tuple(-(q & (mask >> 1)) for mask in masks))


def halve(blocks, masks):
    for mask in masks:
        count = blocks.shape[0] // 2
        blocks = add_low(blocks[count:], shift(blocks[:count], "dp", mask))
    return blocks


def layer_norm(token_rows, gain, shift_by):
    centre = jnp.mean(token_rows, axis=-1, keepdims=True)
    centred = token_rows - centre
    spread = jnp.mean(centred * centred, axis=-1, keepdims=True)
    return centred * lax.rsqrt(spread + 1e-05) * gain + shift_by


def layer_norm_back(token_rows, gain, grad):
    centre = jnp.mean(token_rows, axis=-1, keepdims=True)
    centred = token_rows - centre
    inverse = lax.rsqrt(jnp.mean(centred * centred, axis=-1, keepdims=True) + 1e-05)
    normal = centred * inverse
    scaled = grad * gain
    back = (
        scaled - jnp.mean(scaled, axis=-1, keepdims=True) - normal * jnp.mean(scaled * normal, axis=-1, keepdims=True)
    ) * inverse
    return back, jnp.sum(grad * normal, axis=0), jnp.sum(grad, axis=0)


def gelu_pair(pre_act):
    cdf = 0.5 * (1.0 + lax.erf(pre_act * (0.5**0.5)))
    density = jnp.exp(-0.5 * pre_act * pre_act) * 0.3989422804014327
    return pre_act * cdf, cdf + pre_act * density


def axis_sum(value, axis):
    for bit in range(lax.axis_size(axis).bit_length() - 1):
        value = value + shift(value, axis, 1 << bit)
    return value


def small_step(summed, params, first, second):
    new_first = 0.5 * first + 0.5 * summed
    new_second = 0.5 * second + 0.5 * summed * summed
    direction = new_first / (1.0 - 0.5**STEP) / (jnp.sqrt(new_second / (1.0 - 0.5**STEP)) + 1e-08)
    return new_first, new_second, params - 0.1 * direction


def per_device(
    inputs,
    cotangent,
    lengths,
    held_blocks,
    master,
    first_moment,
    second_moment,
    left_stats,
    right_stats,
    left_basis,
    right_basis,
    small_params,
    small_first,
    small_second,
):
    dp_count = lax.axis_size("dp")
    tp_count = lax.axis_size("tensor")
    me = lax.axis_index("dp")
    place = lax.axis_index("tensor")
    core = me & 1
    rows = inputs.shape[0]
    edge = D // dp_count
    width = D // tp_count
    hidden = FF // tp_count
    half = hidden // 2
    heads = width // HD
    edge_tiles = edge // HD
    hidden_tiles = hidden // HD
    tile_q = edge_tiles * 3 * heads
    tile_o = heads * edge_tiles
    tile_u = edge_tiles * hidden_tiles
    tile_count = master.shape[2]
    near = [1 << bit for bit in range(1, dp_count.bit_length() - 1)]
    far = near[::-1]
    slices = tp_count // 2
    chips = range(dp_count // 2)
    relative = jnp.arange(dp_count, dtype=jnp.int32) ^ me
    block_of = jnp.take(held_blocks, relative, axis=1)

    bias_q = lax.dynamic_slice_in_dim(small_params, place * width, width)
    bias_v = lax.dynamic_slice_in_dim(small_params, D + place * width, width)
    bias_o = small_params[2 * D : 3 * D]
    bias_two = small_params[3 * D : 4 * D]
    gain_one = small_params[4 * D : 5 * D]
    shift_one = small_params[5 * D : 6 * D]
    gain_two = small_params[6 * D : 7 * D]
    shift_two = small_params[7 * D : 8 * D]
    hidden_starts = [(place ^ (2 * j)) * hidden + core * half for j in range(slices)]
    bias_up = jnp.concatenate(
        [lax.dynamic_slice_in_dim(small_params, 8 * D + start, half) for start in hidden_starts]
    )

    token_rows = inputs.astype(F32)
    centred = token_rows - jnp.mean(token_rows, axis=-1, keepdims=True)
    spread = jnp.mean(centred * centred, axis=-1, keepdims=True)
    normal = (centred * lax.rsqrt(spread + 1e-05)).astype(BF)
    ups = [(i, i + 1) for i in range(tp_count - 1)]
    downs = [(i + 1, i) for i in range(tp_count - 1)]
    above, below = [move(normal, "tensor", downs)], [move(normal, "tensor", ups)]

    bounds = [0, tile_q, tile_q + tile_o, tile_q + tile_o + tile_u, tile_count]
    halves, own_qkv, own_out = pack_weights(master[0, 0], core, heads, edge_tiles, hidden_tiles)
    pair = jnp.stack([halves[0], shift(halves[1], "dp", 1)])
    same_core = [list(range(at, dp_count, 2)) for at in range(2)]
    pair_slots = jnp.arange(dp_count, dtype=jnp.int32) ^ core

    def gather_ffn(value):
        value = lax.all_gather(value, "dp", axis=0, tiled=True, axis_index_groups=same_core)
        return scatter_blocks([held_blocks[2][pair_slots], held_blocks[3][pair_slots]], value)

    def gather_all(kind, value):
        value = lax.all_gather(value, "dp", axis=0, tiled=False)
        return scatter_blocks([held_blocks[kind]], value)[0]

    def crossed(mask, odd):
        return [(i, i ^ mask) for i in range(tp_count) if ((i ^ (i >> 1)) & 1) == odd]

    w_qkv = gather_all(0, own_qkv)
    w_first = gather_ffn(pair)
    far_first, outs = [], []
    for step in range(1, tp_count):
        if step > 1:
            below.append(move(below[-1], "tensor", ups[step - 1 :]))
            above.append(move(above[-1], "tensor", downs[: tp_count - step]))
        if step == 2:
            outs = [shift(own_out, "tensor", j) for j in range(1, tp_count)]
        if step == tp_count - 1:
            far_first = [move(pair, "tensor", crossed(2 * j, 0)) for j in range(1, slices)]
            above, below, far_first, outs, pair, w_qkv = sync(above, below, far_first, outs, pair, w_qkv)
        else:
            above, below, outs, own_out, pair = sync(above, below, outs, own_out, pair)

    bias_mixed = jnp.stack(
        [bias_q.reshape(heads, HD), jnp.zeros((heads, HD), F32), bias_v.reshape(heads, HD)], axis=1
    ).reshape(3 * width)
    line = jnp.arange(tp_count, dtype=jnp.int32) - place
    pick = jnp.where(line < 0, -line, jnp.where(line > 0, tp_count - 1 + line, 0))
    normal_all, normed_all, qkv = project(pick, [normal] + below + above, gain_one, shift_one, w_qkv, bias_mixed)
    far_second = [move(pair, "tensor", crossed(2 * j, 1)) for j in range(1, slices)]
    w_out = gather_all(1, jnp.concatenate([own_out] + outs, axis=1))

    ends = jnp.cumsum(lengths[0])
    spot = jnp.arange(SEQ, dtype=jnp.int32) - PROMPT
    started = jnp.max(jnp.where(ends[None, :] <= spot[:, None], ends[None, :], 0), axis=1)
    start_rows = jnp.where(spot < 0, 0, PROMPT + started).astype(jnp.int32)[None]
    attended, peaks = attend(start_rows, qkv)
    others = range(1, slices)
    attended, far_second = sync(attended, far_second)

    def rows_of(value, j):
        return lax.dynamic_slice_in_dim(value, (place ^ j) * rows, rows, 0)

    attended_rows = jnp.concatenate(
        [rows_of(attended, 0)] + [shift(rows_of(attended, j), "tensor", j) for j in range(1, tp_count)], axis=1
    )
    w_far = [gather_ffn(left + right) for left, right in zip(far_first, far_second)]
    attended_rows, w_out, w_first, cotangent = sync(attended_rows, w_out, w_first, cotangent)
    peak_row = lax.dynamic_update_slice(
        jnp.zeros((dp_count * H,), F32), peaks[:, 0, 0], (me * H + place * heads,)
    )
    hidden_rows = token_rows + dot_nt(attended_rows, w_out) + bias_o
    normed_two = layer_norm(hidden_rows, gain_two, shift_two).astype(BF)

    normed_across = shift(normed_two, "tensor", 1)
    normed_sibling = shift(normed_two, "dp", 1)
    back_sibling = shift(cotangent, "dp", 1)
    normed_across, normed_sibling, back_sibling, cotangent, w_far = sync(
        normed_across, normed_sibling, back_sibling, cotangent, w_far
    )
    normed_four = jnp.concatenate(
        [normed_two, normed_sibling, normed_across, shift(normed_across, "dp", 1)], axis=0
    )
    w_up = [w_first[0]] + [value[0] for value in w_far]
    w_down = [w_first[1]] + [value[1] for value in w_far]

    parts = slices + 1
    marks = [16 * (rows // 16 * i // parts) for i in range(parts + 1)]
    back_pieces, activations, slopes = [], [], []
    for j in range(parts):
        back_pieces.append(shift(cotangent[marks[j] : marks[j + 1]], "tensor", 1))
        if j < slices:
            pre_act = jnp.dot(normed_four, w_up[j], preferred_element_type=F32) + bias_up[j * half : (j + 1) * half]
            activation, slope = gelu_pair(pre_act)
            activations.append(activation.astype(BF))
            slopes.append(slope.astype(BF))
        else:
            result_far = matmul_sum(activations, w_down, 2 * rows, 2 * rows)
            result_far, activations = sync(result_far, activations)
        activations, slopes, back_pieces, cotangent = sync(activations, slopes, back_pieces, cotangent)
    back_across = jnp.concatenate(back_pieces, axis=0)
    back_four = jnp.concatenate([cotangent, back_sibling, back_across, shift(back_across, "dp", 1)], axis=0)

    def core_rows(partial):
        return add_low(partial[:rows], shift(partial[rows:], "dp", 1))

    ffn_far = core_rows(result_far)
    blocks_down = grad_blocks(held_blocks[3][pair_slots], back_four, activations, edge)
    blocks_down, ffn_far, back_four = sync(blocks_down, ffn_far, back_four)

    def chips_sum(blocks):
        blocks = blocks.reshape(dp_count // 2, 2, edge, blocks.shape[2])
        return lax.psum_scatter(blocks, "dp", scatter_dimension=0, tiled=False, axis_index_groups=same_core)

    grads_pre, ffn_pieces = [], []
    for j in range(parts):
        ffn_pieces.append(shift(ffn_far[marks[j] : marks[j + 1]], "tensor", 1))
        if j < slices:
            grad_act = jnp.dot(back_four, w_down[j], preferred_element_type=F32)
            grads_pre.append((grad_act * slopes[j].astype(F32)).astype(BF))
        else:
            grad_normed = matmul_sum(grads_pre, w_up)
            grad_normed, grads_pre = sync(grad_normed, grads_pre)
        grads_pre, ffn_pieces, ffn_far = sync(grads_pre, ffn_pieces, ffn_far)
    ffn_across = jnp.concatenate(ffn_pieces, axis=0)
    far_rows = core_rows(grad_normed[2 * rows :])
    far_rows, grads_pre, activations = sync(far_rows, grads_pre, activations)
    middle = rows // 2
    far_low = shift(far_rows[:middle], "tensor", 1)
    blocks_up = grad_blocks(held_blocks[2][pair_slots], normed_four, grads_pre, edge)
    far_low, blocks_up, far_rows, activations = sync(far_low, blocks_up, far_rows, activations)
    far_high = shift(far_rows[middle:], "tensor", 1)
    near_rows = core_rows(grad_normed[: 2 * rows])
    result = matmul_sum(activations, w_down, 0, 2 * rows)
    far_high, near_rows, result = sync(far_high, near_rows, result)
    part_down, part_up = chips_sum(blocks_down), chips_sum(blocks_up)
    grad_two = near_rows.astype(F32) + jnp.concatenate([far_low, far_high], axis=0).astype(F32)

    grad_part, grad_gain_two, grad_shift_two = layer_norm_back(hidden_rows, gain_two, grad_two)
    grad_hidden = cotangent.astype(F32) + grad_part
    branch = grad_hidden.astype(BF)
    grad_attended_rows = jnp.dot(branch, w_out, preferred_element_type=F32).astype(BF)
    grad_attended_rows, branch, result, grads_pre = sync(grad_attended_rows, branch, result, grads_pre)

    arrived = [
        grad_attended_rows[:, j * width : (j + 1) * width]
        if j == 0
        else shift(grad_attended_rows[:, j * width : (j + 1) * width], "tensor", j)
        for j in range(tp_count)
    ]
    grad_attended = jnp.zeros((SEQ, width), BF)
    for j in range(tp_count):
        grad_attended = lax.dynamic_update_slice_in_dim(grad_attended, arrived[j], (place ^ j) * rows, 0)
    ffn_near = core_rows(result)
    grad_attended, branch, ffn_near, part_down, part_up = sync(grad_attended, branch, ffn_near, part_down, part_up)

    def far_slices(part):
        return part[:, :, :half], [part[:, :, j * half : (j + 1) * half] for j in others]

    def far_sum(kept, arrived):
        total = kept.astype(F32)
        for value in arrived:
            total = total + value.astype(F32)
        total = total.astype(BF)
        return join_halves(total[0], shift(total[1], "dp", 1))

    order_near, order_far = halving_order(chips, near), halving_order(chips, far)

    def half_slots(order):
        return jnp.array([2 * q + 1 for q in order] + [2 * q for q in order], jnp.int32)

    grad_qkv_rows = attend_back(start_rows, qkv, grad_attended)
    own_down, far_down = far_slices(part_down)
    own_up, far_up = far_slices(part_up)
    far_down = [shift(value, "tensor", 2 * j) for j, value in zip(others, far_down)]
    grad_qkv_rows, far_down, far_up, branch = sync(grad_qkv_rows, far_down, far_up, branch)

    up_low = [shift(value[:1], "tensor", 2 * j) for j, value in zip(others, far_up)]
    partial = dot_nt(grad_qkv_rows, w_qkv).astype(BF)
    partial, up_low, far_up, grad_qkv_rows = sync(partial, up_low, far_up, grad_qkv_rows)
    up_high = [shift(value[1:], "tensor", 2 * j) for j, value in zip(others, far_up)]
    grads_qkv = grad_blocks(block_of[0][half_slots(order_far)], normed_all, [grad_qkv_rows], edge)
    partial, up_high, grads_qkv, branch = sync(partial, up_high, grads_qkv, branch)
    far_up = [jnp.concatenate(value, axis=0) for value in zip(up_low, up_high)]
    grad_normed_one = lax.psum_scatter(partial, "tensor", scatter_dimension=0, tiled=True).astype(F32)

    grads_out = grad_blocks(block_of[1][half_slots(order_near)], branch, [attended_rows], edge)
    column_sums = jnp.sum(grad_qkv_rows, axis=0, dtype=F32).reshape(heads, 3, HD)
    head_sums = lambda part: lax.dynamic_update_slice(
        jnp.zeros((D,), F32), column_sums[:, part].reshape(width), (place * width,)
    )
    partial_wide = partial.astype(F32)
    grad_bias_up = jnp.concatenate([jnp.sum(value, axis=0, dtype=F32) for value in grads_pre])
    wide = jnp.zeros((FF,), F32)
    for j in range(slices):
        wide = lax.dynamic_update_slice(wide, grad_bias_up[j * half : (j + 1) * half], (hidden_starts[j],))
    totals = jnp.concatenate(
        [
            head_sums(0),
            head_sums(2),
            jnp.sum(branch, axis=0, dtype=F32),
            jnp.sum(cotangent, axis=0, dtype=F32),
            jnp.sum(partial_wide * normal_all.astype(F32), axis=0),
            jnp.sum(partial_wide, axis=0),
            grad_gain_two,
            grad_shift_two,
            wide,
            peak_row,
        ]
    )
    totals = axis_sum(totals, "dp")
    sum_qkv = halve(halve(grads_qkv, [1]), far)[0]
    sum_out = halve(halve(grads_out, [1]), near)[0]
    sum_down = far_sum(own_down, far_down)
    sum_up = far_sum(own_up, far_up)
    outputs = (hidden_rows + ffn_near.astype(F32) + ffn_across.astype(F32) + bias_two).astype(BF)
    grad_normed_one, sum_out, totals = sync(grad_normed_one, sum_out, totals)
    totals = axis_sum(totals, "tensor")
    grad_small = totals[: 8 * D + FF]
    peak_all = jnp.max(totals[8 * D + FF :].reshape(dp_count, H), axis=0)
    total_out = sum_out[:, :width].astype(F32)
    for j in range(1, tp_count):
        total_out = total_out + shift(sum_out[:, j * width : (j + 1) * width], "tensor", j).astype(F32)
    sum_out = total_out.astype(BF)
    rows_part, _, _ = layer_norm_back(token_rows, gain_one, grad_normed_one)
    input_grad = (grad_hidden + rows_part).astype(BF)

    shrink = jnp.sqrt(1.0 / jnp.maximum(peak_all, 1.0))
    small_first_new, small_second_new, small_new = small_step(grad_small, small_params, small_first, small_second)
    small_new = jnp.concatenate([(small_new[:D].reshape(H, HD) * shrink[:, None]).reshape(D), small_new[D:]])

    index = jnp.arange(tile_count, dtype=jnp.int32)
    rates = jnp.where(
        index < bounds[1],
        D ** (-0.5),
        jnp.where(index < bounds[2], (SEQ / (2.0 * D)) ** 0.5, jnp.where(index < bounds[3], D ** (-0.5), FF ** (-0.5))),
    ).astype(F32)
    column = index % (3 * heads)
    shrink_here = lax.dynamic_slice_in_dim(shrink, place * heads, heads)
    factors = jnp.where((index < bounds[1]) & (column < 2 * heads), shrink_here[column % heads], 1.0)
    ones = jnp.ones((tile_count,), F32)
    token_count = float(dp_count * SEQ)
    state = [value[0, 0] for value in (master, first_moment, second_moment, left_stats, right_stats, left_basis, right_basis)]
    tiles_up = sum_up.reshape(edge_tiles, HD, hidden_tiles, HD).transpose(0, 2, 1, 3).reshape(tile_u, HD, HD)
    tiles_down = sum_down.reshape(edge_tiles, HD, hidden_tiles, HD).transpose(2, 0, 1, 3).reshape(tile_u, HD, HD)
    tiles_out = sum_out.reshape(edge_tiles, HD, heads, HD).transpose(2, 0, 1, 3).reshape(tile_o, HD, HD)
    tiles_qkv = sum_qkv.reshape(edge_tiles, HD, heads, 3, HD).transpose(0, 3, 2, 1, 4).reshape(tile_q, HD, HD)
    done = update_tiles(tiles_down, state, rates, ones, bounds[3], None, True, token_count)
    done = update_tiles(tiles_up, state, rates, ones, bounds[2], done, False, token_count)
    done = update_tiles(tiles_qkv, state, rates, factors, 0, done, False, token_count)
    done = update_tiles(tiles_out, state, rates, ones, bounds[1], done, True, token_count)
    return (
        outputs,
        input_grad,
        *[value[None, None] for value in done],
        small_first_new,
        small_second_new,
        small_new,
    )


def solution(mesh):
    rows = P(("dp", "tensor"), None)
    tiles = P("dp", "tensor", None, None, None)
    return jax.shard_map(
        per_device,
        mesh=mesh,
        in_specs=(rows, rows, P("dp", None), P()) + (tiles,) * 7 + (P(), P(), P()),
        out_specs=(rows, rows) + (tiles,) * 8 + (P(), P(), P()),
        check_vma=False,
    )
```

```python
import math

import jax
import jax.numpy as jnp
from jax import lax
from jax.experimental import pallas as pl
from jax.experimental.pallas import tpu as pltpu
from jax.sharding import PartitionSpec as P

D = 2048
H = 16
HD = 128
FF = 8192
PROMPT = 1024
STEP = 5
NS_ITERS = 3
SEQ = 2048
BQ = 256
BF = jnp.bfloat16
F32 = jnp.float32
SCALE = HD ** (-0.5)
LOG2E = 1.4426950408889634
VMEM_CAP = 56 * 1024 * 1024


def cost(seconds):
    return pl.CostEstimate(flops=0, bytes_accessed=int(seconds * 3.5e12), transcendentals=0)


def dot_nt(a, b):
    return lax.dot_general(a, b, (((1,), (1,)), ((), ())), preferred_element_type=F32)


def dot_tn(a, b):
    return lax.dot_general(a, b, (((0,), (0,)), ((), ())), preferred_element_type=F32)


def dot_nn(a, b):
    return lax.dot_general(a, b, (((1,), (0,)), ((), ())), preferred_element_type=F32)


def key_parts(lo):
    if lo < PROMPT:
        return ([(0, lo, False)] if lo else []) + [(lo, lo + BQ, True)]
    return [(0, PROMPT, False), (PROMPT, lo + BQ, True)]


def part_scores(keys, query_block, lo, part, start_row):
    first, last, masked = part
    product = dot_nt(keys[first:last], query_block)
    if masked:
        key_pos = first + lax.broadcasted_iota(jnp.int32, product.shape, 0)
        query_pos = lo + lax.broadcasted_iota(jnp.int32, product.shape, 1)
        seen = (key_pos <= query_pos) & (key_pos >= start_row)
        product = jnp.where(seen, product, -1e30)
    return product


def softmax_parts(scores):
    top = scores[0].max(axis=0, keepdims=True)
    for piece in scores[1:]:
        top = jnp.maximum(top, piece.max(axis=0, keepdims=True))
    weights = [jnp.exp2((piece - top) * (SCALE * LOG2E)) for piece in scores]
    total = weights[0].sum(axis=0, keepdims=True)
    for piece in weights[1:]:
        total = total + piece.sum(axis=0, keepdims=True)
    return top, weights, total


def attend_kernel(start_ref, qkv_ref, out_ref, peak_ref):
    keys = qkv_ref[:, HD : 2 * HD]
    values_t = qkv_ref[:, 2 * HD :].T
    peak = jnp.full((1, BQ), -1e30, F32)
    for lo in range(0, SEQ, BQ):
        query_block = qkv_ref[lo : lo + BQ, :HD]
        start_row = start_ref[:, lo : lo + BQ]
        parts = key_parts(lo)
        scores = [part_scores(keys, query_block, lo, part, start_row) for part in parts]
        top, weights, total = softmax_parts(scores)
        peak = jnp.maximum(peak, top)
        mixed = None
        for (first, last, _), piece in zip(parts, weights):
            term = dot_nn(values_t[:, first:last], piece.astype(BF))
            mixed = term if mixed is None else mixed + term
        out_ref[lo : lo + BQ, :] = (mixed * (1.0 / total)).T.astype(BF)
    peak_ref[...] = jnp.broadcast_to(peak.max(axis=1, keepdims=True) * SCALE, peak_ref.shape)


def attend(start_rows, qkv):
    heads = qkv.shape[1] // (3 * HD)
    return pl.pallas_call(
        attend_kernel,
        grid=(heads,),
        in_specs=[
            pl.BlockSpec((1, SEQ), lambda h: (0, 0)),
            pl.BlockSpec((SEQ, 3 * HD), lambda h: (0, h)),
        ],
        out_specs=[
            pl.BlockSpec((SEQ, HD), lambda h: (0, h)),
            pl.BlockSpec((1, 8, HD), lambda h: (h, 0, 0)),
        ],
        out_shape=[
            jax.ShapeDtypeStruct((SEQ, heads * HD), BF),
            jax.ShapeDtypeStruct((heads, 8, HD), F32),
        ],
        compiler_params=pltpu.CompilerParams(vmem_limit_bytes=VMEM_CAP),
        cost_estimate=cost(heads * 5e-6),
        name="attend",
    )(start_rows, qkv)


def attend_back_kernel(start_ref, qkv_ref, back_ref, out_ref, key_acc, value_acc):
    keys = qkv_ref[:, HD : 2 * HD]
    values = qkv_ref[:, 2 * HD :]
    keys_t = keys.T
    key_acc[...] = jnp.zeros_like(key_acc)
    value_acc[...] = jnp.zeros_like(value_acc)
    for lo in range(0, SEQ, BQ):
        query_block = qkv_ref[lo : lo + BQ, :HD]
        back_block = back_ref[lo : lo + BQ, :]
        start_row = start_ref[:, lo : lo + BQ]
        parts = key_parts(lo)
        scores = [part_scores(keys, query_block, lo, part, start_row) for part in parts]
        top, weights, total = softmax_parts(scores)
        inverse = 1.0 / total
        probs = [piece * inverse for piece in weights]
        grads = [dot_nt(values[first:last], back_block) for first, last, _ in parts]
        mean = None
        for piece, grad in zip(probs, grads):
            term = (piece * grad).sum(axis=0, keepdims=True)
            mean = term if mean is None else mean + term
        query_t = None
        for (first, last, _), piece, grad in zip(parts, probs, grads):
            low = (piece * ((grad - mean) * SCALE)).astype(BF)
            value_acc[first:last, :] += dot_nn(piece.astype(BF), back_block)
            key_acc[first:last, :] += dot_nn(low, query_block)
            term = dot_nn(keys_t[:, first:last], low)
            query_t = term if query_t is None else query_t + term
        out_ref[lo : lo + BQ, :HD] = query_t.T.astype(BF)
    out_ref[:, HD : 2 * HD] = key_acc[...].astype(BF)
    out_ref[:, 2 * HD :] = value_acc[...].astype(BF)


def attend_back(start_rows, qkv, back):
    heads = qkv.shape[1] // (3 * HD)
    return pl.pallas_call(
        attend_back_kernel,
        grid=(heads,),
        in_specs=[
            pl.BlockSpec((1, SEQ), lambda h: (0, 0)),
            pl.BlockSpec((SEQ, 3 * HD), lambda h: (0, h)),
            pl.BlockSpec((SEQ, HD), lambda h: (0, h)),
        ],
        out_specs=pl.BlockSpec((SEQ, 3 * HD), lambda h: (0, h)),
        out_shape=jax.ShapeDtypeStruct(qkv.shape, BF),
        scratch_shapes=[pltpu.VMEM((SEQ, HD), F32), pltpu.VMEM((SEQ, HD), F32)],
        compiler_params=pltpu.CompilerParams(vmem_limit_bytes=VMEM_CAP),
        cost_estimate=cost(heads * 10e-6),
        name="attend_back",
    )(start_rows, qkv, back)


TILE_GROUP = 8


def orthonormal_all(matrices):
    currents = []
    for matrix in matrices:
        frob = jnp.sqrt(jnp.sum(matrix * matrix, axis=(0, 1), keepdims=True))
        currents.append(matrix * (1.0 / (frob + 1e-06)))
    for _ in range(NS_ITERS):
        lows = [current.astype(BF) for current in currents]
        grams = [dot_nt(low, low).astype(BF) for low in lows]
        terms = [dot_nn(gram, low) for gram, low in zip(grams, lows)]
        currents = [1.5 * current - 0.5 * term for current, term in zip(currents, terms)]
    return currents


def update_kernel(tile_group, turned_grad, token_count, *refs):
    rate_ref, factor_ref, grad_ref = refs[:3]
    master_ref, first_ref, second_ref, left_stat_ref, right_stat_ref, left_ref, right_ref = refs[3:10]
    outs = refs[-8:]
    first_out, second_out, master_out, weight_out, left_stat_out, right_stat_out, left_out, right_out = outs
    base = pl.program_id(0) * tile_group
    group = range(tile_group)
    grads = [grad_ref[i] for i in group]
    lefts = [left_ref[i].astype(BF) for i in group]
    rights = [right_ref[i].astype(BF) for i in group]
    if turned_grad:
        outer_rows = [dot_tn(grad, grad) for grad in grads]
        outer_cols = [dot_nt(grad, grad) for grad in grads]
        halves = [dot_nn(grad, left).astype(BF) for grad, left in zip(grads, lefts)]
        rotated = [dot_tn(half, right) for half, right in zip(halves, rights)]
    else:
        outer_rows = [dot_nt(grad, grad) for grad in grads]
        outer_cols = [dot_tn(grad, grad) for grad in grads]
        halves = [dot_nn(grad, right).astype(BF) for grad, right in zip(grads, rights)]
        rotated = [dot_tn(left, half) for left, half in zip(lefts, halves)]
    directions = []
    for i in group:
        new_first = 0.5 * first_ref[i] + 0.5 * rotated[i]
        new_second = 0.5 * second_ref[i] + 0.5 * rotated[i] * rotated[i]
        first_out[i] = new_first
        second_out[i] = new_second
        direction = (
            new_first
            * (1.0 / (1.0 - 0.5**STEP))
            / (jnp.sqrt(new_second * (1.0 / (1.0 - 0.5**STEP))) + 1e-08)
        )
        directions.append(direction.astype(BF))
    turned = [dot_nn(left, direction).astype(BF) for left, direction in zip(lefts, directions)]
    turned = [dot_nt(half, right) for half, right in zip(turned, rights)]
    for i in group:
        master = master_ref[i]
        new_master = (master - rate_ref[base + i] * (turned[i] + 0.1 * master)) * factor_ref[base + i]
        master_out[i] = new_master
        weight_out[i] = new_master.astype(BF)
    moved = []
    for stat_ref, stat_out, outers, bases in (
        (left_stat_ref, left_stat_out, outer_rows, lefts),
        (right_stat_ref, right_stat_out, outer_cols, rights),
    ):
        for i in group:
            new_stat = 0.5 * stat_ref[i] + (0.5 / (HD * token_count)) * outers[i]
            stat_out[i] = new_stat
            moved.append(dot_nn(new_stat.astype(BF), bases[i]))
    moved = orthonormal_all(moved)
    for i in group:
        left_out[i] = moved[i]
        right_out[i] = moved[tile_group + i]


def update_tiles(grads, state, rates, factors, first_tile, earlier, turned_grad, token_count):
    count = grads.shape[0]
    tiles = state[0].shape[0]
    group = math.gcd(math.gcd(count, first_tile), TILE_GROUP)
    offset = first_tile // group
    block = (group, HD, HD)
    here = pl.BlockSpec(block, lambda i: (i + offset, 0, 0))
    smem = pl.BlockSpec(memory_space=pltpu.SMEM)
    kinds = [F32, F32, F32, BF, F32, F32, F32, F32]
    earlier = list(earlier) if earlier is not None else []

    def body(*refs):
        update_kernel(group, turned_grad, token_count, *refs)

    return pl.pallas_call(
        body,
        grid=(count // group,),
        in_specs=[smem, smem, pl.BlockSpec(block, lambda i: (i, 0, 0))]
        + [here] * 7
        + [pl.BlockSpec(memory_space=pl.ANY)] * len(earlier),
        out_specs=[here] * 8,
        out_shape=[jax.ShapeDtypeStruct((tiles, HD, HD), kind) for kind in kinds],
        input_output_aliases={10 + i: i for i in range(len(earlier))},
        compiler_params=pltpu.CompilerParams(vmem_limit_bytes=VMEM_CAP),
        cost_estimate=cost(count * 5e-7),
        name="update_tiles",
    )(rates[first_tile : first_tile + count], factors[first_tile : first_tile + count], grads, *state, *earlier)


def grad_kernel(chunks, parts, block_ref, *refs):
    lefts, rights, out_ref = refs[:chunks], refs[chunks:-1], refs[-1]
    turned = [left[...].T for left in lefts]
    lo = 0
    for j in range(parts):
        mine = rights[j * chunks : (j + 1) * chunks]
        width = mine[0].shape[1]
        step = min(512, width)
        for at in range(0, width, step):
            total = dot_nn(turned[0], mine[0][:, at : at + step])
            for left, right in zip(turned[1:], mine[1:]):
                total = total + dot_nn(left, right[:, at : at + step])
            out_ref[0, :, lo + at : lo + at + step] = total.astype(BF)
        lo += width


def grad_blocks(blocks, lefts, rights, edge):
    count = blocks.shape[0]
    rows = sum(left.shape[0] for left in lefts)
    width = sum(right[0].shape[1] for right in rights)
    flat = [chunk for right in rights for chunk in right]

    def body(*refs):
        grad_kernel(len(lefts), len(rights), *refs)

    return pl.pallas_call(
        body,
        grid_spec=pltpu.PrefetchScalarGridSpec(
            num_scalar_prefetch=1,
            grid=(count,),
            in_specs=[pl.BlockSpec((left.shape[0], edge), lambda i, blocks: (0, blocks[i])) for left in lefts]
            + [pl.BlockSpec(chunk.shape, lambda i, blocks: (0, 0)) for chunk in flat],
            out_specs=pl.BlockSpec((1, edge, width), lambda i, blocks: (i, 0, 0)),
        ),
        out_shape=jax.ShapeDtypeStruct((count, edge, width), BF),
        compiler_params=pltpu.CompilerParams(vmem_limit_bytes=VMEM_CAP),
        cost_estimate=cost(2 * count * edge * width * rows / 8e14),
        name="grad_blocks",
    )(blocks, *lefts, *flat)


def matmul_kernel(terms, *refs):
    lefts, rights, out_ref = refs[:terms], refs[terms : 2 * terms], refs[2 * terms]
    total = dot_nt(lefts[0][...], rights[0][...])
    for left, right in zip(lefts[1:], rights[1:]):
        total = total + dot_nt(left[...], right[...])
    out_ref[...] = total.astype(BF)


def matmul_sum(lefts, rights):
    terms = len(lefts)
    rows, depth = lefts[0].shape
    columns = rights[0].shape[0]
    row_step, step = min(1024, rows), min(512, columns)

    def body(*refs):
        matmul_kernel(terms, *refs)

    return pl.pallas_call(
        body,
        grid=(rows // row_step, columns // step),
        in_specs=[pl.BlockSpec((row_step, depth), lambda m, n: (m, 0))] * terms
        + [pl.BlockSpec((step, depth), lambda m, n: (n, 0))] * terms,
        out_specs=pl.BlockSpec((row_step, step), lambda m, n: (m, n)),
        out_shape=jax.ShapeDtypeStruct((rows, columns), BF),
        compiler_params=pltpu.CompilerParams(vmem_limit_bytes=VMEM_CAP),
        cost_estimate=cost(2 * terms * rows * columns * depth / 8e14),
        name="matmul_sum",
    )(*lefts, *rights)


def pack_kernel(heads, edge_tiles, hidden_tiles, core_ref, tiles_ref, halves_ref, qkv_ref, out_ref):
    core = core_ref[0]
    half = hidden_tiles // 2 * HD
    first = 0
    for row in range(edge_tiles):
        for part in range(3):
            for head in range(heads):
                tile = tiles_ref[first + (row * 3 + part) * heads + head].astype(BF)
                at = (head * 3 + part) * HD
                qkv_ref[row * HD : (row + 1) * HD, at : at + HD] = tile
    first += edge_tiles * 3 * heads
    for head in range(heads):
        for row in range(edge_tiles):
            tile = tiles_ref[first + head * edge_tiles + row].T.astype(BF)
            out_ref[row * HD : (row + 1) * HD, head * HD : (head + 1) * HD] = tile
    first += heads * edge_tiles
    for kind in range(2):
        for row in range(edge_tiles):
            for column in range(hidden_tiles):
                part, inner = divmod(column, hidden_tiles // 2)
                at = kind * half + inner * HD
                if kind == 0:
                    tile = tiles_ref[first + row * hidden_tiles + column].astype(BF)
                else:
                    tile = tiles_ref[first + column * edge_tiles + row].T.astype(BF)
                halves_ref[part ^ core, row * HD : (row + 1) * HD, at : at + HD] = tile
        first += edge_tiles * hidden_tiles


def pack_weights(tiles, core, heads, edge_tiles, hidden_tiles):
    edge = edge_tiles * HD

    def body(*refs):
        pack_kernel(heads, edge_tiles, hidden_tiles, *refs)

    shapes = [(2, edge, hidden_tiles * HD), (edge, 3 * heads * HD), (edge, heads * HD)]
    return pl.pallas_call(
        body,
        grid_spec=pltpu.PrefetchScalarGridSpec(
            num_scalar_prefetch=1,
            grid=(1,),
            in_specs=[pl.BlockSpec(tiles.shape, lambda i, core: (0, 0, 0))],
            out_specs=[pl.BlockSpec(shapes[0], lambda i, core: (0, 0, 0))]
            + [pl.BlockSpec(shape, lambda i, core: (0, 0)) for shape in shapes[1:]],
        ),
        out_shape=[jax.ShapeDtypeStruct(shape, BF) for shape in shapes],
        compiler_params=pltpu.CompilerParams(vmem_limit_bytes=VMEM_CAP),
        cost_estimate=cost(5e-6),
        name="pack_weights",
    )(core[None], tiles)


def scatter_kernel(tables, *refs):
    source_ref, outs = refs[tables], refs[tables + 1 :]
    lo = 0
    for out in outs:
        width = out.shape[1]
        out[...] = source_ref[0, :, lo : lo + width]
        lo += width


def scatter_blocks(tables, source):
    count, edge, columns = source.shape
    parts = len(tables)
    width = columns // parts

    def body(*refs):
        scatter_kernel(parts, *refs)

    def out_spec(k):
        return pl.BlockSpec((edge, width), lambda i, *tables: (tables[k][i], 0))

    return pl.pallas_call(
        body,
        grid_spec=pltpu.PrefetchScalarGridSpec(
            num_scalar_prefetch=parts,
            grid=(count,),
            in_specs=[pl.BlockSpec((1, edge, columns), lambda i, *tables: (i, 0, 0))],
            out_specs=[out_spec(k) for k in range(parts)],
        ),
        out_shape=[jax.ShapeDtypeStruct((count * edge, width), BF)] * parts,
        compiler_params=pltpu.CompilerParams(vmem_limit_bytes=VMEM_CAP),
        cost_estimate=cost(4 * count * edge * columns / 3e12),
        name="scatter_blocks",
    )(*tables, source)


def project_kernel(sources, *refs):
    pick_ref = refs[0]
    pieces = refs[2 : 2 + sources]
    gain_ref, shift_ref, weight_ref, bias_ref = refs[2 + sources : 6 + sources]
    normal_out, normed_out, out_ref = refs[-3:]
    picked = pick_ref[pl.program_id(0)]
    for i in range(sources):

        @pl.when(picked == i)
        def _():
            normal_out[...] = pieces[i][...]

    normed = (normal_out[...].astype(F32) * gain_ref[...] + shift_ref[...]).astype(BF)
    normed_out[...] = normed
    out_ref[...] = (dot_nn(normed, weight_ref[...]) + bias_ref[...]).astype(BF)


def project(pick, place, total, pieces, gain, shift_by, weight, bias, into=()):
    count = pick.shape[0]
    rows, depth = pieces[0].shape
    columns = weight.shape[1]

    def body(*refs):
        project_kernel(len(pieces), *refs)

    def held(shape):
        return pl.BlockSpec(shape, lambda i, pick, place: (0, 0), pipeline_mode=pl.Buffered(1))

    def block(width):
        return pl.BlockSpec((rows, width), lambda i, pick, place: (place[i], 0))

    return pl.pallas_call(
        body,
        grid_spec=pltpu.PrefetchScalarGridSpec(
            num_scalar_prefetch=2,
            grid=(count,),
            in_specs=[held((rows, depth)) for _ in pieces]
            + [held((1, depth)), held((1, depth)), held((depth, columns)), held((1, columns))]
            + [pl.BlockSpec(memory_space=pl.ANY) for _ in into],
            out_specs=[block(depth), block(depth), block(columns)],
        ),
        out_shape=[jax.ShapeDtypeStruct((total * rows, width), BF) for width in (depth, depth, columns)],
        input_output_aliases={2 + len(pieces) + 4 + k: k for k in range(len(into))},
        compiler_params=pltpu.CompilerParams(vmem_limit_bytes=VMEM_CAP),
        cost_estimate=cost(count * 6e-6),
        name="project",
    )(pick, place, *pieces, gain[None], shift_by[None], weight, bias[None], *into)


def sync(*values):
    return lax.optimization_barrier(values)


def shift(value, axis, mask):
    return lax.ppermute(value, axis, [(i, i ^ mask) for i in range(lax.axis_size(axis))])


def move(value, axis, pairs):
    return lax.ppermute(value, axis, pairs)


def beside(value, axis, mask, steps, state):
    total, rows = sum(share for share, _ in steps), value.shape[0]
    pieces, done, first = [], 0, 0
    for share, work in steps:
        done += share
        last = rows // 16 * done // total * 16
        pieces.append(shift(value[first:last], axis, mask))
        first = last
        state = work(state)
        state, pieces, value = sync(state, pieces, value)
    return jnp.concatenate(pieces, axis=0), state


def add_low(left, right):
    return (left.astype(F32) + right.astype(F32)).astype(BF)


def join_halves(mine, other):
    first = (lax.axis_index("dp") & 1) == 0
    return jnp.concatenate([jnp.where(first, mine, other), jnp.where(first, other, mine)], axis=-1)


def halving_order(chips, masks):
    return sorted(chips, key=lambda q: tuple(-(q & (mask >> 1)) for mask in masks))


def halve(blocks, masks):
    for mask in masks:
        count = blocks.shape[0] // 2
        blocks = add_low(blocks[count:], shift(blocks[:count], "dp", mask))
    return blocks


def layer_norm(token_rows, gain, shift_by):
    centre = jnp.mean(token_rows, axis=-1, keepdims=True)
    centred = token_rows - centre
    spread = jnp.mean(centred * centred, axis=-1, keepdims=True)
    return centred * lax.rsqrt(spread + 1e-05) * gain + shift_by


def layer_norm_back(token_rows, gain, grad):
    centre = jnp.mean(token_rows, axis=-1, keepdims=True)
    centred = token_rows - centre
    inverse = lax.rsqrt(jnp.mean(centred * centred, axis=-1, keepdims=True) + 1e-05)
    normal = centred * inverse
    scaled = grad * gain
    back = (
        scaled - jnp.mean(scaled, axis=-1, keepdims=True) - normal * jnp.mean(scaled * normal, axis=-1, keepdims=True)
    ) * inverse
    return back, jnp.sum(grad * normal, axis=0), jnp.sum(grad, axis=0)


def gelu_pair(pre_act):
    cdf = 0.5 * (1.0 + lax.erf(pre_act * (0.5**0.5)))
    density = jnp.exp(-0.5 * pre_act * pre_act) * 0.3989422804014327
    return pre_act * cdf, cdf + pre_act * density


def axis_sum(value, axis):
    for bit in range(lax.axis_size(axis).bit_length() - 1):
        value = value + shift(value, axis, 1 << bit)
    return value


def small_step(summed, params, first, second):
    new_first = 0.5 * first + 0.5 * summed
    new_second = 0.5 * second + 0.5 * summed * summed
    direction = new_first / (1.0 - 0.5**STEP) / (jnp.sqrt(new_second / (1.0 - 0.5**STEP)) + 1e-08)
    return new_first, new_second, params - 0.1 * direction


def per_device(
    inputs,
    cotangent,
    lengths,
    held_blocks,
    master,
    first_moment,
    second_moment,
    left_stats,
    right_stats,
    left_basis,
    right_basis,
    small_params,
    small_first,
    small_second,
):
    dp_count = lax.axis_size("dp")
    tp_count = lax.axis_size("tensor")
    me = lax.axis_index("dp")
    place = lax.axis_index("tensor")
    core = me & 1
    rows = inputs.shape[0]
    edge = D // dp_count
    width = D // tp_count
    hidden = FF // tp_count
    half = hidden // 2
    heads = width // HD
    edge_tiles = edge // HD
    hidden_tiles = hidden // HD
    tile_q = edge_tiles * 3 * heads
    tile_o = heads * edge_tiles
    tile_u = edge_tiles * hidden_tiles
    tile_count = master.shape[2]
    near = [1 << bit for bit in range(1, dp_count.bit_length() - 1)]
    far = near[::-1]
    slices = tp_count // 2
    chips = range(dp_count // 2)
    relative = jnp.arange(dp_count, dtype=jnp.int32) ^ me
    block_of = jnp.take(held_blocks, relative, axis=1)

    bias_q = lax.dynamic_slice_in_dim(small_params, place * width, width)
    bias_v = lax.dynamic_slice_in_dim(small_params, D + place * width, width)
    bias_o = small_params[2 * D : 3 * D]
    bias_two = small_params[3 * D : 4 * D]
    gain_one = small_params[4 * D : 5 * D]
    shift_one = small_params[5 * D : 6 * D]
    gain_two = small_params[6 * D : 7 * D]
    shift_two = small_params[7 * D : 8 * D]
    hidden_starts = [(place ^ (2 * j)) * hidden + core * half for j in range(slices)]
    bias_up = jnp.concatenate(
        [lax.dynamic_slice_in_dim(small_params, 8 * D + start, half) for start in hidden_starts]
    )

    token_rows = inputs.astype(F32)
    centred = token_rows - jnp.mean(token_rows, axis=-1, keepdims=True)
    spread = jnp.mean(centred * centred, axis=-1, keepdims=True)
    normal = (centred * lax.rsqrt(spread + 1e-05)).astype(BF)
    ups = [(i, i + 1) for i in range(tp_count - 1)]
    downs = [(i + 1, i) for i in range(tp_count - 1)]
    above, below = [move(normal, "tensor", downs)], [move(normal, "tensor", ups)]

    bounds = [0, tile_q, tile_q + tile_o, tile_q + tile_o + tile_u, tile_count]
    halves, own_qkv, own_out = pack_weights(master[0, 0], core, heads, edge_tiles, hidden_tiles)
    pair = jnp.stack([halves[0], shift(halves[1], "dp", 1)])
    same_core = [list(range(at, dp_count, 2)) for at in range(2)]
    pair_slots = jnp.arange(dp_count, dtype=jnp.int32) ^ core

    def gather_ffn(value):
        return lax.all_gather(value, "dp", axis=0, tiled=True, axis_index_groups=same_core)

    def scatter_ffn(value):
        return scatter_blocks([held_blocks[2][pair_slots], held_blocks[3][pair_slots]], value)

    def gather_all(kind, value):
        value = lax.all_gather(value, "dp", axis=0, tiled=False)
        return scatter_blocks([held_blocks[kind]], value)[0]

    def crossed(mask, odd):
        return [(i, i ^ mask) for i in range(tp_count) if ((i ^ (i >> 1)) & 1) == odd]

    w_qkv = gather_all(0, own_qkv)
    bias_mixed = jnp.stack(
        [bias_q.reshape(heads, HD), jnp.zeros((heads, HD), F32), bias_v.reshape(heads, HD)], axis=1
    ).reshape(3 * width)
    distance = jnp.arange(tp_count, dtype=jnp.int32) - place
    by_distance = jnp.argsort(jnp.abs(distance)).astype(jnp.int32)
    offset = by_distance - place
    outs = [shift(own_out, "tensor", j) for j in range(1, tp_count)]
    far_first, first_raw, out_raw = [], None, None
    for step in range(1, tp_count):
        if step > 1:
            below.append(move(below[-1], "tensor", ups[step - 1 :]))
            above.append(move(above[-1], "tensor", downs[: tp_count - step]))
        if step == tp_count - 1:
            first_raw = gather_ffn(pair)
            far_first = [move(pair, "tensor", crossed(2 * j, 0)) for j in range(1, slices)]
            w_out = scatter_blocks([held_blocks[1]], out_raw)[0]
            pick = jnp.where(offset < 0, -offset, jnp.where(offset > 0, tp_count - 2 + offset, 0))
            sources = [normal] + below[:-1] + above[:-1]
            projected = project(
                pick[:-1], by_distance[:-1], tp_count, sources, gain_one, shift_one, w_qkv, bias_mixed
            )
            above, below, far_first, pair, w_qkv, w_out, projected = sync(
                above, below, far_first, pair, w_qkv, w_out, projected
            )
        elif step == 1:
            above, below, outs, own_out, pair = sync(above, below, outs, own_out, pair)
            out_raw = lax.all_gather(jnp.concatenate([own_out] + outs, axis=1), "dp", axis=0, tiled=False)
        else:
            above, below, pair = sync(above, below, pair)

    reach = tp_count // 2
    pick = jnp.where(offset < 0, -offset - reach, tp_count - 1 + offset - 2 * reach + 1)
    sources = below[reach - 1 :] + above[reach - 1 :]
    normal_all, normed_all, qkv = project(
        pick[-1:], by_distance[-1:], tp_count, sources, gain_one, shift_one, w_qkv, bias_mixed, projected
    )
    far_second = [move(pair, "tensor", crossed(2 * j, 1)) for j in range(1, slices)]

    ends = jnp.cumsum(lengths[0])
    spot = jnp.arange(SEQ, dtype=jnp.int32) - PROMPT
    started = jnp.max(jnp.where(ends[None, :] <= spot[:, None], ends[None, :], 0), axis=1)
    start_rows = jnp.where(spot < 0, 0, PROMPT + started).astype(jnp.int32)[None]
    attended, peaks = attend(start_rows, qkv)
    others = range(1, slices)
    peak_row = lax.dynamic_update_slice(
        jnp.zeros((dp_count * H,), F32), peaks[:, 0, 0], (me * H + place * heads,)
    )
    attended, far_second = sync(attended, far_second)

    def rows_of(value, j):
        return lax.dynamic_slice_in_dim(value, (place ^ j) * rows, rows, 0)

    def with_core(value):
        return jnp.concatenate([value, shift(value, "dp", 1)], axis=0)

    attended_rows = jnp.concatenate(
        [rows_of(attended, 0)] + [shift(rows_of(attended, j), "tensor", j) for j in range(1, tp_count)], axis=1
    )
    far_raw = [gather_ffn(left + right) for left, right in zip(far_first, far_second)]
    w_first = scatter_ffn(first_raw)
    back_near = with_core(cotangent)
    attended_rows, w_first, cotangent, back_near, w_out = sync(attended_rows, w_first, cotangent, back_near, w_out)
    hidden_rows = token_rows + dot_nt(attended_rows, w_out) + bias_o
    normed_two = layer_norm(hidden_rows, gain_two, shift_two).astype(BF)

    w_up, w_down = [w_first[0]], [w_first[1]]
    biases = [bias_up[j * half : (j + 1) * half] for j in range(slices)]

    def core_rows(partial):
        return add_low(partial[:rows], shift(partial[rows:], "dp", 1))

    def chips_sum(blocks):
        blocks = blocks.reshape(dp_count // 2, 2, edge, blocks.shape[2])
        return lax.psum_scatter(blocks, "dp", scatter_dimension=0, tiled=False, axis_index_groups=same_core)

    pending = [("dp", 1 << bit) for bit in range(dp_count.bit_length() - 1)]
    pending += [("tensor", 1 << bit) for bit in range(1, tp_count.bit_length() - 1)]

    def with_peaks(work):
        def both(state):
            if pending:
                state = dict(state, peaks=state["peaks"] + shift(state["peaks"], *pending.pop(0)))
            return work(state)

        return both

    def near_back(j):
        def work(state):
            if j > 0:
                up, down = scatter_ffn(state.pop("far_raw"))
                w_up.append(up)
                w_down.append(down)
            grad_act = jnp.dot(state["back_near"], w_down[j], preferred_element_type=F32).astype(BF)
            state = dict(state, grad_act=grad_act)
            if j == 0:
                state["normed_near"] = with_core(state.pop("normed"))
            return state

        return work

    def near_up(j):
        def work(state):
            pre_act = jnp.dot(state["normed_near"], w_up[j], preferred_element_type=F32) + biases[j]
            activation, slope = gelu_pair(pre_act)
            low = (state["grad_act"].astype(F32) * slope).astype(BF)
            if j + 1 < slices:
                state = dict(state, far_raw=far_raw[j])
            return dict(state, act_near=state["act_near"] + [activation.astype(BF)], pre_near=state["pre_near"] + [low])

        return work

    def far_up(j):
        def work(state):
            pre_act = jnp.dot(state["normed_far"], w_up[j], preferred_element_type=F32) + biases[j]
            activation, slope = gelu_pair(pre_act)
            return dict(state, act_far=state["act_far"] + [activation.astype(BF)], slopes=state["slopes"] + [slope.astype(BF)])

        return work

    def far_result(state):
        return dict(state, result_far=matmul_sum(state["act_far"], w_down))

    def near_grad(state):
        return dict(
            state, grad_near=matmul_sum(state["pre_near"], w_up), ffn_far=core_rows(state.pop("result_far"))
        )

    def down_blocks(state):
        rights = [list(pair) for pair in zip(state["act_near"], state["act_far"])]
        blocks = grad_blocks(held_blocks[3][pair_slots], [state["back_near"], state["back_far"]], rights, edge)
        return dict(state, down=blocks)

    def far_back(j):
        def work(state):
            grad_act = jnp.dot(state["back_far"], w_down[j], preferred_element_type=F32)
            low = (grad_act * state["slopes"][j].astype(F32)).astype(BF)
            return dict(state, pre_far=state["pre_far"] + [low])

        return work

    def far_grad(state):
        return dict(state, grad_far=matmul_sum(state["pre_far"], w_up))

    def up_blocks(state):
        rights = [list(pair) for pair in zip(state["pre_near"], state["pre_far"])]
        blocks = grad_blocks(held_blocks[2][pair_slots], [state["normed_near"], state["normed_far"]], rights, edge)
        return dict(state, up=blocks)

    def near_result(state):
        return dict(
            state, result_near=matmul_sum(state["act_near"], w_down), near_rows=core_rows(state.pop("grad_near"))
        )

    state = dict(
        back_near=back_near, peaks=peak_row, normed=normed_two, act_near=[], pre_near=[], act_far=[], pre_far=[], slopes=[]
    )
    steps = [(1, with_peaks(work)) for j in range(slices) for work in (near_back(j), near_up(j))]
    normed_across, state = beside(normed_two, "tensor", 1, steps, state)
    state["normed_far"] = with_core(normed_across)
    steps = [(1, with_peaks(far_up(j))) for j in range(slices)]
    steps += [(slices, with_peaks(far_result)), (slices, with_peaks(near_grad))]
    back_across, state = beside(cotangent, "tensor", 1, steps, state)
    state["back_far"] = with_core(back_across)
    middle = rows // 2
    ffn_low, state = beside(state["ffn_far"][:middle], "tensor", 1, [(1, down_blocks)], state)
    part_down = chips_sum(state.pop("down"))
    steps = [(1, far_back(j)) for j in range(slices)] + [(slices, far_grad)]
    ffn_high, state = beside(state.pop("ffn_far")[middle:], "tensor", 1, steps, state)
    ffn_across = jnp.concatenate([ffn_low, ffn_high], axis=0)
    far_rows = core_rows(state.pop("grad_far"))
    state["far_rows"] = far_rows
    state = sync(state)[0]
    cut = rows // 16 * 5 // 8 * 16
    low_rows, state = beside(state["far_rows"][:cut], "tensor", 1, [(1, up_blocks)], state)
    part_up = chips_sum(state.pop("up"))
    high_rows, state = beside(state.pop("far_rows")[cut:], "tensor", 1, [(1, near_result)], state)
    low_rows, high_rows, part_down, state = sync(low_rows, high_rows, part_down, state)
    peak_rows = state["peaks"]
    grad_two = state["near_rows"].astype(F32) + jnp.concatenate([low_rows, high_rows], axis=0).astype(F32)
    result, grads_pre = state["result_near"], list(zip(state["pre_near"], state["pre_far"]))

    def far_slices(part):
        return part[:, :, :half], [part[:, :, j * half : (j + 1) * half] for j in others]

    def to_owners(values):
        return [shift(value, "tensor", 2 * j) for j, value in zip(others, values)]

    order_far = halving_order(chips, far)

    def half_slots(order):
        return jnp.array([2 * q + 1 for q in order] + [2 * q for q in order], jnp.int32)

    own_down, far_down = far_slices(part_down)
    down_low = to_owners([value[:1] for value in far_down])
    grad_part, grad_gain_two, grad_shift_two = layer_norm_back(hidden_rows, gain_two, grad_two)
    grad_hidden = cotangent.astype(F32) + grad_part
    branch = grad_hidden.astype(BF)
    even = jnp.arange(0, dp_count, 2, dtype=jnp.int32)
    out_slots = jnp.concatenate([even + 1 - core, even + core])
    grads_out = grad_blocks(held_blocks[1][out_slots], [branch], [[attended_rows]], edge)
    grad_attended_rows = jnp.dot(branch, w_out, preferred_element_type=F32).astype(BF)
    peak_rows = peak_rows + shift(peak_rows, "tensor", 1)
    grad_attended_rows, branch, result, grads_pre, grads_out, down_low, far_down, peak_rows = sync(
        grad_attended_rows, branch, result, grads_pre, grads_out, down_low, far_down, peak_rows
    )

    arrived = [
        grad_attended_rows[:, j * width : (j + 1) * width]
        if j == 0
        else shift(grad_attended_rows[:, j * width : (j + 1) * width], "tensor", j)
        for j in range(tp_count)
    ]
    grad_attended = jnp.zeros((SEQ, width), BF)
    for j in range(tp_count):
        grad_attended = lax.dynamic_update_slice_in_dim(grad_attended, arrived[j], (place ^ j) * rows, 0)
    sum_out = halve(grads_out, [1])
    grad_attended, branch, result, part_up, far_down, grads_pre, sum_out = sync(
        grad_attended, branch, result, part_up, far_down, grads_pre, sum_out
    )

    def far_sum(kept, arrived):
        total = kept.astype(F32)
        for value in arrived:
            total = total + value.astype(F32)
        total = total.astype(BF)
        return join_halves(total[0], shift(total[1], "dp", 1))

    sum_out = lax.psum_scatter(sum_out, "dp", scatter_dimension=0, tiled=False, axis_index_groups=same_core)
    own_up, far_up = far_slices(part_up)
    down_high = to_owners([value[1:] for value in far_down])
    up_low = to_owners([value[:1] for value in far_up])
    grad_qkv_rows = attend_back(start_rows, qkv, grad_attended)
    grad_qkv_rows, down_high, up_low, far_up, branch, grads_pre = sync(
        grad_qkv_rows, down_high, up_low, far_up, branch, grads_pre
    )
    up_high = to_owners([value[1:] for value in far_up])
    partial = dot_nt(grad_qkv_rows, w_qkv).astype(BF)
    partial, up_high, grad_qkv_rows, branch, grads_pre, sum_out = sync(
        partial, up_high, grad_qkv_rows, branch, grads_pre, sum_out
    )
    far_down = [jnp.concatenate(value, axis=0) for value in zip(down_low, down_high)]
    far_up = [jnp.concatenate(value, axis=0) for value in zip(up_low, up_high)]
    grad_normed_one = lax.psum_scatter(partial, "tensor", scatter_dimension=0, tiled=True).astype(F32)

    grads_qkv = grad_blocks(block_of[0][half_slots(order_far)], [normed_all], [[grad_qkv_rows]], edge)
    grads_qkv, grad_qkv_rows, branch, grads_pre, partial = sync(grads_qkv, grad_qkv_rows, branch, grads_pre, partial)
    column_sums = jnp.sum(grad_qkv_rows, axis=0, dtype=F32).reshape(heads, 3, HD)
    head_sums = lambda part: lax.dynamic_update_slice(
        jnp.zeros((D,), F32), column_sums[:, part].reshape(width), (place * width,)
    )
    partial_wide = partial.astype(F32)
    grad_bias_up = jnp.concatenate([sum(jnp.sum(value, axis=0, dtype=F32) for value in pair) for pair in grads_pre])
    wide = jnp.zeros((FF,), F32)
    for j in range(slices):
        wide = lax.dynamic_update_slice(wide, grad_bias_up[j * half : (j + 1) * half], (hidden_starts[j],))
    totals = jnp.concatenate(
        [
            head_sums(0),
            head_sums(2),
            jnp.sum(branch, axis=0, dtype=F32),
            jnp.sum(cotangent, axis=0, dtype=F32),
            jnp.sum(partial_wide * normal_all.astype(F32), axis=0),
            jnp.sum(partial_wide, axis=0),
            grad_gain_two,
            grad_shift_two,
            wide,
        ]
    )
    sum_qkv = halve(grads_qkv, [1])
    totals = axis_sum(totals, "dp")
    totals, sum_qkv = sync(totals, sum_qkv)
    sum_qkv = halve(sum_qkv, far)[0]
    sum_down = far_sum(own_down, far_down)
    sum_up = far_sum(own_up, far_up)
    ffn_near = core_rows(result)
    outputs = (hidden_rows + ffn_near.astype(F32) + ffn_across.astype(F32) + bias_two).astype(BF)
    peak_all = jnp.max(peak_rows.reshape(dp_count, H), axis=0)
    grad_normed_one, totals, sum_out = sync(grad_normed_one, totals, sum_out)
    grad_small = axis_sum(totals, "tensor")
    outs = [shift(sum_out[:, j * width : (j + 1) * width], "tensor", j) for j in range(1, tp_count)]
    total_out = sum_out[:, :width].astype(F32)
    for value in outs:
        total_out = total_out + value.astype(F32)
    sum_out = total_out.astype(BF)
    rows_part, _, _ = layer_norm_back(token_rows, gain_one, grad_normed_one)
    input_grad = (grad_hidden + rows_part).astype(BF)

    shrink = jnp.sqrt(1.0 / jnp.maximum(peak_all, 1.0))
    small_first_new, small_second_new, small_new = small_step(grad_small, small_params, small_first, small_second)
    small_new = jnp.concatenate([(small_new[:D].reshape(H, HD) * shrink[:, None]).reshape(D), small_new[D:]])

    index = jnp.arange(tile_count, dtype=jnp.int32)
    rates = jnp.where(
        index < bounds[1],
        D ** (-0.5),
        jnp.where(index < bounds[2], (SEQ / (2.0 * D)) ** 0.5, jnp.where(index < bounds[3], D ** (-0.5), FF ** (-0.5))),
    ).astype(F32)
    column = index % (3 * heads)
    shrink_here = lax.dynamic_slice_in_dim(shrink, place * heads, heads)
    factors = jnp.where((index < bounds[1]) & (column < 2 * heads), shrink_here[column % heads], 1.0)
    ones = jnp.ones((tile_count,), F32)
    token_count = float(dp_count * SEQ)
    state = [value[0, 0] for value in (master, first_moment, second_moment, left_stats, right_stats, left_basis, right_basis)]
    tiles_up = sum_up.reshape(edge_tiles, HD, hidden_tiles, HD).transpose(0, 2, 1, 3).reshape(tile_u, HD, HD)
    tiles_down = sum_down.reshape(edge_tiles, HD, hidden_tiles, HD).transpose(2, 0, 1, 3).reshape(tile_u, HD, HD)
    tiles_out = sum_out.reshape(edge_tiles, HD, heads, HD).transpose(2, 0, 1, 3).reshape(tile_o, HD, HD)
    tiles_qkv = sum_qkv.reshape(edge_tiles, HD, heads, 3, HD).transpose(0, 3, 2, 1, 4).reshape(tile_q, HD, HD)
    done = update_tiles(tiles_down, state, rates, ones, bounds[3], None, True, token_count)
    done = update_tiles(tiles_up, state, rates, ones, bounds[2], done, False, token_count)
    done = update_tiles(tiles_qkv, state, rates, factors, 0, done, False, token_count)
    done = update_tiles(tiles_out, state, rates, ones, bounds[1], done, True, token_count)
    return (
        outputs,
        input_grad,
        *[value[None, None] for value in done],
        small_first_new,
        small_second_new,
        small_new,
    )


def solution(mesh):
    rows = P(("dp", "tensor"), None)
    tiles = P("dp", "tensor", None, None, None)
    return jax.shard_map(
        per_device,
        mesh=mesh,
        in_specs=(rows, rows, P("dp", None), P()) + (tiles,) * 7 + (P(), P(), P()),
        out_specs=(rows, rows) + (tiles,) * 8 + (P(), P(), P()),
        check_vma=False,
    )
```

```python
import math

import jax
import jax.numpy as jnp
from jax import lax
from jax.experimental import pallas as pl
from jax.experimental.pallas import tpu as pltpu
from jax.sharding import PartitionSpec as P

D = 2048
H = 16
HD = 128
FF = 8192
PROMPT = 1024
STEP = 5
NS_ITERS = 3
SEQ = 2048
BQ = 256
BF = jnp.bfloat16
F32 = jnp.float32
SCALE = HD ** (-0.5)
LOG2E = 1.4426950408889634
VMEM_CAP = 56 * 1024 * 1024


def cost(seconds):
    return pl.CostEstimate(flops=0, bytes_accessed=int(seconds * 3.5e12), transcendentals=0)


def dot_nt(a, b):
    return lax.dot_general(a, b, (((1,), (1,)), ((), ())), preferred_element_type=F32)


def dot_tn(a, b):
    return lax.dot_general(a, b, (((0,), (0,)), ((), ())), preferred_element_type=F32)


def dot_nn(a, b):
    return lax.dot_general(a, b, (((1,), (0,)), ((), ())), preferred_element_type=F32)


def key_parts(lo):
    if lo < PROMPT:
        return ([(0, lo, False)] if lo else []) + [(lo, lo + BQ, True)]
    return [(0, PROMPT, False), (PROMPT, lo + BQ, True)]


def part_scores(keys, query_block, lo, part, start_row):
    first, last, masked = part
    product = dot_nt(keys[first:last], query_block)
    if masked:
        key_pos = first + lax.broadcasted_iota(jnp.int32, product.shape, 0)
        query_pos = lo + lax.broadcasted_iota(jnp.int32, product.shape, 1)
        seen = (key_pos <= query_pos) & (key_pos >= start_row)
        product = jnp.where(seen, product, -1e30)
    return product


def softmax_parts(scores):
    top = scores[0].max(axis=0, keepdims=True)
    for piece in scores[1:]:
        top = jnp.maximum(top, piece.max(axis=0, keepdims=True))
    weights = [jnp.exp2((piece - top) * (SCALE * LOG2E)) for piece in scores]
    total = weights[0].sum(axis=0, keepdims=True)
    for piece in weights[1:]:
        total = total + piece.sum(axis=0, keepdims=True)
    return top, weights, total


def attend_kernel(start_ref, qkv_ref, out_ref, peak_ref):
    keys = qkv_ref[:, HD : 2 * HD]
    values_t = qkv_ref[:, 2 * HD :].T
    peak = jnp.full((1, BQ), -1e30, F32)
    for lo in range(0, SEQ, BQ):
        query_block = qkv_ref[lo : lo + BQ, :HD]
        start_row = start_ref[:, lo : lo + BQ]
        parts = key_parts(lo)
        scores = [part_scores(keys, query_block, lo, part, start_row) for part in parts]
        top, weights, total = softmax_parts(scores)
        peak = jnp.maximum(peak, top)
        mixed = None
        for (first, last, _), piece in zip(parts, weights):
            term = dot_nn(values_t[:, first:last], piece.astype(BF))
            mixed = term if mixed is None else mixed + term
        out_ref[lo : lo + BQ, :] = (mixed * (1.0 / total)).T.astype(BF)
    peak_ref[...] = jnp.broadcast_to(peak.max(axis=1, keepdims=True) * SCALE, peak_ref.shape)


def attend(start_rows, qkv):
    heads = qkv.shape[1] // (3 * HD)
    return pl.pallas_call(
        attend_kernel,
        grid=(heads,),
        in_specs=[
            pl.BlockSpec((1, SEQ), lambda h: (0, 0)),
            pl.BlockSpec((SEQ, 3 * HD), lambda h: (0, h)),
        ],
        out_specs=[
            pl.BlockSpec((SEQ, HD), lambda h: (0, h)),
            pl.BlockSpec((1, 8, HD), lambda h: (h, 0, 0)),
        ],
        out_shape=[
            jax.ShapeDtypeStruct((SEQ, heads * HD), BF),
            jax.ShapeDtypeStruct((heads, 8, HD), F32),
        ],
        compiler_params=pltpu.CompilerParams(vmem_limit_bytes=VMEM_CAP),
        cost_estimate=cost(heads * 5e-6),
        name="attend",
    )(start_rows, qkv)


def attend_back_kernel(start_ref, qkv_ref, back_ref, out_ref, key_acc, value_acc):
    keys = qkv_ref[:, HD : 2 * HD]
    values = qkv_ref[:, 2 * HD :]
    keys_t = keys.T
    key_acc[...] = jnp.zeros_like(key_acc)
    value_acc[...] = jnp.zeros_like(value_acc)
    for lo in range(0, SEQ, BQ):
        query_block = qkv_ref[lo : lo + BQ, :HD]
        back_block = back_ref[lo : lo + BQ, :]
        start_row = start_ref[:, lo : lo + BQ]
        parts = key_parts(lo)
        scores = [part_scores(keys, query_block, lo, part, start_row) for part in parts]
        top, weights, total = softmax_parts(scores)
        inverse = 1.0 / total
        probs = [piece * inverse for piece in weights]
        grads = [dot_nt(values[first:last], back_block) for first, last, _ in parts]
        mean = None
        for piece, grad in zip(probs, grads):
            term = (piece * grad).sum(axis=0, keepdims=True)
            mean = term if mean is None else mean + term
        query_t = None
        for (first, last, _), piece, grad in zip(parts, probs, grads):
            low = (piece * ((grad - mean) * SCALE)).astype(BF)
            value_acc[first:last, :] += dot_nn(piece.astype(BF), back_block)
            key_acc[first:last, :] += dot_nn(low, query_block)
            term = dot_nn(keys_t[:, first:last], low)
            query_t = term if query_t is None else query_t + term
        out_ref[lo : lo + BQ, :HD] = query_t.T.astype(BF)
    out_ref[:, HD : 2 * HD] = key_acc[...].astype(BF)
    out_ref[:, 2 * HD :] = value_acc[...].astype(BF)


def attend_back(start_rows, qkv, back):
    heads = qkv.shape[1] // (3 * HD)
    return pl.pallas_call(
        attend_back_kernel,
        grid=(heads,),
        in_specs=[
            pl.BlockSpec((1, SEQ), lambda h: (0, 0)),
            pl.BlockSpec((SEQ, 3 * HD), lambda h: (0, h)),
            pl.BlockSpec((SEQ, HD), lambda h: (0, h)),
        ],
        out_specs=pl.BlockSpec((SEQ, 3 * HD), lambda h: (0, h)),
        out_shape=jax.ShapeDtypeStruct(qkv.shape, BF),
        scratch_shapes=[pltpu.VMEM((SEQ, HD), F32), pltpu.VMEM((SEQ, HD), F32)],
        compiler_params=pltpu.CompilerParams(vmem_limit_bytes=VMEM_CAP),
        cost_estimate=cost(heads * 10e-6),
        name="attend_back",
    )(start_rows, qkv, back)


TILE_GROUP = 8


def orthonormal_all(matrices):
    currents = []
    for matrix in matrices:
        frob = jnp.sqrt(jnp.sum(matrix * matrix, axis=(0, 1), keepdims=True))
        currents.append(matrix * (1.0 / (frob + 1e-06)))
    for _ in range(NS_ITERS):
        lows = [current.astype(BF) for current in currents]
        grams = [dot_nt(low, low).astype(BF) for low in lows]
        terms = [dot_nn(gram, low) for gram, low in zip(grams, lows)]
        currents = [1.5 * current - 0.5 * term for current, term in zip(currents, terms)]
    return currents


def update_kernel(tile_group, turned_grad, token_count, *refs):
    rate_ref, factor_ref, grad_ref = refs[:3]
    master_ref, first_ref, second_ref, left_stat_ref, right_stat_ref, left_ref, right_ref = refs[3:10]
    outs = refs[-8:]
    first_out, second_out, master_out, weight_out, left_stat_out, right_stat_out, left_out, right_out = outs
    base = pl.program_id(0) * tile_group
    group = range(tile_group)
    grads = [grad_ref[i] for i in group]
    lefts = [left_ref[i].astype(BF) for i in group]
    rights = [right_ref[i].astype(BF) for i in group]
    if turned_grad:
        outer_rows = [dot_tn(grad, grad) for grad in grads]
        outer_cols = [dot_nt(grad, grad) for grad in grads]
        halves = [dot_nn(grad, left).astype(BF) for grad, left in zip(grads, lefts)]
        rotated = [dot_tn(half, right) for half, right in zip(halves, rights)]
    else:
        outer_rows = [dot_nt(grad, grad) for grad in grads]
        outer_cols = [dot_tn(grad, grad) for grad in grads]
        halves = [dot_nn(grad, right).astype(BF) for grad, right in zip(grads, rights)]
        rotated = [dot_tn(left, half) for left, half in zip(lefts, halves)]
    directions = []
    for i in group:
        new_first = 0.5 * first_ref[i] + 0.5 * rotated[i]
        new_second = 0.5 * second_ref[i] + 0.5 * rotated[i] * rotated[i]
        first_out[i] = new_first
        second_out[i] = new_second
        direction = (
            new_first
            * (1.0 / (1.0 - 0.5**STEP))
            / (jnp.sqrt(new_second * (1.0 / (1.0 - 0.5**STEP))) + 1e-08)
        )
        directions.append(direction.astype(BF))
    turned = [dot_nn(left, direction).astype(BF) for left, direction in zip(lefts, directions)]
    turned = [dot_nt(half, right) for half, right in zip(turned, rights)]
    for i in group:
        master = master_ref[i]
        new_master = (master - rate_ref[base + i] * (turned[i] + 0.1 * master)) * factor_ref[base + i]
        master_out[i] = new_master
        weight_out[i] = new_master.astype(BF)
    moved = []
    for stat_ref, stat_out, outers, bases in (
        (left_stat_ref, left_stat_out, outer_rows, lefts),
        (right_stat_ref, right_stat_out, outer_cols, rights),
    ):
        for i in group:
            new_stat = 0.5 * stat_ref[i] + (0.5 / (HD * token_count)) * outers[i]
            stat_out[i] = new_stat
            moved.append(dot_nn(new_stat.astype(BF), bases[i]))
    moved = orthonormal_all(moved)
    for i in group:
        left_out[i] = moved[i]
        right_out[i] = moved[tile_group + i]


def update_tiles(grads, state, rates, factors, first_tile, earlier, turned_grad, token_count):
    count = grads.shape[0]
    tiles = state[0].shape[0]
    group = math.gcd(math.gcd(count, first_tile), TILE_GROUP)
    offset = first_tile // group
    block = (group, HD, HD)
    here = pl.BlockSpec(block, lambda i: (i + offset, 0, 0))
    smem = pl.BlockSpec(memory_space=pltpu.SMEM)
    kinds = [F32, F32, F32, BF, F32, F32, F32, F32]
    earlier = list(earlier) if earlier is not None else []

    def body(*refs):
        update_kernel(group, turned_grad, token_count, *refs)

    return pl.pallas_call(
        body,
        grid=(count // group,),
        in_specs=[smem, smem, pl.BlockSpec(block, lambda i: (i, 0, 0))]
        + [here] * 7
        + [pl.BlockSpec(memory_space=pl.ANY)] * len(earlier),
        out_specs=[here] * 8,
        out_shape=[jax.ShapeDtypeStruct((tiles, HD, HD), kind) for kind in kinds],
        input_output_aliases={10 + i: i for i in range(len(earlier))},
        compiler_params=pltpu.CompilerParams(vmem_limit_bytes=VMEM_CAP),
        cost_estimate=cost(count * 5e-7),
        name="update_tiles",
    )(rates[first_tile : first_tile + count], factors[first_tile : first_tile + count], grads, *state, *earlier)


def grad_kernel(chunks, parts, block_ref, *refs):
    lefts, rights, out_ref = refs[:chunks], refs[chunks:-1], refs[-1]
    turned = [left[...].T for left in lefts]
    lo = 0
    for j in range(parts):
        mine = rights[j * chunks : (j + 1) * chunks]
        width = mine[0].shape[1]
        step = min(512, width)
        for at in range(0, width, step):
            total = dot_nn(turned[0], mine[0][:, at : at + step])
            for left, right in zip(turned[1:], mine[1:]):
                total = total + dot_nn(left, right[:, at : at + step])
            out_ref[0, :, lo + at : lo + at + step] = total.astype(BF)
        lo += width


def grad_blocks(blocks, lefts, rights, edge):
    count = blocks.shape[0]
    rows = sum(left.shape[0] for left in lefts)
    width = sum(right[0].shape[1] for right in rights)
    flat = [chunk for right in rights for chunk in right]

    def body(*refs):
        grad_kernel(len(lefts), len(rights), *refs)

    return pl.pallas_call(
        body,
        grid_spec=pltpu.PrefetchScalarGridSpec(
            num_scalar_prefetch=1,
            grid=(count,),
            in_specs=[pl.BlockSpec((left.shape[0], edge), lambda i, blocks: (0, blocks[i])) for left in lefts]
            + [pl.BlockSpec(chunk.shape, lambda i, blocks: (0, 0)) for chunk in flat],
            out_specs=pl.BlockSpec((1, edge, width), lambda i, blocks: (i, 0, 0)),
        ),
        out_shape=jax.ShapeDtypeStruct((count, edge, width), BF),
        compiler_params=pltpu.CompilerParams(vmem_limit_bytes=VMEM_CAP),
        cost_estimate=cost(2 * count * edge * width * rows / 8e14),
        name="grad_blocks",
    )(blocks, *lefts, *flat)


def matmul_kernel(terms, *refs):
    lefts, rights, out_ref = refs[:terms], refs[terms : 2 * terms], refs[2 * terms]
    total = dot_nt(lefts[0][...], rights[0][...])
    for left, right in zip(lefts[1:], rights[1:]):
        total = total + dot_nt(left[...], right[...])
    out_ref[...] = total.astype(BF)


def matmul_sum(lefts, rights):
    terms = len(lefts)
    rows, depth = lefts[0].shape
    columns = rights[0].shape[0]
    row_step, step = min(1024, rows), min(512, columns)

    def body(*refs):
        matmul_kernel(terms, *refs)

    return pl.pallas_call(
        body,
        grid=(rows // row_step, columns // step),
        in_specs=[pl.BlockSpec((row_step, depth), lambda m, n: (m, 0))] * terms
        + [pl.BlockSpec((step, depth), lambda m, n: (n, 0))] * terms,
        out_specs=pl.BlockSpec((row_step, step), lambda m, n: (m, n)),
        out_shape=jax.ShapeDtypeStruct((rows, columns), BF),
        compiler_params=pltpu.CompilerParams(vmem_limit_bytes=VMEM_CAP),
        cost_estimate=cost(2 * terms * rows * columns * depth / 8e14),
        name="matmul_sum",
    )(*lefts, *rights)


def pack_kernel(heads, edge_tiles, hidden_tiles, core_ref, tiles_ref, halves_ref, qkv_ref, out_ref):
    core = core_ref[0]
    half = hidden_tiles // 2 * HD
    first = 0
    for row in range(edge_tiles):
        for part in range(3):
            for head in range(heads):
                tile = tiles_ref[first + (row * 3 + part) * heads + head].astype(BF)
                at = (head * 3 + part) * HD
                qkv_ref[row * HD : (row + 1) * HD, at : at + HD] = tile
    first += edge_tiles * 3 * heads
    for head in range(heads):
        for row in range(edge_tiles):
            tile = tiles_ref[first + head * edge_tiles + row].T.astype(BF)
            out_ref[row * HD : (row + 1) * HD, head * HD : (head + 1) * HD] = tile
    first += heads * edge_tiles
    for kind in range(2):
        for row in range(edge_tiles):
            for column in range(hidden_tiles):
                part, inner = divmod(column, hidden_tiles // 2)
                at = kind * half + inner * HD
                if kind == 0:
                    tile = tiles_ref[first + row * hidden_tiles + column].astype(BF)
                else:
                    tile = tiles_ref[first + column * edge_tiles + row].T.astype(BF)
                halves_ref[part ^ core, row * HD : (row + 1) * HD, at : at + HD] = tile
        first += edge_tiles * hidden_tiles


def pack_weights(tiles, core, heads, edge_tiles, hidden_tiles):
    edge = edge_tiles * HD

    def body(*refs):
        pack_kernel(heads, edge_tiles, hidden_tiles, *refs)

    shapes = [(2, edge, hidden_tiles * HD), (edge, 3 * heads * HD), (edge, heads * HD)]
    return pl.pallas_call(
        body,
        grid_spec=pltpu.PrefetchScalarGridSpec(
            num_scalar_prefetch=1,
            grid=(1,),
            in_specs=[pl.BlockSpec(tiles.shape, lambda i, core: (0, 0, 0))],
            out_specs=[pl.BlockSpec(shapes[0], lambda i, core: (0, 0, 0))]
            + [pl.BlockSpec(shape, lambda i, core: (0, 0)) for shape in shapes[1:]],
        ),
        out_shape=[jax.ShapeDtypeStruct(shape, BF) for shape in shapes],
        compiler_params=pltpu.CompilerParams(vmem_limit_bytes=VMEM_CAP),
        cost_estimate=cost(5e-6),
        name="pack_weights",
    )(core[None], tiles)


def scatter_kernel(tables, *refs):
    source_ref, outs = refs[tables], refs[tables + 1 :]
    lo = 0
    for out in outs:
        width = out.shape[1]
        out[...] = source_ref[0, :, lo : lo + width]
        lo += width


def scatter_blocks(tables, source):
    count, edge, columns = source.shape
    parts = len(tables)
    width = columns // parts

    def body(*refs):
        scatter_kernel(parts, *refs)

    def out_spec(k):
        return pl.BlockSpec((edge, width), lambda i, *tables: (tables[k][i], 0))

    return pl.pallas_call(
        body,
        grid_spec=pltpu.PrefetchScalarGridSpec(
            num_scalar_prefetch=parts,
            grid=(count,),
            in_specs=[pl.BlockSpec((1, edge, columns), lambda i, *tables: (i, 0, 0))],
            out_specs=[out_spec(k) for k in range(parts)],
        ),
        out_shape=[jax.ShapeDtypeStruct((count * edge, width), BF)] * parts,
        compiler_params=pltpu.CompilerParams(vmem_limit_bytes=VMEM_CAP),
        cost_estimate=cost(4 * count * edge * columns / 3e12),
        name="scatter_blocks",
    )(*tables, source)


def project_kernel(sources, *refs):
    pick_ref = refs[0]
    pieces = refs[2 : 2 + sources]
    gain_ref, shift_ref, weight_ref, bias_ref = refs[2 + sources : 6 + sources]
    normal_out, normed_out, out_ref = refs[-3:]
    picked = pick_ref[pl.program_id(0)]
    for i in range(sources):

        @pl.when(picked == i)
        def _():
            normal_out[...] = pieces[i][...]

    normed = (normal_out[...].astype(F32) * gain_ref[...] + shift_ref[...]).astype(BF)
    normed_out[...] = normed
    out_ref[...] = (dot_nn(normed, weight_ref[...]) + bias_ref[...]).astype(BF)


def project(pick, place, total, pieces, gain, shift_by, weight, bias, into=()):
    count = pick.shape[0]
    rows, depth = pieces[0].shape
    columns = weight.shape[1]

    def body(*refs):
        project_kernel(len(pieces), *refs)

    def held(shape):
        return pl.BlockSpec(shape, lambda i, pick, place: (0, 0), pipeline_mode=pl.Buffered(1))

    def block(width):
        return pl.BlockSpec((rows, width), lambda i, pick, place: (place[i], 0))

    return pl.pallas_call(
        body,
        grid_spec=pltpu.PrefetchScalarGridSpec(
            num_scalar_prefetch=2,
            grid=(count,),
            in_specs=[held((rows, depth)) for _ in pieces]
            + [held((1, depth)), held((1, depth)), held((depth, columns)), held((1, columns))]
            + [pl.BlockSpec(memory_space=pl.ANY) for _ in into],
            out_specs=[block(depth), block(depth), block(columns)],
        ),
        out_shape=[jax.ShapeDtypeStruct((total * rows, width), BF) for width in (depth, depth, columns)],
        input_output_aliases={2 + len(pieces) + 4 + k: k for k in range(len(into))},
        compiler_params=pltpu.CompilerParams(vmem_limit_bytes=VMEM_CAP),
        cost_estimate=cost(count * 6e-6),
        name="project",
    )(pick, place, *pieces, gain[None], shift_by[None], weight, bias[None], *into)


def sync(*values):
    return lax.optimization_barrier(values)


def shift(value, axis, mask):
    return lax.ppermute(value, axis, [(i, i ^ mask) for i in range(lax.axis_size(axis))])


def move(value, axis, pairs):
    return lax.ppermute(value, axis, pairs)


def beside(value, axis, mask, steps, state):
    total, rows = sum(share for share, _ in steps), value.shape[0]
    pieces, done, first = [], 0, 0
    for share, work in steps:
        done += share
        last = rows // 16 * done // total * 16
        pieces.append(shift(value[first:last], axis, mask))
        first = last
        state = work(state)
        state, pieces, value = sync(state, pieces, value)
    return jnp.concatenate(pieces, axis=0), state


def add_low(left, right):
    return (left.astype(F32) + right.astype(F32)).astype(BF)


def join_halves(mine, other):
    first = (lax.axis_index("dp") & 1) == 0
    return jnp.concatenate([jnp.where(first, mine, other), jnp.where(first, other, mine)], axis=-1)


def halving_order(chips, masks):
    return sorted(chips, key=lambda q: tuple(-(q & (mask >> 1)) for mask in masks))


def halve(blocks, masks):
    for mask in masks:
        count = blocks.shape[0] // 2
        blocks = add_low(blocks[count:], shift(blocks[:count], "dp", mask))
    return blocks


def layer_norm(token_rows, gain, shift_by):
    centre = jnp.mean(token_rows, axis=-1, keepdims=True)
    centred = token_rows - centre
    spread = jnp.mean(centred * centred, axis=-1, keepdims=True)
    return centred * lax.rsqrt(spread + 1e-05) * gain + shift_by


def layer_norm_back(token_rows, gain, grad):
    centre = jnp.mean(token_rows, axis=-1, keepdims=True)
    centred = token_rows - centre
    inverse = lax.rsqrt(jnp.mean(centred * centred, axis=-1, keepdims=True) + 1e-05)
    normal = centred * inverse
    scaled = grad * gain
    back = (
        scaled - jnp.mean(scaled, axis=-1, keepdims=True) - normal * jnp.mean(scaled * normal, axis=-1, keepdims=True)
    ) * inverse
    return back, jnp.sum(grad * normal, axis=0), jnp.sum(grad, axis=0)


def gelu_pair(pre_act):
    cdf = 0.5 * (1.0 + lax.erf(pre_act * (0.5**0.5)))
    density = jnp.exp(-0.5 * pre_act * pre_act) * 0.3989422804014327
    return pre_act * cdf, cdf + pre_act * density


def axis_sum(value, axis):
    for bit in range(lax.axis_size(axis).bit_length() - 1):
        value = value + shift(value, axis, 1 << bit)
    return value


def small_step(summed, params, first, second):
    new_first = 0.5 * first + 0.5 * summed
    new_second = 0.5 * second + 0.5 * summed * summed
    direction = new_first / (1.0 - 0.5**STEP) / (jnp.sqrt(new_second / (1.0 - 0.5**STEP)) + 1e-08)
    return new_first, new_second, params - 0.1 * direction


def per_device(
    inputs,
    cotangent,
    lengths,
    held_blocks,
    master,
    first_moment,
    second_moment,
    left_stats,
    right_stats,
    left_basis,
    right_basis,
    small_params,
    small_first,
    small_second,
):
    dp_count = lax.axis_size("dp")
    tp_count = lax.axis_size("tensor")
    me = lax.axis_index("dp")
    place = lax.axis_index("tensor")
    core = me & 1
    rows = inputs.shape[0]
    edge = D // dp_count
    width = D // tp_count
    hidden = FF // tp_count
    half = hidden // 2
    heads = width // HD
    edge_tiles = edge // HD
    hidden_tiles = hidden // HD
    tile_q = edge_tiles * 3 * heads
    tile_o = heads * edge_tiles
    tile_u = edge_tiles * hidden_tiles
    tile_count = master.shape[2]
    near = [1 << bit for bit in range(1, dp_count.bit_length() - 1)]
    far = near[::-1]
    slices = tp_count // 2
    chips = range(dp_count // 2)
    relative = jnp.arange(dp_count, dtype=jnp.int32) ^ me
    block_of = jnp.take(held_blocks, relative, axis=1)

    bias_q = lax.dynamic_slice_in_dim(small_params, place * width, width)
    bias_v = lax.dynamic_slice_in_dim(small_params, D + place * width, width)
    bias_o = small_params[2 * D : 3 * D]
    bias_two = small_params[3 * D : 4 * D]
    gain_one = small_params[4 * D : 5 * D]
    shift_one = small_params[5 * D : 6 * D]
    gain_two = small_params[6 * D : 7 * D]
    shift_two = small_params[7 * D : 8 * D]
    hidden_starts = [(place ^ (2 * j)) * hidden + core * half for j in range(slices)]
    bias_up = jnp.concatenate(
        [lax.dynamic_slice_in_dim(small_params, 8 * D + start, half) for start in hidden_starts]
    )

    token_rows = inputs.astype(F32)
    centred = token_rows - jnp.mean(token_rows, axis=-1, keepdims=True)
    spread = jnp.mean(centred * centred, axis=-1, keepdims=True)
    normal = (centred * lax.rsqrt(spread + 1e-05)).astype(BF)
    ups = [(i, i + 1) for i in range(tp_count - 1)]
    downs = [(i + 1, i) for i in range(tp_count - 1)]
    above, below = [move(normal, "tensor", downs)], [move(normal, "tensor", ups)]

    bounds = [0, tile_q, tile_q + tile_o, tile_q + tile_o + tile_u, tile_count]
    halves, own_qkv, own_out = pack_weights(master[0, 0], core, heads, edge_tiles, hidden_tiles)
    pair = jnp.stack([halves[0], shift(halves[1], "dp", 1)])
    same_core = [list(range(at, dp_count, 2)) for at in range(2)]
    pair_slots = jnp.arange(dp_count, dtype=jnp.int32) ^ core

    def gather_ffn(value):
        return lax.all_gather(value, "dp", axis=0, tiled=True, axis_index_groups=same_core)

    def scatter_ffn(value):
        return scatter_blocks([held_blocks[2][pair_slots], held_blocks[3][pair_slots]], value)

    def gather_all(kind, value):
        value = lax.all_gather(value, "dp", axis=0, tiled=False)
        return scatter_blocks([held_blocks[kind]], value)[0]

    def crossed(mask, odd):
        return [(i, i ^ mask) for i in range(tp_count) if ((i ^ (i >> 1)) & 1) == odd]

    w_qkv = gather_all(0, own_qkv)
    bias_mixed = jnp.stack(
        [bias_q.reshape(heads, HD), jnp.zeros((heads, HD), F32), bias_v.reshape(heads, HD)], axis=1
    ).reshape(3 * width)
    distance = jnp.arange(tp_count, dtype=jnp.int32) - place
    by_distance = jnp.argsort(jnp.abs(distance)).astype(jnp.int32)
    offset = by_distance - place
    outs = [shift(own_out, "tensor", j) for j in range(1, tp_count)]
    far_first, first_raw, out_raw = [], None, None
    for step in range(1, tp_count):
        if step > 1:
            below.append(move(below[-1], "tensor", ups[step - 1 :]))
            above.append(move(above[-1], "tensor", downs[: tp_count - step]))
        if step == tp_count - 1:
            first_raw = gather_ffn(pair)
            far_first = [move(pair, "tensor", crossed(2 * j, 0)) for j in range(1, slices)]
            w_out = scatter_blocks([held_blocks[1]], out_raw)[0]
            pick = jnp.where(offset < 0, -offset, jnp.where(offset > 0, tp_count - 2 + offset, 0))
            sources = [normal] + below[:-1] + above[:-1]
            projected = project(
                pick[:-1], by_distance[:-1], tp_count, sources, gain_one, shift_one, w_qkv, bias_mixed
            )
            above, below, far_first, pair, w_qkv, w_out, projected = sync(
                above, below, far_first, pair, w_qkv, w_out, projected
            )
        elif step == 1:
            above, below, outs, own_out, pair = sync(above, below, outs, own_out, pair)
            out_raw = lax.all_gather(jnp.concatenate([own_out] + outs, axis=1), "dp", axis=0, tiled=False)
        else:
            above, below, pair = sync(above, below, pair)

    reach = tp_count // 2
    pick = jnp.where(offset < 0, -offset - reach, tp_count - 1 + offset - 2 * reach + 1)
    sources = below[reach - 1 :] + above[reach - 1 :]
    normal_all, normed_all, qkv = project(
        pick[-1:], by_distance[-1:], tp_count, sources, gain_one, shift_one, w_qkv, bias_mixed, projected
    )
    far_second = [move(pair, "tensor", crossed(2 * j, 1)) for j in range(1, slices)]

    ends = jnp.cumsum(lengths[0])
    spot = jnp.arange(SEQ, dtype=jnp.int32) - PROMPT
    started = jnp.max(jnp.where(ends[None, :] <= spot[:, None], ends[None, :], 0), axis=1)
    start_rows = jnp.where(spot < 0, 0, PROMPT + started).astype(jnp.int32)[None]
    attended, peaks = attend(start_rows, qkv)
    others = range(1, slices)
    peak_row = lax.dynamic_update_slice(
        jnp.zeros((dp_count * H,), F32), peaks[:, 0, 0], (me * H + place * heads,)
    )
    attended, far_second = sync(attended, far_second)

    def rows_of(value, j):
        return lax.dynamic_slice_in_dim(value, (place ^ j) * rows, rows, 0)

    def with_core(value):
        return jnp.concatenate([value, shift(value, "dp", 1)], axis=0)

    attended_rows = jnp.concatenate(
        [rows_of(attended, 0)] + [shift(rows_of(attended, j), "tensor", j) for j in range(1, tp_count)], axis=1
    )
    far_raw = [gather_ffn(left + right) for left, right in zip(far_first, far_second)]
    w_first = scatter_ffn(first_raw)
    back_near = with_core(cotangent)
    peak_rows = axis_sum(peak_row, "dp")
    attended_rows, w_first, cotangent, back_near, w_out, peak_rows = sync(
        attended_rows, w_first, cotangent, back_near, w_out, peak_rows
    )
    hidden_rows = token_rows + dot_nt(attended_rows, w_out) + bias_o
    normed_two = layer_norm(hidden_rows, gain_two, shift_two).astype(BF)

    w_up, w_down = [w_first[0]], [w_first[1]]
    biases = [bias_up[j * half : (j + 1) * half] for j in range(slices)]

    def core_rows(partial):
        return add_low(partial[:rows], shift(partial[rows:], "dp", 1))

    def chips_sum(blocks):
        blocks = blocks.reshape(dp_count // 2, 2, edge, blocks.shape[2])
        return lax.psum_scatter(blocks, "dp", scatter_dimension=0, tiled=False, axis_index_groups=same_core)

    def near_back(j):
        def work(state):
            if j > 0:
                up, down = state.pop("arrived")
                w_up.append(up)
                w_down.append(down)
            grad_act = jnp.dot(state["back_near"], w_down[j], preferred_element_type=F32).astype(BF)
            state = dict(state, grad_act=grad_act)
            if j == 0:
                state["normed_near"] = with_core(state.pop("normed"))
            return state

        return work

    def near_up(j):
        def work(state):
            pre_act = jnp.dot(state["normed_near"], w_up[j], preferred_element_type=F32) + biases[j]
            activation, slope = gelu_pair(pre_act)
            low = (state["grad_act"].astype(F32) * slope).astype(BF)
            if j + 1 < slices:
                state = dict(state, far_raw=far_raw[j])
            return dict(state, act_near=state["act_near"] + [activation.astype(BF)], pre_near=state["pre_near"] + [low])

        return work

    def far_up(j):
        def work(state):
            pre_act = jnp.dot(state["normed_far"], w_up[j], preferred_element_type=F32) + biases[j]
            activation, slope = gelu_pair(pre_act)
            return dict(state, act_far=state["act_far"] + [activation.astype(BF)], slopes=state["slopes"] + [slope.astype(BF)])

        return work

    def far_result(state):
        return dict(state, result_far=matmul_sum(state["act_far"], w_down))

    def near_grad(state):
        return dict(
            state, grad_near=matmul_sum(state["pre_near"], w_up), ffn_far=core_rows(state.pop("result_far"))
        )

    def down_blocks(state):
        rights = [list(pair) for pair in zip(state["act_near"], state["act_far"])]
        blocks = grad_blocks(held_blocks[3][pair_slots], [state["back_near"], state["back_far"]], rights, edge)
        return dict(state, down=blocks)

    def far_back(j):
        def work(state):
            grad_act = jnp.dot(state["back_far"], w_down[j], preferred_element_type=F32)
            low = (grad_act * state["slopes"][j].astype(F32)).astype(BF)
            return dict(state, pre_far=state["pre_far"] + [low])

        return work

    def far_grad(state):
        return dict(state, grad_far=matmul_sum(state["pre_far"], w_up))

    def up_blocks(state):
        rights = [list(pair) for pair in zip(state["pre_near"], state["pre_far"])]
        blocks = grad_blocks(held_blocks[2][pair_slots], [state["normed_near"], state["normed_far"]], rights, edge)
        return dict(state, up=blocks)

    def near_result(state):
        return dict(
            state, result_near=matmul_sum(state["act_near"], w_down), near_rows=core_rows(state.pop("grad_near"))
        )

    def both(first, second):
        return lambda state: second(first(state))

    state = dict(
        back_near=back_near, normed=normed_two, act_near=[], pre_near=[], act_far=[], pre_far=[], slopes=[]
    )
    def arrive(state):
        state = dict(state)
        state["arrived"] = scatter_ffn(state.pop("far_raw"))
        return state

    steps = []
    for j in range(slices):
        steps += [(1, arrive)] * (j > 0) + [(2, both(near_back(j), near_up(j)))]
    normed_across, state = beside(normed_two, "tensor", 1, steps, state)
    state["normed_across"] = normed_across

    def far_rows_in(state):
        state = dict(state)
        state["normed_far"] = with_core(state.pop("normed_across"))
        return state

    def back_rows_in(state):
        state = dict(state)
        state["back_far"] = with_core(state.pop("back_across"))
        return state

    work = both(far_rows_in, far_up(0))
    for j in range(1, slices):
        work = both(work, far_up(j))
    steps = [(slices, work)]
    steps += [(slices, far_result), (slices, near_grad)]
    back_across, state = beside(cotangent, "tensor", 1, steps, state)
    state["back_across"] = back_across
    middle = rows // 2
    ffn_low, state = beside(state["ffn_far"][:middle], "tensor", 1, [(1, both(back_rows_in, down_blocks))], state)
    part_down = chips_sum(state.pop("down"))
    steps = [(1, far_back(j)) for j in range(slices)] + [(slices, far_grad)]
    ffn_high, state = beside(state.pop("ffn_far")[middle:], "tensor", 1, steps, state)
    ffn_across = jnp.concatenate([ffn_low, ffn_high], axis=0)
    far_rows = core_rows(state.pop("grad_far"))
    state["far_rows"] = far_rows
    state = sync(state)[0]
    cut = rows // 16 * 5 // 8 * 16
    low_rows, state = beside(state["far_rows"][:cut], "tensor", 1, [(1, up_blocks)], state)
    part_up = chips_sum(state.pop("up"))
    high_rows, state = beside(state.pop("far_rows")[cut:], "tensor", 1, [(1, near_result)], state)
    low_rows, high_rows, part_down, state, peak_rows = sync(low_rows, high_rows, part_down, state, peak_rows)
    grad_two = state["near_rows"].astype(F32) + jnp.concatenate([low_rows, high_rows], axis=0).astype(F32)
    result, grads_pre = state["result_near"], list(zip(state["pre_near"], state["pre_far"]))

    def far_slices(part):
        return part[:, :, :half], [part[:, :, j * half : (j + 1) * half] for j in others]

    def to_owners(values):
        return [shift(value, "tensor", 2 * j) for j, value in zip(others, values)]

    order_far = halving_order(chips, far)

    def half_slots(order):
        return jnp.array([2 * q + 1 for q in order] + [2 * q for q in order], jnp.int32)

    own_down, far_down = far_slices(part_down)
    down_low = to_owners([value[:1] for value in far_down])
    grad_part, grad_gain_two, grad_shift_two = layer_norm_back(hidden_rows, gain_two, grad_two)
    grad_hidden = cotangent.astype(F32) + grad_part
    branch = grad_hidden.astype(BF)
    even = jnp.arange(0, dp_count, 2, dtype=jnp.int32)
    out_slots = jnp.concatenate([even + 1 - core, even + core])
    grads_out = grad_blocks(held_blocks[1][out_slots], [branch], [[attended_rows]], edge)
    grad_attended_rows = jnp.dot(branch, w_out, preferred_element_type=F32).astype(BF)
    peak_rows = peak_rows + shift(peak_rows, "tensor", 1)
    grad_attended_rows, branch, result, grads_pre, grads_out, down_low, far_down, peak_rows = sync(
        grad_attended_rows, branch, result, grads_pre, grads_out, down_low, far_down, peak_rows
    )

    arrived = [
        grad_attended_rows[:, j * width : (j + 1) * width]
        if j == 0
        else shift(grad_attended_rows[:, j * width : (j + 1) * width], "tensor", j)
        for j in range(tp_count)
    ]
    grad_attended = jnp.zeros((SEQ, width), BF)
    for j in range(tp_count):
        grad_attended = lax.dynamic_update_slice_in_dim(grad_attended, arrived[j], (place ^ j) * rows, 0)
    sum_out = halve(grads_out, [1])
    grad_attended, branch, result, part_up, far_down, grads_pre, sum_out = sync(
        grad_attended, branch, result, part_up, far_down, grads_pre, sum_out
    )

    def far_sum(kept, arrived):
        total = kept.astype(F32)
        for value in arrived:
            total = total + value.astype(F32)
        total = total.astype(BF)
        return join_halves(total[0], shift(total[1], "dp", 1))

    sum_out = lax.psum_scatter(sum_out, "dp", scatter_dimension=0, tiled=False, axis_index_groups=same_core)
    own_up, far_up = far_slices(part_up)
    down_high = to_owners([value[1:] for value in far_down])
    up_low = to_owners([value[:1] for value in far_up])
    grad_qkv_rows = attend_back(start_rows, qkv, grad_attended)
    grad_qkv_rows, down_high, up_low, far_up, branch, grads_pre = sync(
        grad_qkv_rows, down_high, up_low, far_up, branch, grads_pre
    )
    up_high = to_owners([value[1:] for value in far_up])
    partial = dot_nt(grad_qkv_rows, w_qkv).astype(BF)
    partial, up_high, grad_qkv_rows, branch, grads_pre, sum_out, peak_rows = sync(
        partial, up_high, grad_qkv_rows, branch, grads_pre, sum_out, peak_rows
    )
    far_down = [jnp.concatenate(value, axis=0) for value in zip(down_low, down_high)]
    far_up = [jnp.concatenate(value, axis=0) for value in zip(up_low, up_high)]
    grad_normed_one = lax.psum_scatter(partial, "tensor", scatter_dimension=0, tiled=True).astype(F32)

    grads_qkv = grad_blocks(block_of[0][half_slots(order_far)], [normed_all], [[grad_qkv_rows]], edge)
    for bit in range(1, tp_count.bit_length() - 1):
        peak_rows = peak_rows + shift(peak_rows, "tensor", 1 << bit)
    grads_qkv, grad_qkv_rows, branch, grads_pre, partial, peak_rows = sync(
        grads_qkv, grad_qkv_rows, branch, grads_pre, partial, peak_rows
    )
    column_sums = jnp.sum(grad_qkv_rows, axis=0, dtype=F32).reshape(heads, 3, HD)
    head_sums = lambda part: lax.dynamic_update_slice(
        jnp.zeros((D,), F32), column_sums[:, part].reshape(width), (place * width,)
    )
    partial_wide = partial.astype(F32)
    grad_bias_up = jnp.concatenate([sum(jnp.sum(value, axis=0, dtype=F32) for value in pair) for pair in grads_pre])
    wide = jnp.zeros((FF,), F32)
    for j in range(slices):
        wide = lax.dynamic_update_slice(wide, grad_bias_up[j * half : (j + 1) * half], (hidden_starts[j],))
    totals = jnp.concatenate(
        [
            head_sums(0),
            head_sums(2),
            jnp.sum(branch, axis=0, dtype=F32),
            jnp.sum(cotangent, axis=0, dtype=F32),
            jnp.sum(partial_wide * normal_all.astype(F32), axis=0),
            jnp.sum(partial_wide, axis=0),
            grad_gain_two,
            grad_shift_two,
            wide,
        ]
    )
    sum_qkv = halve(grads_qkv, [1])
    totals = axis_sum(totals, "dp")
    totals, sum_qkv = sync(totals, sum_qkv)
    sum_down = far_sum(own_down, far_down)
    sum_up = far_sum(own_up, far_up)

    index = jnp.arange(tile_count, dtype=jnp.int32)
    rates = jnp.where(
        index < bounds[1],
        D ** (-0.5),
        jnp.where(index < bounds[2], (SEQ / (2.0 * D)) ** 0.5, jnp.where(index < bounds[3], D ** (-0.5), FF ** (-0.5))),
    ).astype(F32)
    ones = jnp.ones((tile_count,), F32)
    token_count = float(dp_count * SEQ)
    state = [value[0, 0] for value in (master, first_moment, second_moment, left_stats, right_stats, left_basis, right_basis)]
    tiles_up = sum_up.reshape(edge_tiles, HD, hidden_tiles, HD).transpose(0, 2, 1, 3).reshape(tile_u, HD, HD)
    tiles_down = sum_down.reshape(edge_tiles, HD, hidden_tiles, HD).transpose(2, 0, 1, 3).reshape(tile_u, HD, HD)
    count = sum_qkv.shape[0] // 4
    done = list(update_tiles(tiles_down, state, rates, ones, bounds[3], None, True, token_count))
    low_part = shift(sum_qkv[:count], "dp", far[0])
    low_part, done[3], sum_qkv = sync(low_part, done[3], sum_qkv)
    done = list(update_tiles(tiles_up, state, rates, ones, bounds[2], done, False, token_count))
    high_part = shift(sum_qkv[count : 2 * count], "dp", far[0])
    high_part, done[3], sum_qkv = sync(high_part, done[3], sum_qkv)
    sum_qkv = add_low(sum_qkv[2 * count :], jnp.concatenate([low_part, high_part], axis=0))
    sum_qkv = halve(sum_qkv, far[1:])[0]
    ffn_near = core_rows(result)
    outputs = (hidden_rows + ffn_near.astype(F32) + ffn_across.astype(F32) + bias_two).astype(BF)
    peak_all = jnp.max(peak_rows.reshape(dp_count, H), axis=0)
    grad_normed_one, totals, sum_out = sync(grad_normed_one, totals, sum_out)
    grad_small = axis_sum(totals, "tensor")
    outs = [shift(sum_out[:, j * width : (j + 1) * width], "tensor", j) for j in range(1, tp_count)]
    total_out = sum_out[:, :width].astype(F32)
    for value in outs:
        total_out = total_out + value.astype(F32)
    sum_out = total_out.astype(BF)
    rows_part, _, _ = layer_norm_back(token_rows, gain_one, grad_normed_one)
    input_grad = (grad_hidden + rows_part).astype(BF)

    shrink = jnp.sqrt(1.0 / jnp.maximum(peak_all, 1.0))
    small_first_new, small_second_new, small_new = small_step(grad_small, small_params, small_first, small_second)
    small_new = jnp.concatenate([(small_new[:D].reshape(H, HD) * shrink[:, None]).reshape(D), small_new[D:]])

    column = index % (3 * heads)
    shrink_here = lax.dynamic_slice_in_dim(shrink, place * heads, heads)
    factors = jnp.where((index < bounds[1]) & (column < 2 * heads), shrink_here[column % heads], 1.0)
    tiles_out = sum_out.reshape(edge_tiles, HD, heads, HD).transpose(2, 0, 1, 3).reshape(tile_o, HD, HD)
    tiles_qkv = sum_qkv.reshape(edge_tiles, HD, heads, 3, HD).transpose(0, 3, 2, 1, 4).reshape(tile_q, HD, HD)
    done = update_tiles(tiles_qkv, state, rates, factors, 0, done, False, token_count)
    done = update_tiles(tiles_out, state, rates, ones, bounds[1], done, True, token_count)
    return (
        outputs,
        input_grad,
        *[value[None, None] for value in done],
        small_first_new,
        small_second_new,
        small_new,
    )


def solution(mesh):
    rows = P(("dp", "tensor"), None)
    tiles = P("dp", "tensor", None, None, None)
    return jax.shard_map(
        per_device,
        mesh=mesh,
        in_specs=(rows, rows, P("dp", None), P()) + (tiles,) * 7 + (P(), P(), P()),
        out_specs=(rows, rows) + (tiles,) * 8 + (P(), P(), P()),
        check_vma=False,
    )
```

```python
import math

import jax
import jax.numpy as jnp
from jax import lax
from jax.experimental import pallas as pl
from jax.experimental.pallas import tpu as pltpu
from jax.sharding import PartitionSpec as P

D = 2048
H = 16
HD = 128
FF = 8192
PROMPT = 1024
STEP = 5
NS_ITERS = 3
SEQ = 2048
BQ = 256
BF = jnp.bfloat16
F32 = jnp.float32
SCALE = HD ** (-0.5)
LOG2E = 1.4426950408889634
VMEM_CAP = 56 * 1024 * 1024


def cost(seconds):
    return pl.CostEstimate(flops=0, bytes_accessed=int(seconds * 3.5e12), transcendentals=0)


def dot_nt(a, b):
    return lax.dot_general(a, b, (((1,), (1,)), ((), ())), preferred_element_type=F32)


def dot_tn(a, b):
    return lax.dot_general(a, b, (((0,), (0,)), ((), ())), preferred_element_type=F32)


def dot_nn(a, b):
    return lax.dot_general(a, b, (((1,), (0,)), ((), ())), preferred_element_type=F32)


def key_parts(lo):
    if lo < PROMPT:
        return ([(0, lo, False)] if lo else []) + [(lo, lo + BQ, True)]
    return [(0, PROMPT, False), (PROMPT, lo + BQ, True)]


def part_scores(keys, query_block, lo, part, start_row):
    first, last, masked = part
    product = dot_nt(keys[first:last], query_block)
    if masked:
        key_pos = first + lax.broadcasted_iota(jnp.int32, product.shape, 0)
        query_pos = lo + lax.broadcasted_iota(jnp.int32, product.shape, 1)
        seen = (key_pos <= query_pos) & (key_pos >= start_row)
        product = jnp.where(seen, product, -1e30)
    return product


def softmax_parts(scores):
    top = scores[0].max(axis=0, keepdims=True)
    for piece in scores[1:]:
        top = jnp.maximum(top, piece.max(axis=0, keepdims=True))
    weights = [jnp.exp2((piece - top) * (SCALE * LOG2E)) for piece in scores]
    total = weights[0].sum(axis=0, keepdims=True)
    for piece in weights[1:]:
        total = total + piece.sum(axis=0, keepdims=True)
    return top, weights, total


def attend_kernel(start_ref, qkv_ref, out_ref, peak_ref):
    keys = qkv_ref[:, HD : 2 * HD]
    values_t = qkv_ref[:, 2 * HD :].T
    peak = jnp.full((1, BQ), -1e30, F32)
    for lo in range(0, SEQ, BQ):
        query_block = qkv_ref[lo : lo + BQ, :HD]
        start_row = start_ref[:, lo : lo + BQ]
        parts = key_parts(lo)
        scores = [part_scores(keys, query_block, lo, part, start_row) for part in parts]
        top, weights, total = softmax_parts(scores)
        peak = jnp.maximum(peak, top)
        mixed = None
        for (first, last, _), piece in zip(parts, weights):
            term = dot_nn(values_t[:, first:last], piece.astype(BF))
            mixed = term if mixed is None else mixed + term
        out_ref[lo : lo + BQ, :] = (mixed * (1.0 / total)).T.astype(BF)
    peak_ref[...] = jnp.broadcast_to(peak.max(axis=1, keepdims=True) * SCALE, peak_ref.shape)


def attend(start_rows, qkv):
    heads = qkv.shape[1] // (3 * HD)
    return pl.pallas_call(
        attend_kernel,
        grid=(heads,),
        in_specs=[
            pl.BlockSpec((1, SEQ), lambda h: (0, 0)),
            pl.BlockSpec((SEQ, 3 * HD), lambda h: (0, h)),
        ],
        out_specs=[
            pl.BlockSpec((SEQ, HD), lambda h: (0, h)),
            pl.BlockSpec((1, 8, HD), lambda h: (h, 0, 0)),
        ],
        out_shape=[
            jax.ShapeDtypeStruct((SEQ, heads * HD), BF),
            jax.ShapeDtypeStruct((heads, 8, HD), F32),
        ],
        compiler_params=pltpu.CompilerParams(vmem_limit_bytes=VMEM_CAP),
        cost_estimate=cost(heads * 5e-6),
        name="attend",
    )(start_rows, qkv)


def attend_back_kernel(start_ref, qkv_ref, back_ref, out_ref, key_acc, value_acc):
    keys = qkv_ref[:, HD : 2 * HD]
    values = qkv_ref[:, 2 * HD :]
    keys_t = keys.T
    key_acc[...] = jnp.zeros_like(key_acc)
    value_acc[...] = jnp.zeros_like(value_acc)
    for lo in range(0, SEQ, BQ):
        query_block = qkv_ref[lo : lo + BQ, :HD]
        back_block = back_ref[lo : lo + BQ, :]
        start_row = start_ref[:, lo : lo + BQ]
        parts = key_parts(lo)
        scores = [part_scores(keys, query_block, lo, part, start_row) for part in parts]
        top, weights, total = softmax_parts(scores)
        inverse = 1.0 / total
        probs = [piece * inverse for piece in weights]
        grads = [dot_nt(values[first:last], back_block) for first, last, _ in parts]
        mean = None
        for piece, grad in zip(probs, grads):
            term = (piece * grad).sum(axis=0, keepdims=True)
            mean = term if mean is None else mean + term
        query_t = None
        for (first, last, _), piece, grad in zip(parts, probs, grads):
            low = (piece * ((grad - mean) * SCALE)).astype(BF)
            value_acc[first:last, :] += dot_nn(piece.astype(BF), back_block)
            key_acc[first:last, :] += dot_nn(low, query_block)
            term = dot_nn(keys_t[:, first:last], low)
            query_t = term if query_t is None else query_t + term
        out_ref[lo : lo + BQ, :HD] = query_t.T.astype(BF)
    out_ref[:, HD : 2 * HD] = key_acc[...].astype(BF)
    out_ref[:, 2 * HD :] = value_acc[...].astype(BF)


def attend_back(start_rows, qkv, back):
    heads = qkv.shape[1] // (3 * HD)
    return pl.pallas_call(
        attend_back_kernel,
        grid=(heads,),
        in_specs=[
            pl.BlockSpec((1, SEQ), lambda h: (0, 0)),
            pl.BlockSpec((SEQ, 3 * HD), lambda h: (0, h)),
            pl.BlockSpec((SEQ, HD), lambda h: (0, h)),
        ],
        out_specs=pl.BlockSpec((SEQ, 3 * HD), lambda h: (0, h)),
        out_shape=jax.ShapeDtypeStruct(qkv.shape, BF),
        scratch_shapes=[pltpu.VMEM((SEQ, HD), F32), pltpu.VMEM((SEQ, HD), F32)],
        compiler_params=pltpu.CompilerParams(vmem_limit_bytes=VMEM_CAP),
        cost_estimate=cost(heads * 10e-6),
        name="attend_back",
    )(start_rows, qkv, back)


TILE_GROUP = 8


def orthonormal_all(matrices):
    currents = []
    for matrix in matrices:
        frob = jnp.sqrt(jnp.sum(matrix * matrix, axis=(0, 1), keepdims=True))
        currents.append(matrix * (1.0 / (frob + 1e-06)))
    for _ in range(NS_ITERS):
        lows = [current.astype(BF) for current in currents]
        grams = [dot_nt(low, low).astype(BF) for low in lows]
        terms = [dot_nn(gram, low) for gram, low in zip(grams, lows)]
        currents = [1.5 * current - 0.5 * term for current, term in zip(currents, terms)]
    return currents


def update_kernel(tile_group, turned_grad, token_count, *refs):
    rate_ref, factor_ref, grad_ref = refs[:3]
    master_ref, first_ref, second_ref, left_stat_ref, right_stat_ref, left_ref, right_ref = refs[3:10]
    outs = refs[-8:]
    first_out, second_out, master_out, weight_out, left_stat_out, right_stat_out, left_out, right_out = outs
    base = pl.program_id(0) * tile_group
    group = range(tile_group)
    grads = [grad_ref[i] for i in group]
    lefts = [left_ref[i].astype(BF) for i in group]
    rights = [right_ref[i].astype(BF) for i in group]
    if turned_grad:
        outer_rows = [dot_tn(grad, grad) for grad in grads]
        outer_cols = [dot_nt(grad, grad) for grad in grads]
        halves = [dot_nn(grad, left).astype(BF) for grad, left in zip(grads, lefts)]
        rotated = [dot_tn(half, right) for half, right in zip(halves, rights)]
    else:
        outer_rows = [dot_nt(grad, grad) for grad in grads]
        outer_cols = [dot_tn(grad, grad) for grad in grads]
        halves = [dot_nn(grad, right).astype(BF) for grad, right in zip(grads, rights)]
        rotated = [dot_tn(left, half) for left, half in zip(lefts, halves)]
    directions = []
    for i in group:
        new_first = 0.5 * first_ref[i] + 0.5 * rotated[i]
        new_second = 0.5 * second_ref[i] + 0.5 * rotated[i] * rotated[i]
        first_out[i] = new_first
        second_out[i] = new_second
        direction = (
            new_first
            * (1.0 / (1.0 - 0.5**STEP))
            / (jnp.sqrt(new_second * (1.0 / (1.0 - 0.5**STEP))) + 1e-08)
        )
        directions.append(direction.astype(BF))
    turned = [dot_nn(left, direction).astype(BF) for left, direction in zip(lefts, directions)]
    turned = [dot_nt(half, right) for half, right in zip(turned, rights)]
    for i in group:
        master = master_ref[i]
        new_master = (master - rate_ref[base + i] * (turned[i] + 0.1 * master)) * factor_ref[base + i]
        master_out[i] = new_master
        weight_out[i] = new_master.astype(BF)
    moved = []
    for stat_ref, stat_out, outers, bases in (
        (left_stat_ref, left_stat_out, outer_rows, lefts),
        (right_stat_ref, right_stat_out, outer_cols, rights),
    ):
        for i in group:
            new_stat = 0.5 * stat_ref[i] + (0.5 / (HD * token_count)) * outers[i]
            stat_out[i] = new_stat
            moved.append(dot_nn(new_stat.astype(BF), bases[i]))
    moved = orthonormal_all(moved)
    for i in group:
        left_out[i] = moved[i]
        right_out[i] = moved[tile_group + i]


def update_tiles(grads, state, rates, factors, first_tile, earlier, turned_grad, token_count):
    count = grads.shape[0]
    tiles = state[0].shape[0]
    group = math.gcd(math.gcd(count, first_tile), TILE_GROUP)
    offset = first_tile // group
    block = (group, HD, HD)
    here = pl.BlockSpec(block, lambda i: (i + offset, 0, 0))
    smem = pl.BlockSpec(memory_space=pltpu.SMEM)
    kinds = [F32, F32, F32, BF, F32, F32, F32, F32]
    earlier = list(earlier) if earlier is not None else []

    def body(*refs):
        update_kernel(group, turned_grad, token_count, *refs)

    return pl.pallas_call(
        body,
        grid=(count // group,),
        in_specs=[smem, smem, pl.BlockSpec(block, lambda i: (i, 0, 0))]
        + [here] * 7
        + [pl.BlockSpec(memory_space=pl.ANY)] * len(earlier),
        out_specs=[here] * 8,
        out_shape=[jax.ShapeDtypeStruct((tiles, HD, HD), kind) for kind in kinds],
        input_output_aliases={10 + i: i for i in range(len(earlier))},
        compiler_params=pltpu.CompilerParams(vmem_limit_bytes=VMEM_CAP),
        cost_estimate=cost(count * 5e-7),
        name="update_tiles",
    )(rates[first_tile : first_tile + count], factors[first_tile : first_tile + count], grads, *state, *earlier)


def grad_kernel(chunks, parts, block_ref, *refs):
    lefts, rights, out_ref = refs[:chunks], refs[chunks:-1], refs[-1]
    turned = [left[...].T for left in lefts]
    lo = 0
    for j in range(parts):
        mine = rights[j * chunks : (j + 1) * chunks]
        width = mine[0].shape[1]
        step = min(512, width)
        for at in range(0, width, step):
            total = dot_nn(turned[0], mine[0][:, at : at + step])
            for left, right in zip(turned[1:], mine[1:]):
                total = total + dot_nn(left, right[:, at : at + step])
            out_ref[0, :, lo + at : lo + at + step] = total.astype(BF)
        lo += width


def grad_blocks(blocks, lefts, rights, edge):
    count = blocks.shape[0]
    rows = sum(left.shape[0] for left in lefts)
    width = sum(right[0].shape[1] for right in rights)
    flat = [chunk for right in rights for chunk in right]

    def body(*refs):
        grad_kernel(len(lefts), len(rights), *refs)

    return pl.pallas_call(
        body,
        grid_spec=pltpu.PrefetchScalarGridSpec(
            num_scalar_prefetch=1,
            grid=(count,),
            in_specs=[pl.BlockSpec((left.shape[0], edge), lambda i, blocks: (0, blocks[i])) for left in lefts]
            + [pl.BlockSpec(chunk.shape, lambda i, blocks: (0, 0)) for chunk in flat],
            out_specs=pl.BlockSpec((1, edge, width), lambda i, blocks: (i, 0, 0)),
        ),
        out_shape=jax.ShapeDtypeStruct((count, edge, width), BF),
        compiler_params=pltpu.CompilerParams(vmem_limit_bytes=VMEM_CAP),
        cost_estimate=cost(2 * count * edge * width * rows / 8e14),
        name="grad_blocks",
    )(blocks, *lefts, *flat)


def matmul_kernel(terms, *refs):
    lefts, rights, outs = refs[:terms], refs[terms : 2 * terms], refs[2 * terms :]
    total = dot_nt(lefts[0][...], rights[0][...])
    for left, right in zip(lefts[1:], rights[1:]):
        total = total + dot_nt(left[...], right[...])
    rows = outs[0].shape[0]
    outs[0][...] = total[:rows].astype(BF)
    outs[1][...] = total[rows:].astype(BF)


def matmul_sum(lefts, rights, seconds):
    terms = len(lefts)
    rows, depth = lefts[0].shape
    columns = rights[0].shape[0]
    step = min(512, columns)

    def body(*refs):
        matmul_kernel(terms, *refs)

    return pl.pallas_call(
        body,
        grid=(columns // step,),
        in_specs=[pl.BlockSpec((rows, depth), lambda n: (0, 0))] * terms
        + [pl.BlockSpec((step, depth), lambda n: (n, 0))] * terms,
        out_specs=[pl.BlockSpec((rows // 2, step), lambda n: (0, n))] * 2,
        out_shape=[jax.ShapeDtypeStruct((rows // 2, columns), BF)] * 2,
        compiler_params=pltpu.CompilerParams(vmem_limit_bytes=VMEM_CAP),
        cost_estimate=cost(seconds),
        name="matmul_sum",
    )(*lefts, *rights)


def pack_kernel(heads, edge_tiles, hidden_tiles, core_ref, tiles_ref, halves_ref, qkv_ref, out_ref):
    core = core_ref[0]
    half = hidden_tiles // 2 * HD
    first = 0
    for row in range(edge_tiles):
        for part in range(3):
            for head in range(heads):
                tile = tiles_ref[first + (row * 3 + part) * heads + head].astype(BF)
                at = (head * 3 + part) * HD
                qkv_ref[row * HD : (row + 1) * HD, at : at + HD] = tile
    first += edge_tiles * 3 * heads
    for head in range(heads):
        for row in range(edge_tiles):
            tile = tiles_ref[first + head * edge_tiles + row].T.astype(BF)
            out_ref[row * HD : (row + 1) * HD, head * HD : (head + 1) * HD] = tile
    first += heads * edge_tiles
    for kind in range(2):
        for row in range(edge_tiles):
            for column in range(hidden_tiles):
                part, inner = divmod(column, hidden_tiles // 2)
                at = kind * half + inner * HD
                if kind == 0:
                    tile = tiles_ref[first + row * hidden_tiles + column].astype(BF)
                else:
                    tile = tiles_ref[first + column * edge_tiles + row].T.astype(BF)
                halves_ref[part ^ core, row * HD : (row + 1) * HD, at : at + HD] = tile
        first += edge_tiles * hidden_tiles


def pack_weights(tiles, core, heads, edge_tiles, hidden_tiles):
    edge = edge_tiles * HD

    def body(*refs):
        pack_kernel(heads, edge_tiles, hidden_tiles, *refs)

    shapes = [(2, edge, hidden_tiles * HD), (edge, 3 * heads * HD), (edge, heads * HD)]
    return pl.pallas_call(
        body,
        grid_spec=pltpu.PrefetchScalarGridSpec(
            num_scalar_prefetch=1,
            grid=(1,),
            in_specs=[pl.BlockSpec(tiles.shape, lambda i, core: (0, 0, 0))],
            out_specs=[pl.BlockSpec(shapes[0], lambda i, core: (0, 0, 0))]
            + [pl.BlockSpec(shape, lambda i, core: (0, 0)) for shape in shapes[1:]],
        ),
        out_shape=[jax.ShapeDtypeStruct(shape, BF) for shape in shapes],
        compiler_params=pltpu.CompilerParams(vmem_limit_bytes=VMEM_CAP),
        cost_estimate=cost(5e-6),
        name="pack_weights",
    )(core[None], tiles)


def scatter_kernel(tables, *refs):
    source_ref, outs = refs[tables], refs[tables + 1 :]
    lo = 0
    for out in outs:
        width = out.shape[1]
        out[...] = source_ref[0, :, lo : lo + width]
        lo += width


def scatter_blocks(tables, source):
    count, edge, columns = source.shape
    parts = len(tables)
    width = columns // parts

    def body(*refs):
        scatter_kernel(parts, *refs)

    def out_spec(k):
        return pl.BlockSpec((edge, width), lambda i, *tables: (tables[k][i], 0))

    return pl.pallas_call(
        body,
        grid_spec=pltpu.PrefetchScalarGridSpec(
            num_scalar_prefetch=parts,
            grid=(count,),
            in_specs=[pl.BlockSpec((1, edge, columns), lambda i, *tables: (i, 0, 0))],
            out_specs=[out_spec(k) for k in range(parts)],
        ),
        out_shape=[jax.ShapeDtypeStruct((count * edge, width), BF)] * parts,
        compiler_params=pltpu.CompilerParams(vmem_limit_bytes=VMEM_CAP),
        cost_estimate=cost(4 * count * edge * columns / 3e12),
        name="scatter_blocks",
    )(*tables, source)


def project_kernel(sources, *refs):
    pick_ref = refs[0]
    pieces = refs[2 : 2 + sources]
    gain_ref, shift_ref, weight_ref, bias_ref = refs[2 + sources : 6 + sources]
    normal_out, normed_out, out_ref = refs[-3:]
    picked = pick_ref[pl.program_id(0)]
    for i in range(sources):

        @pl.when(picked == i)
        def _():
            normal_out[...] = pieces[i][...]

    normed = (normal_out[...].astype(F32) * gain_ref[...] + shift_ref[...]).astype(BF)
    normed_out[...] = normed
    out_ref[...] = (dot_nn(normed, weight_ref[...]) + bias_ref[...]).astype(BF)


def project(pick, place, total, pieces, gain, shift_by, weight, bias, into=()):
    count = pick.shape[0]
    rows, depth = pieces[0].shape
    columns = weight.shape[1]

    def body(*refs):
        project_kernel(len(pieces), *refs)

    def held(shape):
        return pl.BlockSpec(shape, lambda i, pick, place: (0, 0), pipeline_mode=pl.Buffered(1))

    def block(width):
        return pl.BlockSpec((rows, width), lambda i, pick, place: (place[i], 0))

    return pl.pallas_call(
        body,
        grid_spec=pltpu.PrefetchScalarGridSpec(
            num_scalar_prefetch=2,
            grid=(count,),
            in_specs=[held((rows, depth)) for _ in pieces]
            + [held((1, depth)), held((1, depth)), held((depth, columns)), held((1, columns))]
            + [pl.BlockSpec(memory_space=pl.ANY) for _ in into],
            out_specs=[block(depth), block(depth), block(columns)],
        ),
        out_shape=[jax.ShapeDtypeStruct((total * rows, width), BF) for width in (depth, depth, columns)],
        input_output_aliases={2 + len(pieces) + 4 + k: k for k in range(len(into))},
        compiler_params=pltpu.CompilerParams(vmem_limit_bytes=VMEM_CAP),
        cost_estimate=cost(count * 6e-6),
        name="project",
    )(pick, place, *pieces, gain[None], shift_by[None], weight, bias[None], *into)


def sync(*values):
    return lax.optimization_barrier(values)


def shift(value, axis, mask):
    return lax.ppermute(value, axis, [(i, i ^ mask) for i in range(lax.axis_size(axis))])


def move(value, axis, pairs):
    return lax.ppermute(value, axis, pairs)


def beside(value, axis, mask, steps, state):
    total, rows = sum(share for share, _ in steps), value.shape[0]
    pieces, done, first = [], 0, 0
    for share, work in steps:
        done += share
        last = rows // 16 * done // total * 16
        pieces.append(shift(value[first:last], axis, mask))
        first = last
        state = work(state)
        state, pieces, value = sync(state, pieces, value)
    return jnp.concatenate(pieces, axis=0), state


def add_low(left, right):
    return (left.astype(F32) + right.astype(F32)).astype(BF)


def join_halves(mine, other):
    first = (lax.axis_index("dp") & 1) == 0
    return jnp.concatenate([jnp.where(first, mine, other), jnp.where(first, other, mine)], axis=-1)


def halving_order(chips, masks):
    return sorted(chips, key=lambda q: tuple(-(q & (mask >> 1)) for mask in masks))


def halve(blocks, masks):
    for mask in masks:
        count = blocks.shape[0] // 2
        blocks = add_low(blocks[count:], shift(blocks[:count], "dp", mask))
    return blocks


def layer_norm(token_rows, gain, shift_by):
    centre = jnp.mean(token_rows, axis=-1, keepdims=True)
    centred = token_rows - centre
    spread = jnp.mean(centred * centred, axis=-1, keepdims=True)
    return centred * lax.rsqrt(spread + 1e-05) * gain + shift_by


def layer_norm_back(token_rows, gain, grad):
    centre = jnp.mean(token_rows, axis=-1, keepdims=True)
    centred = token_rows - centre
    inverse = lax.rsqrt(jnp.mean(centred * centred, axis=-1, keepdims=True) + 1e-05)
    normal = centred * inverse
    scaled = grad * gain
    back = (
        scaled - jnp.mean(scaled, axis=-1, keepdims=True) - normal * jnp.mean(scaled * normal, axis=-1, keepdims=True)
    ) * inverse
    return back, jnp.sum(grad * normal, axis=0), jnp.sum(grad, axis=0)


def gelu_pair(pre_act):
    cdf = 0.5 * (1.0 + lax.erf(pre_act * (0.5**0.5)))
    density = jnp.exp(-0.5 * pre_act * pre_act) * 0.3989422804014327
    return pre_act * cdf, cdf + pre_act * density


def axis_sum(value, axis):
    for bit in range(lax.axis_size(axis).bit_length() - 1):
        value = value + shift(value, axis, 1 << bit)
    return value


def small_step(summed, params, first, second):
    new_first = 0.5 * first + 0.5 * summed
    new_second = 0.5 * second + 0.5 * summed * summed
    direction = new_first / (1.0 - 0.5**STEP) / (jnp.sqrt(new_second / (1.0 - 0.5**STEP)) + 1e-08)
    return new_first, new_second, params - 0.1 * direction


def per_device(
    inputs,
    cotangent,
    lengths,
    held_blocks,
    master,
    first_moment,
    second_moment,
    left_stats,
    right_stats,
    left_basis,
    right_basis,
    small_params,
    small_first,
    small_second,
):
    dp_count = lax.axis_size("dp")
    tp_count = lax.axis_size("tensor")
    me = lax.axis_index("dp")
    place = lax.axis_index("tensor")
    core = me & 1
    rows = inputs.shape[0]
    edge = D // dp_count
    width = D // tp_count
    hidden = FF // tp_count
    half = hidden // 2
    heads = width // HD
    edge_tiles = edge // HD
    hidden_tiles = hidden // HD
    tile_q = edge_tiles * 3 * heads
    tile_o = heads * edge_tiles
    tile_u = edge_tiles * hidden_tiles
    tile_count = master.shape[2]
    near = [1 << bit for bit in range(1, dp_count.bit_length() - 1)]
    far = near[::-1]
    slices = tp_count // 2
    chips = range(dp_count // 2)
    relative = jnp.arange(dp_count, dtype=jnp.int32) ^ me
    block_of = jnp.take(held_blocks, relative, axis=1)

    bias_q = lax.dynamic_slice_in_dim(small_params, place * width, width)
    bias_v = lax.dynamic_slice_in_dim(small_params, D + place * width, width)
    bias_o = small_params[2 * D : 3 * D]
    bias_two = small_params[3 * D : 4 * D]
    gain_one = small_params[4 * D : 5 * D]
    shift_one = small_params[5 * D : 6 * D]
    gain_two = small_params[6 * D : 7 * D]
    shift_two = small_params[7 * D : 8 * D]
    hidden_starts = [(place ^ (2 * j)) * hidden + core * half for j in range(slices)]
    bias_up = jnp.concatenate(
        [lax.dynamic_slice_in_dim(small_params, 8 * D + start, half) for start in hidden_starts]
    )

    token_rows = inputs.astype(F32)
    centred = token_rows - jnp.mean(token_rows, axis=-1, keepdims=True)
    spread = jnp.mean(centred * centred, axis=-1, keepdims=True)
    normal = (centred * lax.rsqrt(spread + 1e-05)).astype(BF)
    ups = [(i, i + 1) for i in range(tp_count - 1)]
    downs = [(i + 1, i) for i in range(tp_count - 1)]
    above, below = [move(normal, "tensor", downs)], [move(normal, "tensor", ups)]

    bounds = [0, tile_q, tile_q + tile_o, tile_q + tile_o + tile_u, tile_count]
    halves, own_qkv, own_out = pack_weights(master[0, 0], core, heads, edge_tiles, hidden_tiles)
    pair = jnp.stack([halves[0], shift(halves[1], "dp", 1)])
    same_core = [list(range(at, dp_count, 2)) for at in range(2)]
    pair_slots = jnp.arange(dp_count, dtype=jnp.int32) ^ core

    def gather_ffn(value):
        return lax.all_gather(value, "dp", axis=0, tiled=True, axis_index_groups=same_core)

    def scatter_ffn(value):
        return scatter_blocks([held_blocks[2][pair_slots], held_blocks[3][pair_slots]], value)

    def gather_all(kind, value):
        value = lax.all_gather(value, "dp", axis=0, tiled=False)
        return scatter_blocks([held_blocks[kind]], value)[0]

    def crossed(mask, odd):
        return [(i, i ^ mask) for i in range(tp_count) if ((i ^ (i >> 1)) & 1) == odd]

    w_qkv = gather_all(0, own_qkv)
    bias_mixed = jnp.stack(
        [bias_q.reshape(heads, HD), jnp.zeros((heads, HD), F32), bias_v.reshape(heads, HD)], axis=1
    ).reshape(3 * width)
    distance = jnp.arange(tp_count, dtype=jnp.int32) - place
    by_distance = jnp.argsort(jnp.abs(distance)).astype(jnp.int32)
    offset = by_distance - place
    outs = [shift(own_out, "tensor", j) for j in range(1, tp_count)]
    far_first, first_raw, out_raw = [], None, None
    for step in range(1, tp_count):
        if step > 1:
            below.append(move(below[-1], "tensor", ups[step - 1 :]))
            above.append(move(above[-1], "tensor", downs[: tp_count - step]))
        if step == tp_count - 1:
            first_raw = gather_ffn(pair)
            far_first = [move(pair, "tensor", crossed(2 * j, 0)) for j in range(1, slices)]
            w_out = scatter_blocks([held_blocks[1]], out_raw)[0]
            pick = jnp.where(offset < 0, -offset, jnp.where(offset > 0, tp_count - 2 + offset, 0))
            sources = [normal] + below[:-1] + above[:-1]
            projected = project(
                pick[:-1], by_distance[:-1], tp_count, sources, gain_one, shift_one, w_qkv, bias_mixed
            )
            above, below, far_first, pair, w_qkv, w_out, projected = sync(
                above, below, far_first, pair, w_qkv, w_out, projected
            )
        elif step == 1:
            above, below, outs, own_out, pair = sync(above, below, outs, own_out, pair)
            out_raw = lax.all_gather(jnp.concatenate([own_out] + outs, axis=1), "dp", axis=0, tiled=False)
        else:
            above, below, pair = sync(above, below, pair)

    reach = tp_count // 2
    pick = jnp.where(offset < 0, -offset - reach, tp_count - 1 + offset - 2 * reach + 1)
    sources = below[reach - 1 :] + above[reach - 1 :]
    normal_all, normed_all, qkv = project(
        pick[-1:], by_distance[-1:], tp_count, sources, gain_one, shift_one, w_qkv, bias_mixed, projected
    )
    far_second = [move(pair, "tensor", crossed(2 * j, 1)) for j in range(1, slices)]

    ends = jnp.cumsum(lengths[0])
    spot = jnp.arange(SEQ, dtype=jnp.int32) - PROMPT
    started = jnp.max(jnp.where(ends[None, :] <= spot[:, None], ends[None, :], 0), axis=1)
    start_rows = jnp.where(spot < 0, 0, PROMPT + started).astype(jnp.int32)[None]
    attended, peaks = attend(start_rows, qkv)
    others = range(1, slices)
    peak_row = lax.dynamic_update_slice(
        jnp.zeros((dp_count * H,), F32), peaks[:, 0, 0], (me * H + place * heads,)
    )
    attended, far_second = sync(attended, far_second)

    def rows_of(value, j):
        return lax.dynamic_slice_in_dim(value, (place ^ j) * rows, rows, 0)

    def with_core(value):
        return jnp.concatenate([value, shift(value, "dp", 1)], axis=0)

    attended_rows = jnp.concatenate(
        [rows_of(attended, 0)] + [shift(rows_of(attended, j), "tensor", j) for j in range(1, tp_count)], axis=1
    )
    far_raw = [gather_ffn(left + right) for left, right in zip(far_first, far_second)]
    w_first = scatter_ffn(first_raw)
    back_near = with_core(cotangent)
    peak_rows = axis_sum(peak_row, "dp")
    attended_rows, w_first, cotangent, back_near, w_out, peak_rows = sync(
        attended_rows, w_first, cotangent, back_near, w_out, peak_rows
    )
    hidden_rows = token_rows + dot_nt(attended_rows, w_out) + bias_o
    normed_two = layer_norm(hidden_rows, gain_two, shift_two).astype(BF)

    w_up, w_down = [w_first[0]], [w_first[1]]
    biases = [bias_up[j * half : (j + 1) * half] for j in range(slices)]

    def core_rows(partial):
        return add_low(partial[0], shift(partial[1], "dp", 1))

    def chips_sum(blocks):
        blocks = blocks.reshape(dp_count // 2, 2, edge, blocks.shape[2])
        return lax.psum_scatter(blocks, "dp", scatter_dimension=0, tiled=False, axis_index_groups=same_core)

    def near_back(j):
        def work(state):
            if j > 0:
                up, down = state.pop("arrived")
                w_up.append(up)
                w_down.append(down)
            grad_act = jnp.dot(state["back_near"], w_down[j], preferred_element_type=F32).astype(BF)
            state = dict(state, grad_act=grad_act)
            if j == 0:
                state["normed_near"] = with_core(state.pop("normed"))
            return state

        return work

    def near_up(j):
        def work(state):
            pre_act = jnp.dot(state["normed_near"], w_up[j], preferred_element_type=F32) + biases[j]
            activation, slope = gelu_pair(pre_act)
            low = (state["grad_act"].astype(F32) * slope).astype(BF)
            if j + 1 < slices:
                state = dict(state, far_raw=far_raw[j])
            return dict(state, act_near=state["act_near"] + [activation.astype(BF)], pre_near=state["pre_near"] + [low])

        return work

    def far_up(j):
        def work(state):
            pre_act = jnp.dot(state["normed_far"], w_up[j], preferred_element_type=F32) + biases[j]
            activation, slope = gelu_pair(pre_act)
            return dict(state, act_far=state["act_far"] + [activation.astype(BF)], slopes=state["slopes"] + [slope.astype(BF)])

        return work

    def far_result(state):
        return dict(state, result_far=matmul_sum(state["act_far"], w_down, 1e-5))

    def near_grad(state):
        return dict(
            state, grad_near=matmul_sum(state["pre_near"], w_up, 1e-5), ffn_far=core_rows(state.pop("result_far"))
        )

    def down_blocks(state):
        rights = [list(pair) for pair in zip(state["act_near"], state["act_far"])]
        blocks = grad_blocks(held_blocks[3][pair_slots], [state["back_near"], state["back_far"]], rights, edge)
        return dict(state, down=blocks)

    def far_back(j):
        def work(state):
            grad_act = jnp.dot(state["back_far"], w_down[j], preferred_element_type=F32)
            low = (grad_act * state["slopes"][j].astype(F32)).astype(BF)
            return dict(state, pre_far=state["pre_far"] + [low])

        return work

    def far_grad(state):
        return dict(state, grad_far=matmul_sum(state["pre_far"], w_up, 2e-6))

    def up_blocks(state):
        rights = [list(pair) for pair in zip(state["pre_near"], state["pre_far"])]
        blocks = grad_blocks(held_blocks[2][pair_slots], [state["normed_near"], state["normed_far"]], rights, edge)
        return dict(state, up=blocks)

    def near_result(state):
        return dict(
            state, result_near=matmul_sum(state["act_near"], w_down, 1e-5), near_rows=core_rows(state.pop("grad_near"))
        )

    def both(first, second):
        return lambda state: second(first(state))

    state = dict(
        back_near=back_near, normed=normed_two, act_near=[], pre_near=[], act_far=[], pre_far=[], slopes=[]
    )
    def arrive(state):
        state = dict(state)
        state["arrived"] = scatter_ffn(state.pop("far_raw"))
        return state

    steps = []
    for j in range(slices):
        steps += [(1, arrive)] * (j > 0) + [(2, both(near_back(j), near_up(j)))]
    normed_across, state = beside(normed_two, "tensor", 1, steps, state)
    state["normed_across"] = normed_across

    def far_rows_in(state):
        state = dict(state)
        state["normed_far"] = with_core(state.pop("normed_across"))
        return state

    def back_rows_in(state):
        state = dict(state)
        state["back_far"] = with_core(state.pop("back_across"))
        return state

    work = both(far_rows_in, far_up(0))
    for j in range(1, slices):
        work = both(work, far_up(j))
    steps = [(slices, work)]
    steps += [(slices, far_result), (slices, near_grad)]
    back_across, state = beside(cotangent, "tensor", 1, steps, state)
    state["back_across"] = back_across
    middle = rows // 2
    ffn_low, state = beside(state["ffn_far"][:middle], "tensor", 1, [(1, both(back_rows_in, down_blocks))], state)
    part_down = chips_sum(state.pop("down"))
    work = far_back(0)
    for j in range(1, slices):
        work = both(work, far_back(j))
    steps = [(1, both(work, far_grad))]
    ffn_high, state = beside(state.pop("ffn_far")[middle:], "tensor", 1, steps, state)
    ffn_across = jnp.concatenate([ffn_low, ffn_high], axis=0)
    far_rows = core_rows(state.pop("grad_far"))
    state["far_rows"] = far_rows
    state = sync(state)[0]
    cut = rows // 16 * 5 // 8 * 16
    low_rows, state = beside(state["far_rows"][:cut], "tensor", 1, [(1, up_blocks)], state)
    part_up = chips_sum(state.pop("up"))
    high_rows, state = beside(state.pop("far_rows")[cut:], "tensor", 1, [(1, near_result)], state)
    low_rows, high_rows, part_down, state, peak_rows = sync(low_rows, high_rows, part_down, state, peak_rows)
    grad_two = state["near_rows"].astype(F32) + jnp.concatenate([low_rows, high_rows], axis=0).astype(F32)
    result, grads_pre = state["result_near"], list(zip(state["pre_near"], state["pre_far"]))

    def far_slices(part):
        return part[:, :, :half], [part[:, :, j * half : (j + 1) * half] for j in others]

    def to_owners(values):
        return [shift(value, "tensor", 2 * j) for j, value in zip(others, values)]

    order_far = halving_order(chips, far)

    def half_slots(order):
        return jnp.array([2 * q + 1 for q in order] + [2 * q for q in order], jnp.int32)

    own_down, far_down = far_slices(part_down)
    down_low = to_owners([value[:1] for value in far_down])
    grad_part, grad_gain_two, grad_shift_two = layer_norm_back(hidden_rows, gain_two, grad_two)
    grad_hidden = cotangent.astype(F32) + grad_part
    branch = grad_hidden.astype(BF)
    even = jnp.arange(0, dp_count, 2, dtype=jnp.int32)
    out_slots = jnp.concatenate([even + 1 - core, even + core])
    grads_out = grad_blocks(held_blocks[1][out_slots], [branch], [[attended_rows]], edge)
    grad_attended_rows = jnp.dot(branch, w_out, preferred_element_type=F32).astype(BF)
    peak_rows = peak_rows + shift(peak_rows, "tensor", 1)
    grad_attended_rows, branch, result, grads_pre, grads_out, down_low, far_down, peak_rows = sync(
        grad_attended_rows, branch, result, grads_pre, grads_out, down_low, far_down, peak_rows
    )

    arrived = [
        grad_attended_rows[:, j * width : (j + 1) * width]
        if j == 0
        else shift(grad_attended_rows[:, j * width : (j + 1) * width], "tensor", j)
        for j in range(tp_count)
    ]
    grad_attended = jnp.zeros((SEQ, width), BF)
    for j in range(tp_count):
        grad_attended = lax.dynamic_update_slice_in_dim(grad_attended, arrived[j], (place ^ j) * rows, 0)
    sum_out = halve(grads_out, [1])
    grad_attended, branch, result, part_up, far_down, grads_pre, sum_out = sync(
        grad_attended, branch, result, part_up, far_down, grads_pre, sum_out
    )

    def far_sum(kept, arrived):
        total = kept.astype(F32)
        for value in arrived:
            total = total + value.astype(F32)
        total = total.astype(BF)
        return join_halves(total[0], shift(total[1], "dp", 1))

    sum_out = lax.psum_scatter(sum_out, "dp", scatter_dimension=0, tiled=False, axis_index_groups=same_core)
    own_up, far_up = far_slices(part_up)
    down_high = to_owners([value[1:] for value in far_down])
    up_low = to_owners([value[:1] for value in far_up])
    grad_qkv_rows = attend_back(start_rows, qkv, grad_attended)
    grad_qkv_rows, down_high, up_low, far_up, branch, grads_pre = sync(
        grad_qkv_rows, down_high, up_low, far_up, branch, grads_pre
    )
    up_high = to_owners([value[1:] for value in far_up])
    partial = dot_nt(grad_qkv_rows, w_qkv).astype(BF)
    partial, up_high, grad_qkv_rows, branch, grads_pre, sum_out, peak_rows = sync(
        partial, up_high, grad_qkv_rows, branch, grads_pre, sum_out, peak_rows
    )
    far_down = [jnp.concatenate(value, axis=0) for value in zip(down_low, down_high)]
    far_up = [jnp.concatenate(value, axis=0) for value in zip(up_low, up_high)]
    grad_normed_one = lax.psum_scatter(partial, "tensor", scatter_dimension=0, tiled=True).astype(F32)

    grads_qkv = grad_blocks(block_of[0][half_slots(order_far)], [normed_all], [[grad_qkv_rows]], edge)
    for bit in range(1, tp_count.bit_length() - 1):
        peak_rows = peak_rows + shift(peak_rows, "tensor", 1 << bit)
    grads_qkv, grad_qkv_rows, branch, grads_pre, partial, peak_rows = sync(
        grads_qkv, grad_qkv_rows, branch, grads_pre, partial, peak_rows
    )
    column_sums = jnp.sum(grad_qkv_rows, axis=0, dtype=F32).reshape(heads, 3, HD)
    head_sums = lambda part: lax.dynamic_update_slice(
        jnp.zeros((D,), F32), column_sums[:, part].reshape(width), (place * width,)
    )
    partial_wide = partial.astype(F32)
    grad_bias_up = jnp.concatenate([sum(jnp.sum(value, axis=0, dtype=F32) for value in pair) for pair in grads_pre])
    wide = jnp.zeros((FF,), F32)
    for j in range(slices):
        wide = lax.dynamic_update_slice(wide, grad_bias_up[j * half : (j + 1) * half], (hidden_starts[j],))
    totals = jnp.concatenate(
        [
            head_sums(0),
            head_sums(2),
            jnp.sum(branch, axis=0, dtype=F32),
            jnp.sum(cotangent, axis=0, dtype=F32),
            jnp.sum(partial_wide * normal_all.astype(F32), axis=0),
            jnp.sum(partial_wide, axis=0),
            grad_gain_two,
            grad_shift_two,
            wide,
        ]
    )
    sum_qkv = halve(grads_qkv, [1])
    totals = axis_sum(totals, "dp")
    totals, sum_qkv = sync(totals, sum_qkv)
    sum_down = far_sum(own_down, far_down)
    sum_up = far_sum(own_up, far_up)

    index = jnp.arange(tile_count, dtype=jnp.int32)
    rates = jnp.where(
        index < bounds[1],
        D ** (-0.5),
        jnp.where(index < bounds[2], (SEQ / (2.0 * D)) ** 0.5, jnp.where(index < bounds[3], D ** (-0.5), FF ** (-0.5))),
    ).astype(F32)
    ones = jnp.ones((tile_count,), F32)
    token_count = float(dp_count * SEQ)
    state = [value[0, 0] for value in (master, first_moment, second_moment, left_stats, right_stats, left_basis, right_basis)]
    tiles_up = sum_up.reshape(edge_tiles, HD, hidden_tiles, HD).transpose(0, 2, 1, 3).reshape(tile_u, HD, HD)
    tiles_down = sum_down.reshape(edge_tiles, HD, hidden_tiles, HD).transpose(2, 0, 1, 3).reshape(tile_u, HD, HD)
    count = sum_qkv.shape[0] // 4
    done = list(update_tiles(tiles_down, state, rates, ones, bounds[3], None, True, token_count))
    low_part = shift(sum_qkv[:count], "dp", far[0])
    low_part, done[3], sum_qkv = sync(low_part, done[3], sum_qkv)
    done = list(update_tiles(tiles_up, state, rates, ones, bounds[2], done, False, token_count))
    high_part = shift(sum_qkv[count : 2 * count], "dp", far[0])
    high_part, done[3], sum_qkv = sync(high_part, done[3], sum_qkv)
    sum_qkv = add_low(sum_qkv[2 * count :], jnp.concatenate([low_part, high_part], axis=0))
    sum_qkv = halve(sum_qkv, far[1:])[0]
    ffn_near = core_rows(result)
    outputs = (hidden_rows + ffn_near.astype(F32) + ffn_across.astype(F32) + bias_two).astype(BF)
    peak_all = jnp.max(peak_rows.reshape(dp_count, H), axis=0)
    grad_normed_one, totals, sum_out = sync(grad_normed_one, totals, sum_out)
    grad_small = axis_sum(totals, "tensor")
    outs = [shift(sum_out[:, j * width : (j + 1) * width], "tensor", j) for j in range(1, tp_count)]
    total_out = sum_out[:, :width].astype(F32)
    for value in outs:
        total_out = total_out + value.astype(F32)
    sum_out = total_out.astype(BF)
    rows_part, _, _ = layer_norm_back(token_rows, gain_one, grad_normed_one)
    input_grad = (grad_hidden + rows_part).astype(BF)

    shrink = jnp.sqrt(1.0 / jnp.maximum(peak_all, 1.0))
    small_first_new, small_second_new, small_new = small_step(grad_small, small_params, small_first, small_second)
    small_new = jnp.concatenate([(small_new[:D].reshape(H, HD) * shrink[:, None]).reshape(D), small_new[D:]])

    column = index % (3 * heads)
    shrink_here = lax.dynamic_slice_in_dim(shrink, place * heads, heads)
    factors = jnp.where((index < bounds[1]) & (column < 2 * heads), shrink_here[column % heads], 1.0)
    tiles_out = sum_out.reshape(edge_tiles, HD, heads, HD).transpose(2, 0, 1, 3).reshape(tile_o, HD, HD)
    tiles_qkv = sum_qkv.reshape(edge_tiles, HD, heads, 3, HD).transpose(0, 3, 2, 1, 4).reshape(tile_q, HD, HD)
    done = update_tiles(tiles_qkv, state, rates, factors, 0, done, False, token_count)
    done = update_tiles(tiles_out, state, rates, ones, bounds[1], done, True, token_count)
    return (
        outputs,
        input_grad,
        *[value[None, None] for value in done],
        small_first_new,
        small_second_new,
        small_new,
    )


def solution(mesh):
    rows = P(("dp", "tensor"), None)
    tiles = P("dp", "tensor", None, None, None)
    return jax.shard_map(
        per_device,
        mesh=mesh,
        in_specs=(rows, rows, P("dp", None), P()) + (tiles,) * 7 + (P(), P(), P()),
        out_specs=(rows, rows) + (tiles,) * 8 + (P(), P(), P()),
        check_vma=False,
    )
```

```python
import math

import jax
import jax.numpy as jnp
from jax import lax
from jax.experimental import pallas as pl
from jax.experimental.pallas import tpu as pltpu
from jax.sharding import PartitionSpec as P

D = 2048
H = 16
HD = 128
FF = 8192
PROMPT = 1024
STEP = 5
NS_ITERS = 3
SEQ = 2048
BQ = 256
BF = jnp.bfloat16
F32 = jnp.float32
SCALE = HD ** (-0.5)
LOG2E = 1.4426950408889634
VMEM_CAP = 56 * 1024 * 1024


def cost(seconds):
    return pl.CostEstimate(flops=0, bytes_accessed=int(seconds * 3.5e12), transcendentals=0)


def dot_nt(a, b):
    return lax.dot_general(a, b, (((1,), (1,)), ((), ())), preferred_element_type=F32)


def dot_tn(a, b):
    return lax.dot_general(a, b, (((0,), (0,)), ((), ())), preferred_element_type=F32)


def dot_nn(a, b):
    return lax.dot_general(a, b, (((1,), (0,)), ((), ())), preferred_element_type=F32)


def key_parts(lo):
    if lo < PROMPT:
        return ([(0, lo, False)] if lo else []) + [(lo, lo + BQ, True)]
    return [(0, PROMPT, False), (PROMPT, lo + BQ, True)]


def part_scores(keys, query_block, lo, part, start_row):
    first, last, masked = part
    product = dot_nt(keys[first:last], query_block)
    if masked:
        key_pos = first + lax.broadcasted_iota(jnp.int32, product.shape, 0)
        query_pos = lo + lax.broadcasted_iota(jnp.int32, product.shape, 1)
        seen = (key_pos <= query_pos) & (key_pos >= start_row)
        product = jnp.where(seen, product, -1e30)
    return product


def softmax_parts(scores):
    top = scores[0].max(axis=0, keepdims=True)
    for piece in scores[1:]:
        top = jnp.maximum(top, piece.max(axis=0, keepdims=True))
    weights = [jnp.exp2((piece - top) * (SCALE * LOG2E)) for piece in scores]
    total = weights[0].sum(axis=0, keepdims=True)
    for piece in weights[1:]:
        total = total + piece.sum(axis=0, keepdims=True)
    return top, weights, total


def attend_kernel(start_ref, qkv_ref, out_ref, peak_ref):
    keys = qkv_ref[:, HD : 2 * HD]
    values_t = qkv_ref[:, 2 * HD :].T
    peak = jnp.full((1, BQ), -1e30, F32)
    for lo in range(0, SEQ, BQ):
        query_block = qkv_ref[lo : lo + BQ, :HD]
        start_row = start_ref[:, lo : lo + BQ]
        parts = key_parts(lo)
        scores = [part_scores(keys, query_block, lo, part, start_row) for part in parts]
        top, weights, total = softmax_parts(scores)
        peak = jnp.maximum(peak, top)
        mixed = None
        for (first, last, _), piece in zip(parts, weights):
            term = dot_nn(values_t[:, first:last], piece.astype(BF))
            mixed = term if mixed is None else mixed + term
        out_ref[lo : lo + BQ, :] = (mixed * (1.0 / total)).T.astype(BF)
    peak_ref[...] = jnp.broadcast_to(peak.max(axis=1, keepdims=True) * SCALE, peak_ref.shape)


def attend(start_rows, qkv):
    heads = qkv.shape[1] // (3 * HD)
    return pl.pallas_call(
        attend_kernel,
        grid=(heads,),
        in_specs=[
            pl.BlockSpec((1, SEQ), lambda h: (0, 0)),
            pl.BlockSpec((SEQ, 3 * HD), lambda h: (0, h)),
        ],
        out_specs=[
            pl.BlockSpec((SEQ, HD), lambda h: (0, h)),
            pl.BlockSpec((1, 8, HD), lambda h: (h, 0, 0)),
        ],
        out_shape=[
            jax.ShapeDtypeStruct((SEQ, heads * HD), BF),
            jax.ShapeDtypeStruct((heads, 8, HD), F32),
        ],
        compiler_params=pltpu.CompilerParams(vmem_limit_bytes=VMEM_CAP),
        cost_estimate=cost(heads * 5e-6),
        name="attend",
    )(start_rows, qkv)


def attend_back_kernel(start_ref, qkv_ref, back_ref, out_ref, key_acc, value_acc):
    keys = qkv_ref[:, HD : 2 * HD]
    values = qkv_ref[:, 2 * HD :]
    keys_t = keys.T
    key_acc[...] = jnp.zeros_like(key_acc)
    value_acc[...] = jnp.zeros_like(value_acc)
    for lo in range(0, SEQ, BQ):
        query_block = qkv_ref[lo : lo + BQ, :HD]
        back_block = back_ref[lo : lo + BQ, :]
        start_row = start_ref[:, lo : lo + BQ]
        parts = key_parts(lo)
        scores = [part_scores(keys, query_block, lo, part, start_row) for part in parts]
        top, weights, total = softmax_parts(scores)
        inverse = 1.0 / total
        probs = [piece * inverse for piece in weights]
        grads = [dot_nt(values[first:last], back_block) for first, last, _ in parts]
        mean = None
        for piece, grad in zip(probs, grads):
            term = (piece * grad).sum(axis=0, keepdims=True)
            mean = term if mean is None else mean + term
        query_t = None
        for (first, last, _), piece, grad in zip(parts, probs, grads):
            low = (piece * ((grad - mean) * SCALE)).astype(BF)
            value_acc[first:last, :] += dot_nn(piece.astype(BF), back_block)
            key_acc[first:last, :] += dot_nn(low, query_block)
            term = dot_nn(keys_t[:, first:last], low)
            query_t = term if query_t is None else query_t + term
        out_ref[lo : lo + BQ, :HD] = query_t.T.astype(BF)
    out_ref[:, HD : 2 * HD] = key_acc[...].astype(BF)
    out_ref[:, 2 * HD :] = value_acc[...].astype(BF)


def attend_back(start_rows, qkv, back):
    heads = qkv.shape[1] // (3 * HD)
    return pl.pallas_call(
        attend_back_kernel,
        grid=(heads,),
        in_specs=[
            pl.BlockSpec((1, SEQ), lambda h: (0, 0)),
            pl.BlockSpec((SEQ, 3 * HD), lambda h: (0, h)),
            pl.BlockSpec((SEQ, HD), lambda h: (0, h)),
        ],
        out_specs=pl.BlockSpec((SEQ, 3 * HD), lambda h: (0, h)),
        out_shape=jax.ShapeDtypeStruct(qkv.shape, BF),
        scratch_shapes=[pltpu.VMEM((SEQ, HD), F32), pltpu.VMEM((SEQ, HD), F32)],
        compiler_params=pltpu.CompilerParams(vmem_limit_bytes=VMEM_CAP),
        cost_estimate=cost(heads * 10e-6),
        name="attend_back",
    )(start_rows, qkv, back)


TILE_GROUP = 8


def orthonormal_all(matrices):
    currents = []
    for matrix in matrices:
        frob = jnp.sqrt(jnp.sum(matrix * matrix, axis=(0, 1), keepdims=True))
        currents.append(matrix * (1.0 / (frob + 1e-06)))
    for _ in range(NS_ITERS):
        lows = [current.astype(BF) for current in currents]
        grams = [dot_nt(low, low).astype(BF) for low in lows]
        terms = [dot_nn(gram, low) for gram, low in zip(grams, lows)]
        currents = [1.5 * current - 0.5 * term for current, term in zip(currents, terms)]
    return currents


def update_kernel(tile_group, turned_grad, token_count, *refs):
    rate_ref, factor_ref, grad_ref = refs[:3]
    master_ref, first_ref, second_ref, left_stat_ref, right_stat_ref, left_ref, right_ref = refs[3:10]
    outs = refs[-8:]
    first_out, second_out, master_out, weight_out, left_stat_out, right_stat_out, left_out, right_out = outs
    base = pl.program_id(0) * tile_group
    group = range(tile_group)
    grads = [grad_ref[i] for i in group]
    lefts = [left_ref[i].astype(BF) for i in group]
    rights = [right_ref[i].astype(BF) for i in group]
    if turned_grad:
        outer_rows = [dot_tn(grad, grad) for grad in grads]
        outer_cols = [dot_nt(grad, grad) for grad in grads]
        halves = [dot_nn(grad, left).astype(BF) for grad, left in zip(grads, lefts)]
        rotated = [dot_tn(half, right) for half, right in zip(halves, rights)]
    else:
        outer_rows = [dot_nt(grad, grad) for grad in grads]
        outer_cols = [dot_tn(grad, grad) for grad in grads]
        halves = [dot_nn(grad, right).astype(BF) for grad, right in zip(grads, rights)]
        rotated = [dot_tn(left, half) for left, half in zip(lefts, halves)]
    directions = []
    for i in group:
        new_first = 0.5 * first_ref[i] + 0.5 * rotated[i]
        new_second = 0.5 * second_ref[i] + 0.5 * rotated[i] * rotated[i]
        first_out[i] = new_first
        second_out[i] = new_second
        direction = (
            new_first
            * (1.0 / (1.0 - 0.5**STEP))
            / (jnp.sqrt(new_second * (1.0 / (1.0 - 0.5**STEP))) + 1e-08)
        )
        directions.append(direction.astype(BF))
    turned = [dot_nn(left, direction).astype(BF) for left, direction in zip(lefts, directions)]
    turned = [dot_nt(half, right) for half, right in zip(turned, rights)]
    for i in group:
        master = master_ref[i]
        new_master = (master - rate_ref[base + i] * (turned[i] + 0.1 * master)) * factor_ref[base + i]
        master_out[i] = new_master
        weight_out[i] = new_master.astype(BF)
    moved = []
    for stat_ref, stat_out, outers, bases in (
        (left_stat_ref, left_stat_out, outer_rows, lefts),
        (right_stat_ref, right_stat_out, outer_cols, rights),
    ):
        for i in group:
            new_stat = 0.5 * stat_ref[i] + (0.5 / (HD * token_count)) * outers[i]
            stat_out[i] = new_stat
            moved.append(dot_nn(new_stat.astype(BF), bases[i]))
    moved = orthonormal_all(moved)
    for i in group:
        left_out[i] = moved[i]
        right_out[i] = moved[tile_group + i]


def update_tiles(grads, state, rates, factors, first_tile, earlier, turned_grad, token_count):
    count = grads.shape[0]
    tiles = state[0].shape[0]
    group = math.gcd(math.gcd(count, first_tile), TILE_GROUP)
    offset = first_tile // group
    block = (group, HD, HD)
    here = pl.BlockSpec(block, lambda i: (i + offset, 0, 0))
    smem = pl.BlockSpec(memory_space=pltpu.SMEM)
    kinds = [F32, F32, F32, BF, F32, F32, F32, F32]
    earlier = list(earlier) if earlier is not None else []

    def body(*refs):
        update_kernel(group, turned_grad, token_count, *refs)

    return pl.pallas_call(
        body,
        grid=(count // group,),
        in_specs=[smem, smem, pl.BlockSpec(block, lambda i: (i, 0, 0))]
        + [here] * 7
        + [pl.BlockSpec(memory_space=pl.ANY)] * len(earlier),
        out_specs=[here] * 8,
        out_shape=[jax.ShapeDtypeStruct((tiles, HD, HD), kind) for kind in kinds],
        input_output_aliases={10 + i: i for i in range(len(earlier))},
        compiler_params=pltpu.CompilerParams(vmem_limit_bytes=VMEM_CAP),
        cost_estimate=cost(count * 5e-7),
        name="update_tiles",
    )(rates[first_tile : first_tile + count], factors[first_tile : first_tile + count], grads, *state, *earlier)


def grad_kernel(chunks, parts, block_ref, *refs):
    lefts, rights, out_ref = refs[:chunks], refs[chunks:-1], refs[-1]
    turned = [left[...].T for left in lefts]
    lo = 0
    for j in range(parts):
        mine = rights[j * chunks : (j + 1) * chunks]
        width = mine[0].shape[1]
        step = min(512, width)
        for at in range(0, width, step):
            total = dot_nn(turned[0], mine[0][:, at : at + step])
            for left, right in zip(turned[1:], mine[1:]):
                total = total + dot_nn(left, right[:, at : at + step])
            out_ref[0, :, lo + at : lo + at + step] = total.astype(BF)
        lo += width


def grad_blocks(blocks, lefts, rights, edge):
    count = blocks.shape[0]
    rows = sum(left.shape[0] for left in lefts)
    width = sum(right[0].shape[1] for right in rights)
    flat = [chunk for right in rights for chunk in right]

    def body(*refs):
        grad_kernel(len(lefts), len(rights), *refs)

    return pl.pallas_call(
        body,
        grid_spec=pltpu.PrefetchScalarGridSpec(
            num_scalar_prefetch=1,
            grid=(count,),
            in_specs=[pl.BlockSpec((left.shape[0], edge), lambda i, blocks: (0, blocks[i])) for left in lefts]
            + [pl.BlockSpec(chunk.shape, lambda i, blocks: (0, 0)) for chunk in flat],
            out_specs=pl.BlockSpec((1, edge, width), lambda i, blocks: (i, 0, 0)),
        ),
        out_shape=jax.ShapeDtypeStruct((count, edge, width), BF),
        compiler_params=pltpu.CompilerParams(vmem_limit_bytes=VMEM_CAP),
        cost_estimate=cost(2 * count * edge * width * rows / 8e14),
        name="grad_blocks",
    )(blocks, *lefts, *flat)


def matmul_kernel(terms, *refs):
    lefts, rights, outs = refs[:terms], refs[terms : 2 * terms], refs[2 * terms :]
    total = dot_nt(lefts[0][...], rights[0][...])
    for left, right in zip(lefts[1:], rights[1:]):
        total = total + dot_nt(left[...], right[...])
    rows = outs[0].shape[0]
    outs[0][...] = total[:rows].astype(BF)
    outs[1][...] = total[rows:].astype(BF)


def matmul_sum(lefts, rights, seconds):
    terms = len(lefts)
    rows, depth = lefts[0].shape
    columns = rights[0].shape[0]
    step = min(512, columns)

    def body(*refs):
        matmul_kernel(terms, *refs)

    return pl.pallas_call(
        body,
        grid=(columns // step,),
        in_specs=[pl.BlockSpec((rows, depth), lambda n: (0, 0))] * terms
        + [pl.BlockSpec((step, depth), lambda n: (n, 0))] * terms,
        out_specs=[pl.BlockSpec((rows // 2, step), lambda n: (0, n))] * 2,
        out_shape=[jax.ShapeDtypeStruct((rows // 2, columns), BF)] * 2,
        compiler_params=pltpu.CompilerParams(vmem_limit_bytes=VMEM_CAP),
        cost_estimate=cost(seconds),
        name="matmul_sum",
    )(*lefts, *rights)


def pack_kernel(heads, edge_tiles, hidden_tiles, core_ref, tiles_ref, halves_ref, qkv_ref, out_ref):
    core = core_ref[0]
    half = hidden_tiles // 2 * HD
    first = 0
    for row in range(edge_tiles):
        for part in range(3):
            for head in range(heads):
                tile = tiles_ref[first + (row * 3 + part) * heads + head].astype(BF)
                at = (head * 3 + part) * HD
                qkv_ref[row * HD : (row + 1) * HD, at : at + HD] = tile
    first += edge_tiles * 3 * heads
    for head in range(heads):
        for row in range(edge_tiles):
            tile = tiles_ref[first + head * edge_tiles + row].T.astype(BF)
            out_ref[row * HD : (row + 1) * HD, head * HD : (head + 1) * HD] = tile
    first += heads * edge_tiles
    for kind in range(2):
        for row in range(edge_tiles):
            for column in range(hidden_tiles):
                part, inner = divmod(column, hidden_tiles // 2)
                at = kind * half + inner * HD
                if kind == 0:
                    tile = tiles_ref[first + row * hidden_tiles + column].astype(BF)
                else:
                    tile = tiles_ref[first + column * edge_tiles + row].T.astype(BF)
                halves_ref[part ^ core, row * HD : (row + 1) * HD, at : at + HD] = tile
        first += edge_tiles * hidden_tiles


def pack_weights(tiles, core, heads, edge_tiles, hidden_tiles):
    edge = edge_tiles * HD

    def body(*refs):
        pack_kernel(heads, edge_tiles, hidden_tiles, *refs)

    shapes = [(2, edge, hidden_tiles * HD), (edge, 3 * heads * HD), (edge, heads * HD)]
    return pl.pallas_call(
        body,
        grid_spec=pltpu.PrefetchScalarGridSpec(
            num_scalar_prefetch=1,
            grid=(1,),
            in_specs=[pl.BlockSpec(tiles.shape, lambda i, core: (0, 0, 0))],
            out_specs=[pl.BlockSpec(shapes[0], lambda i, core: (0, 0, 0))]
            + [pl.BlockSpec(shape, lambda i, core: (0, 0)) for shape in shapes[1:]],
        ),
        out_shape=[jax.ShapeDtypeStruct(shape, BF) for shape in shapes],
        compiler_params=pltpu.CompilerParams(vmem_limit_bytes=VMEM_CAP),
        cost_estimate=cost(5e-6),
        name="pack_weights",
    )(core[None], tiles)


def scatter_kernel(tables, *refs):
    source_ref, outs = refs[tables], refs[tables + 1 :]
    lo = 0
    for out in outs:
        width = out.shape[1]
        out[...] = source_ref[0, :, lo : lo + width]
        lo += width


def scatter_blocks(tables, source):
    count, edge, columns = source.shape
    parts = len(tables)
    width = columns // parts

    def body(*refs):
        scatter_kernel(parts, *refs)

    def out_spec(k):
        return pl.BlockSpec((edge, width), lambda i, *tables: (tables[k][i], 0))

    return pl.pallas_call(
        body,
        grid_spec=pltpu.PrefetchScalarGridSpec(
            num_scalar_prefetch=parts,
            grid=(count,),
            in_specs=[pl.BlockSpec((1, edge, columns), lambda i, *tables: (i, 0, 0))],
            out_specs=[out_spec(k) for k in range(parts)],
        ),
        out_shape=[jax.ShapeDtypeStruct((count * edge, width), BF)] * parts,
        compiler_params=pltpu.CompilerParams(vmem_limit_bytes=VMEM_CAP),
        cost_estimate=cost(4 * count * edge * columns / 3e12),
        name="scatter_blocks",
    )(*tables, source)


def project_kernel(sources, *refs):
    pick_ref = refs[0]
    pieces = refs[2 : 2 + sources]
    gain_ref, shift_ref, weight_ref, bias_ref = refs[2 + sources : 6 + sources]
    normal_out, normed_out, out_ref = refs[-3:]
    picked = pick_ref[pl.program_id(0)]
    for i in range(sources):

        @pl.when(picked == i)
        def _():
            normal_out[...] = pieces[i][...]

    normed = (normal_out[...].astype(F32) * gain_ref[...] + shift_ref[...]).astype(BF)
    normed_out[...] = normed
    out_ref[...] = (dot_nn(normed, weight_ref[...]) + bias_ref[...]).astype(BF)


def project(pick, place, total, pieces, gain, shift_by, weight, bias, into=()):
    count = pick.shape[0]
    rows, depth = pieces[0].shape
    columns = weight.shape[1]

    def body(*refs):
        project_kernel(len(pieces), *refs)

    def held(shape):
        return pl.BlockSpec(shape, lambda i, pick, place: (0, 0), pipeline_mode=pl.Buffered(1))

    def block(width):
        return pl.BlockSpec((rows, width), lambda i, pick, place: (place[i], 0))

    return pl.pallas_call(
        body,
        grid_spec=pltpu.PrefetchScalarGridSpec(
            num_scalar_prefetch=2,
            grid=(count,),
            in_specs=[held((rows, depth)) for _ in pieces]
            + [held((1, depth)), held((1, depth)), held((depth, columns)), held((1, columns))]
            + [pl.BlockSpec(memory_space=pl.ANY) for _ in into],
            out_specs=[block(depth), block(depth), block(columns)],
        ),
        out_shape=[jax.ShapeDtypeStruct((total * rows, width), BF) for width in (depth, depth, columns)],
        input_output_aliases={2 + len(pieces) + 4 + k: k for k in range(len(into))},
        compiler_params=pltpu.CompilerParams(vmem_limit_bytes=VMEM_CAP),
        cost_estimate=cost(count * 6e-6),
        name="project",
    )(pick, place, *pieces, gain[None], shift_by[None], weight, bias[None], *into)


def sync(*values):
    return lax.optimization_barrier(values)


def shift(value, axis, mask):
    return lax.ppermute(value, axis, [(i, i ^ mask) for i in range(lax.axis_size(axis))])


def move(value, axis, pairs):
    return lax.ppermute(value, axis, pairs)


def beside(value, axis, mask, steps, state):
    total, rows = sum(share for share, _ in steps), value.shape[0]
    pieces, done, first = [], 0, 0
    for share, work in steps:
        done += share
        last = rows // 16 * done // total * 16
        pieces.append(shift(value[first:last], axis, mask))
        first = last
        state = work(state)
        state, pieces, value = sync(state, pieces, value)
    return jnp.concatenate(pieces, axis=0), state


def add_low(left, right):
    return (left.astype(F32) + right.astype(F32)).astype(BF)


def join_halves(mine, other):
    first = (lax.axis_index("dp") & 1) == 0
    return jnp.concatenate([jnp.where(first, mine, other), jnp.where(first, other, mine)], axis=-1)


def halving_order(chips, masks):
    return sorted(chips, key=lambda q: tuple(-(q & (mask >> 1)) for mask in masks))


def halve(blocks, masks):
    for mask in masks:
        count = blocks.shape[0] // 2
        blocks = add_low(blocks[count:], shift(blocks[:count], "dp", mask))
    return blocks


def layer_norm(token_rows, gain, shift_by):
    centre = jnp.mean(token_rows, axis=-1, keepdims=True)
    centred = token_rows - centre
    spread = jnp.mean(centred * centred, axis=-1, keepdims=True)
    return centred * lax.rsqrt(spread + 1e-05) * gain + shift_by


def layer_norm_back(token_rows, gain, grad):
    centre = jnp.mean(token_rows, axis=-1, keepdims=True)
    centred = token_rows - centre
    inverse = lax.rsqrt(jnp.mean(centred * centred, axis=-1, keepdims=True) + 1e-05)
    normal = centred * inverse
    scaled = grad * gain
    back = (
        scaled - jnp.mean(scaled, axis=-1, keepdims=True) - normal * jnp.mean(scaled * normal, axis=-1, keepdims=True)
    ) * inverse
    return back, jnp.sum(grad * normal, axis=0), jnp.sum(grad, axis=0)


def gelu_pair(pre_act):
    cdf = 0.5 * (1.0 + lax.erf(pre_act * (0.5**0.5)))
    density = jnp.exp(-0.5 * pre_act * pre_act) * 0.3989422804014327
    return pre_act * cdf, cdf + pre_act * density


def axis_sum(value, axis):
    for bit in range(lax.axis_size(axis).bit_length() - 1):
        value = value + shift(value, axis, 1 << bit)
    return value


def small_step(summed, params, first, second):
    new_first = 0.5 * first + 0.5 * summed
    new_second = 0.5 * second + 0.5 * summed * summed
    direction = new_first / (1.0 - 0.5**STEP) / (jnp.sqrt(new_second / (1.0 - 0.5**STEP)) + 1e-08)
    return new_first, new_second, params - 0.1 * direction


def per_device(
    inputs,
    cotangent,
    lengths,
    held_blocks,
    master,
    first_moment,
    second_moment,
    left_stats,
    right_stats,
    left_basis,
    right_basis,
    small_params,
    small_first,
    small_second,
):
    dp_count = lax.axis_size("dp")
    tp_count = lax.axis_size("tensor")
    me = lax.axis_index("dp")
    place = lax.axis_index("tensor")
    core = me & 1
    rows = inputs.shape[0]
    edge = D // dp_count
    width = D // tp_count
    hidden = FF // tp_count
    half = hidden // 2
    heads = width // HD
    edge_tiles = edge // HD
    hidden_tiles = hidden // HD
    tile_q = edge_tiles * 3 * heads
    tile_o = heads * edge_tiles
    tile_u = edge_tiles * hidden_tiles
    tile_count = master.shape[2]
    near = [1 << bit for bit in range(1, dp_count.bit_length() - 1)]
    far = near[::-1]
    slices = tp_count // 2
    chips = range(dp_count // 2)
    relative = jnp.arange(dp_count, dtype=jnp.int32) ^ me
    block_of = jnp.take(held_blocks, relative, axis=1)

    bias_q = lax.dynamic_slice_in_dim(small_params, place * width, width)
    bias_v = lax.dynamic_slice_in_dim(small_params, D + place * width, width)
    bias_o = small_params[2 * D : 3 * D]
    bias_two = small_params[3 * D : 4 * D]
    gain_one = small_params[4 * D : 5 * D]
    shift_one = small_params[5 * D : 6 * D]
    gain_two = small_params[6 * D : 7 * D]
    shift_two = small_params[7 * D : 8 * D]
    hidden_starts = [(place ^ (2 * j)) * hidden + core * half for j in range(slices)]
    bias_up = jnp.concatenate(
        [lax.dynamic_slice_in_dim(small_params, 8 * D + start, half) for start in hidden_starts]
    )

    token_rows = inputs.astype(F32)
    centred = token_rows - jnp.mean(token_rows, axis=-1, keepdims=True)
    spread = jnp.mean(centred * centred, axis=-1, keepdims=True)
    normal = (centred * lax.rsqrt(spread + 1e-05)).astype(BF)
    ups = [(i, i + 1) for i in range(tp_count - 1)]
    downs = [(i + 1, i) for i in range(tp_count - 1)]
    above, below = [move(normal, "tensor", downs)], [move(normal, "tensor", ups)]

    bounds = [0, tile_q, tile_q + tile_o, tile_q + tile_o + tile_u, tile_count]
    halves, own_qkv, own_out = pack_weights(master[0, 0], core, heads, edge_tiles, hidden_tiles)
    pair = jnp.stack([halves[0], shift(halves[1], "dp", 1)])
    same_core = [list(range(at, dp_count, 2)) for at in range(2)]
    pair_slots = jnp.arange(dp_count, dtype=jnp.int32) ^ core

    def gather_ffn(value):
        return lax.all_gather(value, "dp", axis=0, tiled=True, axis_index_groups=same_core)

    def scatter_ffn(value):
        return scatter_blocks([held_blocks[2][pair_slots], held_blocks[3][pair_slots]], value)

    def gather_all(kind, value):
        value = lax.all_gather(value, "dp", axis=0, tiled=False)
        return scatter_blocks([held_blocks[kind]], value)[0]

    def crossed(mask, odd):
        return [(i, i ^ mask) for i in range(tp_count) if ((i ^ (i >> 1)) & 1) == odd]

    w_qkv = gather_all(0, own_qkv)
    bias_mixed = jnp.stack(
        [bias_q.reshape(heads, HD), jnp.zeros((heads, HD), F32), bias_v.reshape(heads, HD)], axis=1
    ).reshape(3 * width)
    distance = jnp.arange(tp_count, dtype=jnp.int32) - place
    by_distance = jnp.argsort(jnp.abs(distance)).astype(jnp.int32)
    offset = by_distance - place
    outs = [shift(own_out, "tensor", j) for j in range(1, tp_count)]
    far_first, first_raw, out_raw = [], None, None
    for step in range(1, tp_count):
        if step > 1:
            below.append(move(below[-1], "tensor", ups[step - 1 :]))
            above.append(move(above[-1], "tensor", downs[: tp_count - step]))
        if step == tp_count - 1:
            first_raw = gather_ffn(pair)
            far_first = [move(pair, "tensor", crossed(2 * j, 0)) for j in range(1, slices)]
            w_out = scatter_blocks([held_blocks[1]], out_raw)[0]
            pick = jnp.where(offset < 0, -offset, jnp.where(offset > 0, tp_count - 2 + offset, 0))
            sources = [normal] + below[:-1] + above[:-1]
            projected = project(
                pick[:-1], by_distance[:-1], tp_count, sources, gain_one, shift_one, w_qkv, bias_mixed
            )
            above, below, far_first, pair, w_qkv, w_out, projected = sync(
                above, below, far_first, pair, w_qkv, w_out, projected
            )
        elif step == 1:
            above, below, outs, own_out, pair = sync(above, below, outs, own_out, pair)
            out_raw = lax.all_gather(jnp.concatenate([own_out] + outs, axis=1), "dp", axis=0, tiled=False)
        else:
            above, below, pair = sync(above, below, pair)

    reach = tp_count // 2
    pick = jnp.where(offset < 0, -offset - reach, tp_count - 1 + offset - 2 * reach + 1)
    sources = below[reach - 1 :] + above[reach - 1 :]
    normal_all, normed_all, qkv = project(
        pick[-1:], by_distance[-1:], tp_count, sources, gain_one, shift_one, w_qkv, bias_mixed, projected
    )
    far_second = [move(pair, "tensor", crossed(2 * j, 1)) for j in range(1, slices)]

    ends = jnp.cumsum(lengths[0])
    spot = jnp.arange(SEQ, dtype=jnp.int32) - PROMPT
    started = jnp.max(jnp.where(ends[None, :] <= spot[:, None], ends[None, :], 0), axis=1)
    start_rows = jnp.where(spot < 0, 0, PROMPT + started).astype(jnp.int32)[None]
    attended, peaks = attend(start_rows, qkv)
    others = range(1, slices)
    peak_row = lax.dynamic_update_slice(
        jnp.zeros((dp_count * H,), F32), peaks[:, 0, 0], (me * H + place * heads,)
    )
    attended, far_second = sync(attended, far_second)

    def rows_of(value, j):
        return lax.dynamic_slice_in_dim(value, (place ^ j) * rows, rows, 0)

    def with_core(value):
        return jnp.concatenate([value, shift(value, "dp", 1)], axis=0)

    attended_rows = jnp.concatenate(
        [rows_of(attended, 0)] + [shift(rows_of(attended, j), "tensor", j) for j in range(1, tp_count)], axis=1
    )
    far_raw = [gather_ffn(left + right) for left, right in zip(far_first, far_second)]
    w_first = scatter_ffn(first_raw)
    back_near = with_core(cotangent)
    peak_rows = axis_sum(peak_row, "dp")
    attended_rows, w_first, cotangent, back_near, w_out, peak_rows = sync(
        attended_rows, w_first, cotangent, back_near, w_out, peak_rows
    )
    hidden_rows = token_rows + dot_nt(attended_rows, w_out) + bias_o
    normed_two = layer_norm(hidden_rows, gain_two, shift_two).astype(BF)

    w_up, w_down = [w_first[0]], [w_first[1]]
    biases = [bias_up[j * half : (j + 1) * half] for j in range(slices)]

    def core_rows(partial):
        return add_low(partial[0], shift(partial[1], "dp", 1))

    def chips_sum(blocks):
        blocks = blocks.reshape(dp_count // 2, 2, edge, blocks.shape[2])
        return lax.psum_scatter(blocks, "dp", scatter_dimension=0, tiled=False, axis_index_groups=same_core)

    def near_back(j):
        def work(state):
            if j > 0:
                up, down = state.pop("arrived")
                w_up.append(up)
                w_down.append(down)
            grad_act = jnp.dot(state["back_near"], w_down[j], preferred_element_type=F32).astype(BF)
            state = dict(state, grad_act=grad_act)
            if j == 0:
                state["normed_near"] = with_core(state.pop("normed"))
            return state

        return work

    def near_up(j):
        def work(state):
            pre_act = jnp.dot(state["normed_near"], w_up[j], preferred_element_type=F32) + biases[j]
            activation, slope = gelu_pair(pre_act)
            low = (state["grad_act"].astype(F32) * slope).astype(BF)
            if j + 1 < slices:
                state = dict(state, far_raw=far_raw[j])
            return dict(state, act_near=state["act_near"] + [activation.astype(BF)], pre_near=state["pre_near"] + [low])

        return work

    def far_up(j):
        def work(state):
            pre_act = jnp.dot(state["normed_far"], w_up[j], preferred_element_type=F32) + biases[j]
            activation, slope = gelu_pair(pre_act)
            return dict(state, act_far=state["act_far"] + [activation.astype(BF)], slopes=state["slopes"] + [slope.astype(BF)])

        return work

    def far_result(state):
        return dict(state, result_far=matmul_sum(state["act_far"], w_down, 1e-5))

    def near_grad(state):
        return dict(
            state, grad_near=matmul_sum(state["pre_near"], w_up, 1e-5), ffn_far=core_rows(state.pop("result_far"))
        )

    def down_blocks(state):
        rights = [list(pair) for pair in zip(state["act_near"], state["act_far"])]
        blocks = grad_blocks(held_blocks[3][pair_slots], [state["back_near"], state["back_far"]], rights, edge)
        return dict(state, down=blocks)

    def far_back(j):
        def work(state):
            grad_act = jnp.dot(state["back_far"], w_down[j], preferred_element_type=F32)
            low = (grad_act * state["slopes"][j].astype(F32)).astype(BF)
            return dict(state, pre_far=state["pre_far"] + [low])

        return work

    def far_grad(state):
        return dict(state, grad_far=matmul_sum(state["pre_far"], w_up, 2e-6))

    def up_blocks(state):
        rights = [list(pair) for pair in zip(state["pre_near"], state["pre_far"])]
        blocks = grad_blocks(held_blocks[2][pair_slots], [state["normed_near"], state["normed_far"]], rights, edge)
        return dict(state, up=blocks)

    def near_result(state):
        return dict(
            state, result_near=matmul_sum(state["act_near"], w_down, 1e-5), near_rows=core_rows(state.pop("grad_near"))
        )

    def both(first, second):
        return lambda state: second(first(state))

    state = dict(
        back_near=back_near, normed=normed_two, act_near=[], pre_near=[], act_far=[], pre_far=[], slopes=[]
    )
    def arrive(state):
        state = dict(state)
        state["arrived"] = scatter_ffn(state.pop("far_raw"))
        return state

    steps = []
    for j in range(slices):
        steps += [(3, arrive)] * (j > 0) + [(6 if j else 7, both(near_back(j), near_up(j)))]
    normed_across, state = beside(normed_two, "tensor", 1, steps, state)
    state["normed_across"] = normed_across

    def far_rows_in(state):
        state = dict(state)
        state["normed_far"] = with_core(state.pop("normed_across"))
        return state

    def back_rows_in(state):
        state = dict(state)
        state["back_far"] = with_core(state.pop("back_across"))
        return state

    work = both(far_rows_in, far_up(0))
    for j in range(1, slices):
        work = both(work, far_up(j))
    steps = [(13, work)]
    steps += [(9, far_result), (10, near_grad)]
    back_across, state = beside(cotangent, "tensor", 1, steps, state)
    state["back_across"] = back_across
    middle = rows // 2
    ffn_low, state = beside(state["ffn_far"][:middle], "tensor", 1, [(1, both(back_rows_in, down_blocks))], state)
    part_down = chips_sum(state.pop("down"))
    work = far_back(0)
    for j in range(1, slices):
        work = both(work, far_back(j))
    steps = [(1, both(work, far_grad))]
    ffn_high, state = beside(state.pop("ffn_far")[middle:], "tensor", 1, steps, state)
    ffn_across = jnp.concatenate([ffn_low, ffn_high], axis=0)
    far_rows = core_rows(state.pop("grad_far"))
    state["far_rows"] = far_rows
    state = sync(state)[0]
    cut = rows // 16 * 5 // 8 * 16
    low_rows, state = beside(state["far_rows"][:cut], "tensor", 1, [(1, up_blocks)], state)
    part_up = chips_sum(state.pop("up"))
    high_rows, state = beside(state.pop("far_rows")[cut:], "tensor", 1, [(1, near_result)], state)
    low_rows, high_rows, part_down, state, peak_rows = sync(low_rows, high_rows, part_down, state, peak_rows)
    grad_two = state["near_rows"].astype(F32) + jnp.concatenate([low_rows, high_rows], axis=0).astype(F32)
    result, grads_pre = state["result_near"], list(zip(state["pre_near"], state["pre_far"]))

    def far_slices(part):
        return part[:, :, :half], [part[:, :, j * half : (j + 1) * half] for j in others]

    def to_owners(values):
        return [shift(value, "tensor", 2 * j) for j, value in zip(others, values)]

    order_far = halving_order(chips, far)

    def half_slots(order):
        return jnp.array([2 * q + 1 for q in order] + [2 * q for q in order], jnp.int32)

    own_down, far_down = far_slices(part_down)
    down_low = to_owners([value[:1] for value in far_down])
    grad_part, grad_gain_two, grad_shift_two = layer_norm_back(hidden_rows, gain_two, grad_two)
    grad_hidden = cotangent.astype(F32) + grad_part
    branch = grad_hidden.astype(BF)
    even = jnp.arange(0, dp_count, 2, dtype=jnp.int32)
    out_slots = jnp.concatenate([even + 1 - core, even + core])
    grads_out = grad_blocks(held_blocks[1][out_slots], [branch], [[attended_rows]], edge)
    grad_attended_rows = jnp.dot(branch, w_out, preferred_element_type=F32).astype(BF)
    peak_rows = peak_rows + shift(peak_rows, "tensor", 1)
    grad_attended_rows, branch, result, grads_pre, grads_out, down_low, far_down, peak_rows = sync(
        grad_attended_rows, branch, result, grads_pre, grads_out, down_low, far_down, peak_rows
    )

    arrived = [
        grad_attended_rows[:, j * width : (j + 1) * width]
        if j == 0
        else shift(grad_attended_rows[:, j * width : (j + 1) * width], "tensor", j)
        for j in range(tp_count)
    ]
    grad_attended = jnp.zeros((SEQ, width), BF)
    for j in range(tp_count):
        grad_attended = lax.dynamic_update_slice_in_dim(grad_attended, arrived[j], (place ^ j) * rows, 0)
    sum_out = halve(grads_out, [1])
    grad_attended, branch, result, part_up, far_down, grads_pre, sum_out = sync(
        grad_attended, branch, result, part_up, far_down, grads_pre, sum_out
    )

    def far_sum(kept, arrived):
        total = kept.astype(F32)
        for value in arrived:
            total = total + value.astype(F32)
        total = total.astype(BF)
        return join_halves(total[0], shift(total[1], "dp", 1))

    sum_out = lax.psum_scatter(sum_out, "dp", scatter_dimension=0, tiled=False, axis_index_groups=same_core)
    own_up, far_up = far_slices(part_up)
    down_high = to_owners([value[1:] for value in far_down])
    up_low = to_owners([value[:1] for value in far_up])
    grad_qkv_rows = attend_back(start_rows, qkv, grad_attended)
    grad_qkv_rows, down_high, up_low, far_up, branch, grads_pre = sync(
        grad_qkv_rows, down_high, up_low, far_up, branch, grads_pre
    )
    up_high = to_owners([value[1:] for value in far_up])
    partial = dot_nt(grad_qkv_rows, w_qkv).astype(BF)
    partial, up_high, grad_qkv_rows, branch, grads_pre, sum_out, peak_rows = sync(
        partial, up_high, grad_qkv_rows, branch, grads_pre, sum_out, peak_rows
    )
    far_down = [jnp.concatenate(value, axis=0) for value in zip(down_low, down_high)]
    far_up = [jnp.concatenate(value, axis=0) for value in zip(up_low, up_high)]
    grad_normed_one = lax.psum_scatter(partial, "tensor", scatter_dimension=0, tiled=True).astype(F32)

    grads_qkv = grad_blocks(block_of[0][half_slots(order_far)], [normed_all], [[grad_qkv_rows]], edge)
    for bit in range(1, tp_count.bit_length() - 1):
        peak_rows = peak_rows + shift(peak_rows, "tensor", 1 << bit)
    grads_qkv, grad_qkv_rows, branch, grads_pre, partial, peak_rows = sync(
        grads_qkv, grad_qkv_rows, branch, grads_pre, partial, peak_rows
    )
    column_sums = jnp.sum(grad_qkv_rows, axis=0, dtype=F32).reshape(heads, 3, HD)
    head_sums = lambda part: lax.dynamic_update_slice(
        jnp.zeros((D,), F32), column_sums[:, part].reshape(width), (place * width,)
    )
    partial_wide = partial.astype(F32)
    grad_bias_up = jnp.concatenate([sum(jnp.sum(value, axis=0, dtype=F32) for value in pair) for pair in grads_pre])
    wide = jnp.zeros((FF,), F32)
    for j in range(slices):
        wide = lax.dynamic_update_slice(wide, grad_bias_up[j * half : (j + 1) * half], (hidden_starts[j],))
    totals = jnp.concatenate(
        [
            head_sums(0),
            head_sums(2),
            jnp.sum(branch, axis=0, dtype=F32),
            jnp.sum(cotangent, axis=0, dtype=F32),
            jnp.sum(partial_wide * normal_all.astype(F32), axis=0),
            jnp.sum(partial_wide, axis=0),
            grad_gain_two,
            grad_shift_two,
            wide,
        ]
    )
    sum_qkv = halve(grads_qkv, [1])
    totals = axis_sum(totals, "dp")
    totals, sum_qkv = sync(totals, sum_qkv)
    sum_down = far_sum(own_down, far_down)
    sum_up = far_sum(own_up, far_up)

    index = jnp.arange(tile_count, dtype=jnp.int32)
    rates = jnp.where(
        index < bounds[1],
        D ** (-0.5),
        jnp.where(index < bounds[2], (SEQ / (2.0 * D)) ** 0.5, jnp.where(index < bounds[3], D ** (-0.5), FF ** (-0.5))),
    ).astype(F32)
    ones = jnp.ones((tile_count,), F32)
    token_count = float(dp_count * SEQ)
    state = [value[0, 0] for value in (master, first_moment, second_moment, left_stats, right_stats, left_basis, right_basis)]
    tiles_up = sum_up.reshape(edge_tiles, HD, hidden_tiles, HD).transpose(0, 2, 1, 3).reshape(tile_u, HD, HD)
    tiles_down = sum_down.reshape(edge_tiles, HD, hidden_tiles, HD).transpose(2, 0, 1, 3).reshape(tile_u, HD, HD)
    count = sum_qkv.shape[0] // 4
    done = list(update_tiles(tiles_down, state, rates, ones, bounds[3], None, True, token_count))
    low_part = shift(sum_qkv[:count], "dp", far[0])
    low_part, done[3], sum_qkv = sync(low_part, done[3], sum_qkv)
    done = list(update_tiles(tiles_up, state, rates, ones, bounds[2], done, False, token_count))
    high_part = shift(sum_qkv[count : 2 * count], "dp", far[0])
    high_part, done[3], sum_qkv = sync(high_part, done[3], sum_qkv)
    sum_qkv = add_low(sum_qkv[2 * count :], jnp.concatenate([low_part, high_part], axis=0))
    sum_qkv = halve(sum_qkv, far[1:])[0]
    ffn_near = core_rows(result)
    outputs = (hidden_rows + ffn_near.astype(F32) + ffn_across.astype(F32) + bias_two).astype(BF)
    peak_all = jnp.max(peak_rows.reshape(dp_count, H), axis=0)
    grad_normed_one, totals, sum_out = sync(grad_normed_one, totals, sum_out)
    grad_small = axis_sum(totals, "tensor")
    outs = [shift(sum_out[:, j * width : (j + 1) * width], "tensor", j) for j in range(1, tp_count)]
    total_out = sum_out[:, :width].astype(F32)
    for value in outs:
        total_out = total_out + value.astype(F32)
    sum_out = total_out.astype(BF)
    rows_part, _, _ = layer_norm_back(token_rows, gain_one, grad_normed_one)
    input_grad = (grad_hidden + rows_part).astype(BF)

    shrink = jnp.sqrt(1.0 / jnp.maximum(peak_all, 1.0))
    small_first_new, small_second_new, small_new = small_step(grad_small, small_params, small_first, small_second)
    small_new = jnp.concatenate([(small_new[:D].reshape(H, HD) * shrink[:, None]).reshape(D), small_new[D:]])

    column = index % (3 * heads)
    shrink_here = lax.dynamic_slice_in_dim(shrink, place * heads, heads)
    factors = jnp.where((index < bounds[1]) & (column < 2 * heads), shrink_here[column % heads], 1.0)
    tiles_out = sum_out.reshape(edge_tiles, HD, heads, HD).transpose(2, 0, 1, 3).reshape(tile_o, HD, HD)
    tiles_qkv = sum_qkv.reshape(edge_tiles, HD, heads, 3, HD).transpose(0, 3, 2, 1, 4).reshape(tile_q, HD, HD)
    done = update_tiles(tiles_qkv, state, rates, factors, 0, done, False, token_count)
    done = update_tiles(tiles_out, state, rates, ones, bounds[1], done, True, token_count)
    return (
        outputs,
        input_grad,
        *[value[None, None] for value in done],
        small_first_new,
        small_second_new,
        small_new,
    )


def solution(mesh):
    rows = P(("dp", "tensor"), None)
    tiles = P("dp", "tensor", None, None, None)
    return jax.shard_map(
        per_device,
        mesh=mesh,
        in_specs=(rows, rows, P("dp", None), P()) + (tiles,) * 7 + (P(), P(), P()),
        out_specs=(rows, rows) + (tiles,) * 8 + (P(), P(), P()),
        check_vma=False,
    )
```
